32 devices in a mesh: dp: 16 (over z, x, core), tensor: 2 (over y).
Axes of the slice: x: 2, y: 2, z: 4, core: 2. Of those that a mesh axis runs over, the one named last changes fastest.
Arguments:
- layer_input: bfloat16 [8192, 2048], P(('dp', 'tensor')), may hold values from -12 to 12
- doc_lengths: int32 [16, 3], P('dp'), may hold values from 63 to 384, as said below
- ln1_gain: float32 [2048], P(('dp', 'tensor')), may hold values from 0.1 to 1.9
- ln1_bias: float32 [2048], P(('dp', 'tensor')), may hold values from -1.75 to 1.75
- ln2_gain: float32 [2048], P(('dp', 'tensor')), may hold values from 0.1 to 1.9
- ln2_bias: float32 [2048], P(('dp', 'tensor')), may hold values from -1.75 to 1.75
- w_qkv: bfloat16 [2048, 6144], P('dp', 'tensor'), may hold values from -0.125 to 0.125
- b_qkv: bfloat16 [6144], P(('tensor', 'dp')), may hold values from -1.75 to 1.75
- w_dense: bfloat16 [2048, 2048], P('tensor', 'dp'), may hold values from -0.5 to 0.5
- b_dense: float32 [2048], P(('dp', 'tensor')), may hold values from -1.75 to 1.75
- w_fc1: bfloat16 [2048, 8192], P('dp', 'tensor'), may hold values from -0.125 to 0.125
- b_fc1: bfloat16 [8192], P(('tensor', 'dp')), may hold values from -1.75 to 1.75
- w_fc2: bfloat16 [8192, 2048], P('tensor', 'dp'), may hold values from -0.0625 to 0.0625
- b_fc2: float32 [2048], P(('dp', 'tensor')), may hold values from -1.75 to 1.75
- cotangent: bfloat16 [8192, 2048], P(('dp', 'tensor')), may hold values from -12 to 12
Outputs:
- output: bfloat16 [8192, 2048], P(('dp', 'tensor'))
- input_grad: bfloat16 [8192, 2048], P(('dp', 'tensor'))
- ln1_gain_grad: float32 [2048], P(('dp', 'tensor'))
- ln1_bias_grad: float32 [2048], P(('dp', 'tensor'))
- ln2_gain_grad: float32 [2048], P(('dp', 'tensor'))
- ln2_bias_grad: float32 [2048], P(('dp', 'tensor'))
- w_qkv_grad: float32 [2048, 6144], P('dp', 'tensor')
- b_qkv_grad: float32 [6144], P(('tensor', 'dp'))
- w_dense_grad: float32 [2048, 2048], P('tensor', 'dp')
- b_dense_grad: float32 [2048], P(('dp', 'tensor'))
- w_fc1_grad: float32 [2048, 8192], P('dp', 'tensor')
- b_fc1_grad: float32 [8192], P(('tensor', 'dp'))
- w_fc2_grad: float32 [8192, 2048], P('tensor', 'dp')
- b_fc2_grad: float32 [2048], P(('dp', 'tensor'))
The draws below stay inside these ranges and needn't reach their ends.
Inputs may be any that keep to these rules, and one draw needn't show every extreme that they name: `doc_lengths`: row d gives the lengths of the 3 documents packed in order from the first row of group d; their sum lies above 256 and at most 512, and equals 512 for some group; the rows after it are padding.
All inputs are finite; a program needn't handle non-finite values.
Results may differ from the reference program's by a relative error of at most 0.0091.
Values may be sent and summed in bfloat16 or wider, within the bound.
No kernel may reach another device: no remote copies, remote signals or barrier semaphores. Data moves between devices by JAX's collectives and lax.ppermute only.
A program may use at most 320 MiB of HBM per device.

```python
import math
import jax
import jax.numpy as jnp
from jax import lax

D = 2048
H = 8
HD = 256
FF = 8192
ROT = 64
TOK_DEV = 256
MIN_DOC = 64
DOCS = 3
ROWS = 512
TOKENS = 8192
N_DP = 16
N_TENSOR = 2


def draw_doc_lengths(key, part):
    key = jax.random.fold_in(key, 7)
    key_pad, key_full, key_cut = jax.random.split(key, 3)
    rows = TOK_DEV * N_TENSOR
    pad = jax.random.randint(key_pad, (N_DP,), 0, TOK_DEV - MIN_DOC + 1)
    full = jax.random.randint(key_full, (), 0, N_DP)
    pad = jnp.where(jnp.arange(N_DP) == full, 0, pad)
    live = (rows - pad).astype(jnp.int32)
    spread = live - DOCS * MIN_DOC
    picks = jax.random.randint(key_cut, (N_DP, DOCS - 1), 0, spread[:, None] + 1)
    picks = jnp.sort(picks, axis=1)
    cuts = picks + MIN_DOC * jnp.arange(1, DOCS, dtype=jnp.int32)[None, :]
    cuts = jnp.where(cuts == TOK_DEV, cuts + 1, cuts)
    ends = jnp.concatenate([cuts, live[:, None]], axis=1)
    starts = jnp.concatenate([jnp.zeros((N_DP, 1), jnp.int32), cuts], axis=1)
    lengths = (ends - starts).astype(jnp.int32)
    longest = jnp.concatenate([jnp.full((1,), rows - (DOCS - 1) * MIN_DOC, jnp.int32), jnp.full((DOCS - 1,), MIN_DOC, jnp.int32)])
    chosen = (jnp.arange(N_DP) == full)[:, None]
    return jnp.where(chosen, longest[None, :], lengths).astype(jnp.int32)


def with_spikes(drawn, key, source, target, shards_of, factor):
    owner, partner = [(jnp.arange(drawn.shape[dim]) // (drawn.shape[dim] // shards_of)).reshape([-1 if axis == dim else 1 for axis in range(drawn.ndim)]) for dim in (source, target)]
    chosen = jax.random.permutation(key, shards_of)[partner]
    strong = (owner == chosen) | (owner == (partner + shards_of // 2) % shards_of)
    return jnp.where(strong, factor * drawn, drawn)


def levels(rng, shape, pieces, least, top_value):
    level, own = 1.0, jax.random.fold_in(rng, 6)
    for dim, blocks in pieces:
        draws = jnp.exp(jax.random.uniform(jax.random.fold_in(own, dim), (blocks,), jnp.float32, least / len(pieces), top_value / len(pieces)))
        level = level * jnp.repeat(draws, shape[dim] // blocks).reshape([-1 if axis == dim else 1 for axis in range(len(shape))])
    return level


def scatter_about(rng, extent, scale, bound, pieces=(), kind=jnp.bfloat16):
    values = scale * jax.random.normal(rng, extent, jnp.float32)
    if pieces:
        values = values * levels(rng, extent, pieces, -0.22, 0.18)
    return jnp.clip(values, -bound, bound).astype(kind)


def noise_with(key, dims, deviation, bound, shards, heavy, held_as=jnp.bfloat16):
    drawn = deviation * jax.random.normal(key, dims, jnp.float32)
    if shards:
        drawn = drawn * levels(key, dims, shards, -0.22, 0.18)
    return jnp.clip(with_spikes(drawn, jax.random.fold_in(key, 3), *heavy), -bound, bound).astype(held_as)


def setup_inputs(seed: int = 0) -> dict:
    key_of = jax.random.split(jax.random.key(seed), 16)
    return {
        "layer_input": noise_with(key_of[0], (TOKENS, D), 1.0, 12.0, ((0, 32),), (0, 1, 32, 2.75)),
        "doc_lengths": draw_doc_lengths(jax.random.fold_in(key_of[15], 71), 0),
        "ln1_gain": jnp.clip(1.0 + 0.18 * jax.random.normal(key_of[2], (D,), jnp.float32), 0.1, 1.9),
        "ln1_bias": scatter_about(key_of[3], (D,), 0.3, 1.75, ((0, 32),), jnp.float32),
        "ln2_gain": jnp.clip(1.0 + 0.18 * jax.random.normal(key_of[4], (D,), jnp.float32), 0.1, 1.9),
        "ln2_bias": scatter_about(key_of[5], (D,), 0.3, 1.75, ((0, 32),), jnp.float32),
        "w_qkv": scatter_about(key_of[6], (D, 3 * D), D ** -0.5, 0.125, ((0, 16), (1, 2))),
        "b_qkv": scatter_about(key_of[7], (3 * D,), 0.3, 1.75, ((0, 32),)),
        "w_dense": scatter_about(key_of[8], (D, D), (D // 16) ** -0.5, 0.5, ((0, 2), (1, 16))),
        "b_dense": scatter_about(key_of[9], (D,), 0.3, 1.75, ((0, 32),), jnp.float32),
        "w_fc1": scatter_about(key_of[10], (D, FF), D ** -0.5, 0.125, ((0, 16), (1, 2))),
        "b_fc1": scatter_about(key_of[11], (FF,), 0.3, 1.75, ((0, 32),)),
        "w_fc2": scatter_about(key_of[12], (FF, D), FF ** -0.5, 0.0625, ((0, 2), (1, 16))),
        "b_fc2": scatter_about(key_of[13], (D,), 0.3, 1.75, ((0, 32),), jnp.float32),
        "cotangent": noise_with(key_of[14], (TOKENS, D), 1.0, 12.0, ((0, 32),), (0, 1, 32, 2.75)),
    }


@jax.custom_vjp
def low(v):
    return lax.optimization_barrier(v.astype(jnp.bfloat16)).astype(jnp.float32)

@jax.custom_vjp
def low_back(v):
    return v

def low_keep(v):
    return (low(v), None)

def low_pass(kept, grad):
    return (grad,)

def back_keep(v):
    return (v, None)

def back_low(kept, grad):
    return (low(grad),)
low.defvjp(low_keep, low_pass)
low_back.defvjp(back_keep, back_low)
EPSILON = 1e-05
HIGH = lax.Precision.HIGHEST

def layer_norm(rows, gain, shift):
    mean = lax.optimization_barrier(jnp.mean(rows, axis=-1, keepdims=True))
    centred = rows - mean
    spread = lax.optimization_barrier(jnp.mean(centred * centred, axis=-1, keepdims=True))
    return centred * lax.rsqrt(spread + EPSILON) * gain + shift

def layout(lengths, count):
    places = jnp.arange(count, dtype=jnp.int32)
    ends = jnp.cumsum(lengths).astype(jnp.int32)
    segment = lax.optimization_barrier(jnp.sum((places[:, None] >= ends[None, :]).astype(jnp.int32), axis=1))
    starts = jnp.concatenate([jnp.zeros((1,), jnp.int32), ends]).astype(jnp.int32)
    slots = jnp.arange(starts.shape[0], dtype=jnp.int32)
    start = lax.optimization_barrier(jnp.sum(jnp.where(segment[:, None] == slots[None, :], starts[None, :], 0), axis=1))
    return (segment, places - start)

def angles(position, width):
    half = width // 2
    freq = 10000.0 ** (-(2.0 * jnp.arange(half, dtype=jnp.float32)) / width)
    turn = position.astype(jnp.float32)[:, None] * freq[None, :]
    turn = jnp.concatenate([turn, turn], axis=1)
    return (jnp.cos(turn)[:, None, :], jnp.sin(turn)[:, None, :])

def rotate(field, cosine, sine):
    width = cosine.shape[-1]
    half = width // 2
    part = field[..., :width]
    turned = jnp.concatenate([-part[..., half:], part[..., :half]], axis=-1)
    return jnp.concatenate([part * cosine + turned * sine, field[..., width:]], axis=-1)

def visibility(segment):
    places = jnp.arange(segment.shape[0], dtype=jnp.int32)
    same = segment[:, None] == segment[None, :]
    causal = places[None, :] <= places[:, None]
    live = (segment[:, None] < DOCS) | (places[:, None] == places[None, :])
    return same & causal & live

def group_forward(input_rows, lengths, params):
    gain_one, shift_one, gain_two, shift_two, w_qkv, b_qkv, w_dense, b_dense, w_fc1, b_fc1, w_fc2, b_fc2 = params
    count = input_rows.shape[0]
    segment, position = layout(lengths, count)
    normed_one = low(layer_norm(input_rows, gain_one, shift_one))
    normed_two = low(layer_norm(input_rows, gain_two, shift_two))
    qkv = low_back(jnp.dot(normed_one, w_qkv, precision=HIGH) + b_qkv).reshape(count, H, 3, HD)
    cosine, sine = angles(position, ROT)
    query = low(rotate(qkv[:, :, 0], cosine, sine))
    key = low(rotate(qkv[:, :, 1], cosine, sine))
    value = low(qkv[:, :, 2])
    scale = 1.0 / math.sqrt(HD)
    raw = jnp.einsum('qhd,khd->hqk', query, key, precision=HIGH) * scale
    scores = low_back(jnp.where(visibility(segment)[None], raw, -1e+30))
    peak = lax.optimization_barrier(jnp.max(scores, axis=-1, keepdims=True))
    expo = jnp.exp(scores - peak)
    probs = expo / lax.optimization_barrier(jnp.sum(expo, axis=-1, keepdims=True))
    mixed = jnp.einsum('hqk,khd->qhd', low(probs), value, precision=HIGH)
    mixed = low(low_back(mixed)).reshape(count, D)
    attention = jnp.dot(mixed, w_dense, precision=HIGH)
    pre = low_back(jnp.dot(normed_two, w_fc1, precision=HIGH) + b_fc1)
    hidden = low(jax.nn.gelu(pre, approximate=False))
    feed = jnp.dot(hidden, w_fc2, precision=HIGH)
    return input_rows + attention + b_dense + feed + b_fc2

def reference(layer_input, doc_lengths, ln1_gain, ln1_bias, ln2_gain, ln2_bias, w_qkv, b_qkv, w_dense, b_dense, w_fc1, b_fc1, w_fc2, b_fc2, cotangent):
    params = tuple((p.astype(jnp.float32) for p in (ln1_gain, ln1_bias, ln2_gain, ln2_bias, w_qkv, b_qkv, w_dense, b_dense, w_fc1, b_fc1, w_fc2, b_fc2)))
    input_float = layer_input.astype(jnp.float32)

    def forward(inputs, weights):
        blocks = inputs.reshape(N_DP, ROWS, D)
        step = jax.checkpoint(group_forward)

        def one_group(pair):
            return step(pair[0], pair[1], weights)
        return lax.map(one_group, (blocks, doc_lengths)).reshape(TOKENS, D)
    result, pull = jax.vjp(forward, input_float, params)
    input_gradient, grads = pull(cotangent.astype(jnp.float32))
    return (result.astype(jnp.bfloat16), input_gradient.astype(jnp.bfloat16), grads[0], grads[1], grads[2], grads[3], grads[4], grads[5], grads[6], grads[7], grads[8], grads[9], grads[10], grads[11])
```

```python
import functools
import math

import jax
import jax.numpy as jnp
from jax import lax
from jax.experimental import pallas as pl
from jax.experimental.pallas import tpu as pltpu
from jax.sharding import PartitionSpec as P

HD = 256
ROT = 64
DOCS = 3
EPSILON = 1e-05
INNER = 4
LANES = 128
FEED = (1, 1, 1, 1)
AXES = ("dp", "tensor")
BF = jnp.bfloat16
F32 = jnp.float32
NT = ((1,), (1,))
NN = ((1,), (0,))
TN = ((0,), (0,))
VMEM_LIMIT = 56 * 2**20


def dot(a, b, dims):
    return lax.dot_general(a, b, (dims, ((), ())), preferred_element_type=F32)


def take_weights(parts, gain_ref, w1, w2, cols):
    own, near, far_one, far_two, passed_one, passed_two = parts
    for b in range(16):
        lanes = slice(b * LANES, (b + 1) * LANES)
        k = b % 4
        if b < 4:
            block = own[k].astype(F32)
        elif b < 8:
            block = near[k].astype(F32)
        elif b < 12:
            block = far_one[k].astype(F32) + passed_one[k].astype(F32)
        else:
            block = far_two[k].astype(F32) + passed_two[k].astype(F32)
        w1[:, lanes] = (block[:cols] * gain_ref[:, lanes]).astype(BF)
        w2[:, lanes] = block[cols:].astype(BF)


def give_grads(acc1, acc2, col, gain_ref, shift_ref, w1, cols, own_ref, rest_ref, norm_ref):
    for b in range(16):
        lanes = slice(b * LANES, (b + 1) * LANES)
        gain = gain_ref[:, lanes]
        m = acc1[:, lanes]
        w = w1[:, lanes].astype(F32)
        to, k = (own_ref, b) if b < 4 else (rest_ref, b - 4)
        to[k, :cols] = (m * gain + col[...] * shift_ref[:, lanes]).astype(BF)
        to[k, cols:] = acc2[:, lanes].astype(BF)
        norm_ref[0:1, lanes] = jnp.sum(w * m, axis=0, keepdims=True) / gain
        norm_ref[1:2, lanes] = jnp.sum(w * col[...], axis=0, keepdims=True) / gain


def stream(step, sources, buffers, sems):
    steps = len(sources[0]) // 2

    def copies(s):
        made = []
        for blocks, buffer in zip(sources, buffers):
            for k in (2 * s, 2 * s + 1):
                at = 0
                for ref in blocks[k]:
                    rows, cols = ref.shape
                    to = buffer.at[s % 2, pl.ds((k % 2) * rows, rows), pl.ds(at, cols)]
                    made.append(pltpu.make_async_copy(ref, to, sems.at[s % 2, len(made)]))
                    at += cols
        return made

    def begin(s):
        for c in copies(s):
            c.start()

    def arrive():
        for s in range(steps):
            @pl.when(step == s)
            def _(s=s):
                if s + 1 < steps:
                    begin(s + 1)
                for c in copies(s):
                    c.wait()

    return begin, arrive


def split_refs(shape, refs):
    refs, arrays = list(refs), []
    for counts in shape:
        arrays.append([[refs.pop(0) for _ in range(n)] for n in counts])
    return arrays, refs


def feed_kernel(shape, cols, *refs):
    sources, refs = split_refs(shape, refs)
    p0, p1, p2, p3, p4, p5, gain_ref, shift_ref, ratio_ref, bias_ref = refs[:10]
    hidden_ref, pre_grad_ref, w1, w2, own_ref, rest_ref, norm_ref, sum_ref = refs[10:18]
    acc1, acc2, col, row, unit_buf, cot_buf, sems = refs[18:]
    step = pl.program_id(0)
    begin, arrive = stream(step, sources, (unit_buf, cot_buf), sems)

    @pl.when(step == 0)
    def _():
        begin(0)
        take_weights((p0, p1, p2, p3, p4, p5), gain_ref, w1, w2, cols)
        row[...] = jnp.sum(dot(ratio_ref[...], w1[...], NT), axis=0, keepdims=True) + bias_ref[...]
        acc1[...] = jnp.zeros_like(acc1)
        acc2[...] = jnp.zeros_like(acc2)
        col[...] = jnp.zeros_like(col)
        sum_ref[...] = jnp.zeros_like(sum_ref)

    arrive()
    slot = lax.rem(step, 2)
    unit = unit_buf[slot]
    cot = cot_buf[slot]
    pre = dot(unit, w1[...], NT) + row[...]
    back = dot(cot, w2[...], NT)
    phi = 0.5 * (1.0 + lax.erf(pre * (1.0 / math.sqrt(2.0))))
    slope = phi + pre * (jnp.exp(-0.5 * pre * pre) * (1.0 / math.sqrt(2.0 * math.pi)))
    hidden = (pre * phi).astype(BF)
    pre_grad = (back * slope).astype(BF)
    hidden_ref[...] = hidden
    pre_grad_ref[...] = pre_grad
    acc1[...] += dot(pre_grad, unit, TN)
    acc2[...] += dot(hidden, cot, TN)
    col[...] += dot(pre_grad, jnp.ones((pre_grad.shape[0], LANES), BF), TN)
    sum_ref[...] += jnp.sum(pre_grad.astype(F32), axis=0, keepdims=True)

    @pl.when(step == pl.num_programs(0) - 1)
    def _():
        give_grads(acc1, acc2, col, gain_ref, shift_ref, w1, cols, own_ref, rest_ref, norm_ref)


def whole(shape):
    return pl.BlockSpec(shape, lambda *_: (0,) * len(shape), pipeline_mode=pl.Buffered(1))


def flat(arrays):
    return [p for blocks in arrays for block in blocks for p in block]


def counts(arrays):
    return tuple(tuple(len(block) for block in blocks) for blocks in arrays)


def stream_scratch(rows, width):
    return [pltpu.VMEM((2, rows, width), BF), pltpu.VMEM((2, rows, width), BF), pltpu.SemaphoreType.DMA((2, 8))]


ANYWHERE = pl.BlockSpec(memory_space=pl.ANY)


def feed_call(arrays, weights, gain, shift, ratio, bias):
    own = arrays[0][0][0]
    block, rows, width = 2 * own.shape[0], 8 * own.shape[0], own.shape[1]
    cols = bias.shape[1]
    pieces = flat(arrays)
    cb = pl.BlockSpec((block, cols), lambda r: (r, 0))
    shapes = [
        jax.ShapeDtypeStruct((rows, cols), BF),
        jax.ShapeDtypeStruct((rows, cols), BF),
        jax.ShapeDtypeStruct((cols, width), BF),
        jax.ShapeDtypeStruct((cols, width), BF),
        jax.ShapeDtypeStruct((4, 2 * cols, LANES), BF),
        jax.ShapeDtypeStruct((12, 2 * cols, LANES), BF),
        jax.ShapeDtypeStruct((2, width), F32),
        jax.ShapeDtypeStruct((1, cols), F32),
    ]
    return pl.pallas_call(
        functools.partial(feed_kernel, counts(arrays), cols),
        grid=(rows // block,),
        out_shape=shapes,
        in_specs=[ANYWHERE] * len(pieces)
        + [whole(w.shape) for w in weights]
        + [whole(v.shape) for v in (gain, shift, ratio, bias)],
        out_specs=[cb, cb] + [whole(s.shape) for s in shapes[2:]],
        scratch_shapes=[
            pltpu.VMEM((cols, width), F32), pltpu.VMEM((cols, width), F32), pltpu.VMEM((cols, LANES), F32),
            pltpu.VMEM((1, cols), F32),
        ]
        + stream_scratch(block, width),
        compiler_params=pltpu.CompilerParams(vmem_limit_bytes=VMEM_LIMIT),
        cost_estimate=pl.CostEstimate(flops=8 * rows * width * cols, bytes_accessed=4 * rows * width, transcendentals=0),
        name="feed",
    )(*pieces, *weights, gain, shift, ratio, bias)


def attention_kernel(shape, cols, lengths, half_ref, *refs):
    sources, refs = split_refs(shape, refs)
    p0, p1, p2, p3, p4, p5, gain_ref, shift_ref, ratio_ref, bias_ref = refs[:10]
    cos_ref, sin_up_ref, sin_down_ref = refs[10:13]
    mixed_ref, qkv_grad_ref, w1, w2, own_ref, rest_ref, norm_ref, sum_ref = refs[13:21]
    acc1, acc2, col, row, unit_buf, cot_buf, sems = refs[21:]
    group = pl.program_id(0)
    begin, arrive = stream(group, sources, (unit_buf, cot_buf), sems)

    @pl.when(group == 0)
    def _():
        begin(0)
        take_weights((p0, p1, p2, p3, p4, p5), gain_ref, w1, w2, cols)
        row[...] = jnp.sum(dot(ratio_ref[...], w1[...], NT), axis=0, keepdims=True) + bias_ref[...]
        acc1[...] = jnp.zeros_like(acc1)
        acc2[...] = jnp.zeros_like(acc2)
        col[...] = jnp.zeros_like(col)
        sum_ref[...] = jnp.zeros_like(sum_ref)

    arrive()
    slot = lax.rem(group, 2)
    unit = unit_buf[slot]
    cot = cot_buf[slot]
    count = unit.shape[0]
    cosine, sin_up, sin_down = cos_ref[...], sin_up_ref[...], sin_down_ref[...]
    half = ROT // 2

    def turn(u):
        p = u[:, :LANES]
        p = p * cosine + pltpu.roll(p, LANES - half, 1) * sin_up + pltpu.roll(p, half, 1) * sin_down
        return jnp.concatenate([p, u[:, LANES:]], axis=1)

    def unturn(u):
        p = u[:, :LANES]
        p = p * cosine + pltpu.roll(p * sin_up, half, 1) + pltpu.roll(p * sin_down, LANES - half, 1)
        return jnp.concatenate([p, u[:, LANES:]], axis=1)

    qkv = dot(unit, w1[...], NT) + row[...]
    query = turn(qkv[:, :HD]).astype(BF)
    key = turn(qkv[:, HD : 2 * HD]).astype(BF)
    value = qkv[:, 2 * HD :].astype(BF)
    back = dot(cot, w2[...], NT).astype(BF)

    shift = half_ref[0]
    at = lax.broadcasted_iota(jnp.int32, (count, 1), 0) + shift
    at = jnp.where(at >= count, at - count, at)
    to = lax.broadcasted_iota(jnp.int32, (1, count), 1) + shift
    to = jnp.where(to >= count, to - count, to)
    end, seg_at, seg_to = 0, jnp.zeros_like(at), jnp.zeros_like(to)
    for k in range(DOCS):
        end = end + lengths[group, k]
        seg_at = seg_at + jnp.where(at >= end, 1, 0)
        seg_to = seg_to + jnp.where(to >= end, 1, 0)
    seg_at = jnp.where(seg_at == DOCS, DOCS + at, seg_at)
    seg_to = jnp.where(seg_to == DOCS, DOCS + to, seg_to)
    visible = (seg_at == seg_to) & (to <= at)

    scale = 1.0 / math.sqrt(HD)
    scores = jnp.where(visible, dot(query, key, NT) * scale, -1e30)
    expo = jnp.exp(scores - jnp.max(scores, axis=1, keepdims=True))
    probs = expo / jnp.sum(expo, axis=1, keepdims=True)
    low = probs.astype(BF)
    mixed = dot(low, value, NN).astype(BF)
    value_grad = dot(low, back, TN)
    probs_grad = dot(back, value, NT)
    inner = jnp.sum(probs * probs_grad, axis=1, keepdims=True)
    score_grad = (probs * (probs_grad - inner)).astype(BF)
    query_grad = unturn(dot(score_grad, key, NN) * scale)
    key_grad = unturn(dot(score_grad, query, TN) * scale)
    qkv_grad = jnp.concatenate([query_grad, key_grad, value_grad], axis=1).astype(BF)
    mixed_ref[...] = mixed
    qkv_grad_ref[...] = qkv_grad
    acc1[...] += dot(qkv_grad, unit, TN)
    acc2[...] += dot(mixed, cot, TN)
    col[...] += dot(qkv_grad, jnp.ones((count, LANES), BF), TN)
    sum_ref[...] += jnp.sum(qkv_grad.astype(F32), axis=0, keepdims=True)

    @pl.when(group == pl.num_programs(0) - 1)
    def _():
        give_grads(acc1, acc2, col, gain_ref, shift_ref, w1, cols, own_ref, rest_ref, norm_ref)


def attention_call(lengths, half, arrays, weights, gain, shift, ratio, bias, turns):
    own = arrays[0][0][0]
    count, rows, width = 2 * own.shape[0], 8 * own.shape[0], own.shape[1]
    cols, ctx = bias.shape[1], HD
    pieces = flat(arrays)
    smem = pl.BlockSpec(memory_space=pltpu.SMEM)
    shapes = [
        jax.ShapeDtypeStruct((rows, ctx), BF),
        jax.ShapeDtypeStruct((rows, cols), BF),
        jax.ShapeDtypeStruct((cols, width), BF),
        jax.ShapeDtypeStruct((ctx, width), BF),
        jax.ShapeDtypeStruct((4, cols + ctx, LANES), BF),
        jax.ShapeDtypeStruct((12, cols + ctx, LANES), BF),
        jax.ShapeDtypeStruct((2, width), F32),
        jax.ShapeDtypeStruct((1, cols), F32),
    ]
    return pl.pallas_call(
        functools.partial(attention_kernel, counts(arrays), cols),
        grid=(rows // count,),
        out_shape=shapes,
        in_specs=[smem, smem]
        + [ANYWHERE] * len(pieces)
        + [whole(w.shape) for w in weights]
        + [whole(v.shape) for v in (gain, shift, ratio, bias)]
        + [pl.BlockSpec((count, LANES), lambda r: (r, 0))] * 3,
        out_specs=[pl.BlockSpec((count, ctx), lambda r: (r, 0)), pl.BlockSpec((count, cols), lambda r: (r, 0))]
        + [whole(s.shape) for s in shapes[2:]],
        scratch_shapes=[
            pltpu.VMEM((cols, width), F32), pltpu.VMEM((ctx, width), F32), pltpu.VMEM((cols, LANES), F32),
            pltpu.VMEM((1, cols), F32),
        ]
        + stream_scratch(count, width),
        compiler_params=pltpu.CompilerParams(vmem_limit_bytes=VMEM_LIMIT),
        cost_estimate=pl.CostEstimate(
            flops=4 * rows * width * (cols + ctx), bytes_accessed=4 * rows * width, transcendentals=0
        ),
        name="attention",
    )(lengths, half, *pieces, *weights, gain, shift, ratio, bias, *turns)


def join_kernel(n, *refs):
    total = dot(refs[0][...], refs[n][...], NN)
    for j in range(1, n):
        total += dot(refs[j][...], refs[n + j][...], NN)
    refs[2 * n][...] = total.astype(BF)


def join_call(acts, weights, sent):
    rows, width = acts[0].shape[0], weights[0].shape[1]
    block = rows // 8
    place = (lambda r: 4 * (r // 2) + r % 2 + 2) if sent else (lambda r: 4 * (r // 2) + r % 2)
    flops = sum(rows * a.shape[1] * width for a in acts)
    return pl.pallas_call(
        functools.partial(join_kernel, len(acts)),
        grid=(4,),
        out_shape=jax.ShapeDtypeStruct((rows // 2, width), BF),
        in_specs=[pl.BlockSpec((block, a.shape[1]), lambda r: (place(r), 0)) for a in acts]
        + [whole(w.shape) for w in weights],
        out_specs=pl.BlockSpec((block, width), lambda r: (r, 0)),
        compiler_params=pltpu.CompilerParams(vmem_limit_bytes=VMEM_LIMIT),
        cost_estimate=pl.CostEstimate(flops=flops, bytes_accessed=2 * rows * width, transcendentals=0),
        name="join",
    )(*acts, *weights)


def after(v, *others):
    return lax.optimization_barrier((v, *others))[0]


def make(dp, tensor):
    outer = dp // INNER
    face = INNER * tensor
    total = dp * tensor
    short = outer == 4

    def permute(v, pairs):
        return lax.ppermute(v, AXES, pairs)

    def flip(v, k):
        return permute(v, [(l, l ^ k) for l in range(total)])

    def hop(v, moves):
        return permute(v, [(a * face + f, b * face + f) for a, b in moves for f in range(face)])

    column_groups = [[o * face + f for o in range(outer)] for f in range(face)]
    ring_groups = [[o * face + i * tensor + t for i in range(INNER)] for o in range(outer) for t in range(tensor)]

    order_table = [[0, 1, 2, 3], [1, 0, 2, 3], [2, 3, 1, 0], [3, 2, 1, 0]]
    back_table = [[0, 1, 2, 3], [1, 0, 2, 3], [3, 2, 0, 1], [3, 2, 1, 0]]

    def blocks(v, table, o):
        if not short:
            return v
        width = v.shape[-1] // outer
        row = jnp.array(table, jnp.int32)[o]
        return jnp.concatenate(
            [lax.dynamic_slice_in_dim(v, row[j] * width, width, axis=v.ndim - 1) for j in range(outer)], axis=-1
        )

    def swap_ring(v):
        return lax.all_to_all(v, AXES, split_axis=0, concat_axis=0, tiled=True, axis_index_groups=ring_groups)

    def gather_step(v, token):
        if not short:
            every = lax.all_gather(v, AXES, axis=0, tiled=True, axis_index_groups=column_groups)
            n = v.shape[1]
            every = every.transpose(1, 0, 2).reshape(n, 16, LANES).transpose(1, 0, 2)
            none = jnp.zeros_like(every[:4])
            return [every[:4], every[4:8], every[8:12], every[12:], none, none], token
        v = after(v, token[0])
        near = flip(v, face)
        far_one = hop(v, [(1, 2), (2, 1)])
        far_two = hop(near, [(1, 2), (2, 1)])
        ready_one = after(far_one, token[1])
        passed_one = hop(ready_one, [(1, 0), (2, 3)])
        ready_two = after(far_two, passed_one)
        passed_two = hop(ready_two, [(1, 0), (2, 3)])
        return [v, near, far_one, far_two, passed_one, passed_two], (near, passed_two)

    def reduce_outer(own, rest, tokens):
        if not short:
            v = jnp.concatenate([own, rest], axis=0)
            n = v.shape[1]
            v = v.transpose(1, 0, 2).reshape(n, dp, -1).transpose(1, 0, 2)
            return lax.psum_scatter(v, AXES, scatter_dimension=0, tiled=True, axis_index_groups=column_groups)
        first = hop(rest, [(0, 1), (3, 2)])
        if tokens[0] is not None:
            first = after(first, tokens[0])
        far = (rest[4:].astype(F32) + first[4:].astype(F32)).astype(BF)
        second = hop(far, [(1, 2), (2, 1)])
        if tokens[1] is not None:
            second = after(second, tokens[1])
        near = (rest[:4].astype(F32) + second[4:].astype(F32)).astype(BF)
        third = hop(near, [(1, 0), (2, 3)])
        if tokens[2] is not None:
            third = after(third, tokens[2])
        total = own.astype(F32) + first[:4].astype(F32) + second[:4].astype(F32) + third.astype(F32)
        return total.astype(BF)

    def reduce_face(kept, sent):
        m = kept.shape[0] // 4
        half = kept.shape[1] // 2
        other = flip(sent, 2)

        def part(k, left):
            cut = slice(0, half) if left else slice(half, 2 * half)
            rows = slice(k * m, (k + 1) * m)
            return kept[rows, cut].astype(F32) + other[rows, cut].astype(F32)

        x1 = flip(jnp.concatenate([part(3, True), part(2, True)], axis=1).astype(BF), 4)
        t1 = flip(jnp.concatenate([part(3, False), part(1, False)], axis=1).astype(BF), 1)
        t2 = flip((part(1, True) + x1[:, :half].astype(F32)).astype(BF), 1)
        x2 = flip((part(2, False) + t1[:, :half].astype(F32)).astype(BF), 4)
        left = part(0, True) + x1[:, half:].astype(F32) + t2.astype(F32)
        right = part(0, False) + t1[:, half:].astype(F32) + x2.astype(F32)
        return jnp.concatenate([left, right], axis=1)

    def per_device(
        layer_input, doc_lengths, ln1_gain, ln1_bias, ln2_gain, ln2_bias, w_qkv, b_qkv, w_dense, b_dense,
        w_fc1, b_fc1, w_fc2, b_fc2, cotangent,
    ):
        d, t = lax.axis_index("dp"), lax.axis_index("tensor")
        o, i = d // INNER, d % INNER
        own_rows, width = layer_input.shape
        group_rows = own_rows * tensor
        strip = width // dp
        ctx = w_dense.shape[0] // INNER
        hidden_own = w_fc1.shape[1] // INNER
        qkv_own = w_qkv.shape[1] // INNER
        unit_cols = hidden_own // sum(FEED)
        sizes = [n * unit_cols for n in FEED]
        starts = [sum(sizes[:c]) for c in range(len(sizes))]

        cot_own = blocks(cotangent, order_table, o)
        cot_t, cot_x, cot_c = flip(cot_own, 1), flip(cot_own, 4), flip(cot_own, 2)

        fc1 = w_fc1.T.reshape(INNER, hidden_own, strip)
        fc2 = w_fc2.reshape(INNER, hidden_own, strip)
        pieces = [
            jnp.concatenate([fc1[:, s : s + n], fc2[:, s : s + n]], axis=1) for s, n in zip(starts, sizes)
        ]
        qkv_piece = jnp.concatenate(
            [w_qkv.T.reshape(INNER, qkv_own, strip), w_dense.reshape(INNER, ctx, strip)], axis=1
        )
        ring = [swap_ring(pieces[0])]

        input_own = layer_input.astype(F32)
        mean = jnp.mean(input_own, axis=-1, keepdims=True)
        centred = input_own - mean
        rstd = lax.rsqrt(jnp.mean(centred * centred, axis=-1, keepdims=True) + EPSILON)
        unit_float = centred * rstd
        unit_own = blocks(unit_float.astype(BF), order_table, o)
        unit_t, unit_x, unit_c = flip(unit_own, 1), flip(unit_own, 4), flip(unit_own, 2)

        second = after(jnp.concatenate([pieces[1], qkv_piece], axis=1), unit_own, ring[0])
        second = swap_ring(second)
        n = pieces[1].shape[1]
        ring += [second[:, :n], second[:, n:]]

        cot_b = flip(cot_x, 1)
        cot_tc, cot_xc = flip(cot_t, 2), flip(cot_x, 2)
        cot_bc = flip(cot_b, 2)
        mid = width // 2
        unit_bl, unit_br = flip(unit_t[:, :mid], 4), flip(unit_x[:, mid:], 1)
        unit_tc, unit_xc = flip(unit_t, 2), flip(unit_x, 2)
        unit_blc, unit_brc = flip(unit_bl, 2), flip(unit_br, 2)
        arrays = [
            [[unit_own], [unit_t], [unit_c], [unit_tc], [unit_x], [unit_bl, unit_br], [unit_xc], [unit_blc, unit_brc]],
            [[cot_own], [cot_t], [cot_c], [cot_tc], [cot_x], [cot_b], [cot_xc], [cot_bc]],
        ]

        third = after(jnp.concatenate(pieces[2:], axis=1), second, unit_x)
        third = swap_ring(third)
        at = 0
        for p in pieces[2:]:
            ring.append(third[:, at : at + p.shape[1]])
            at += p.shape[1]

        full = []
        token = (pieces[0], pieces[0])
        for w in ring:
            got, token = gather_step(w, token)
            full.append(got)

        piece = width // total
        small = jnp.concatenate(
            [ln1_gain, ln1_bias, ln2_gain, ln2_bias, b_dense + b_fc2, b_qkv.astype(F32), b_fc1.astype(F32),
             doc_lengths[0].astype(F32), jnp.zeros((128 - DOCS,), F32)]
        )
        small = jnp.broadcast_to(after(small, unit_own, ring[0])[None], (total, small.shape[0]))
        small = lax.all_to_all(small, AXES, split_axis=0, concat_axis=0, tiled=True)
        small = after(small, second)
        vectors = small[:, : 5 * piece].reshape(total, 5, piece).transpose(1, 0, 2).reshape(5, width)
        vectors = blocks(vectors, order_table, o)
        gain_one, shift_one, gain_two, shift_two, bias_out = (vectors[j : j + 1] for j in range(5))
        nq, nf = b_qkv.shape[0], b_fc1.shape[0]
        mine = lax.dynamic_index_in_dim(small.reshape(dp, tensor, -1), t, 1, keepdims=False)
        at = 5 * piece
        bias_qkv = lax.dynamic_slice_in_dim(mine[:, at : at + nq].reshape(1, -1), i * qkv_own, qkv_own, axis=1)
        bias_fc1 = lax.dynamic_slice_in_dim(
            mine[:, at + nq : at + nq + nf].reshape(1, -1), i * hidden_own, hidden_own, axis=1
        )
        docs = mine[:, at + nq + nf : at + nq + nf + DOCS]
        docs = lax.dynamic_slice_in_dim(docs, o * INNER, INNER, axis=0)
        docs = jnp.concatenate([lax.dynamic_slice_in_dim(docs, i ^ g, 1, axis=0) for g in range(INNER)], axis=0)
        lengths = jnp.round(docs).astype(jnp.int32)

        def fine(v):
            high = v.astype(BF)
            low = (v - high.astype(F32)).astype(BF)
            return jnp.concatenate([high, low, jnp.zeros((14, v.shape[1]), BF)], axis=0)

        ratio_one = fine(shift_one / gain_one)
        ratio_two = fine(shift_two / gain_two)

        place = (jnp.arange(group_rows, dtype=jnp.int32) + t * own_rows) % group_rows
        ends = jnp.cumsum(lengths, axis=1)
        begin = jnp.zeros((INNER, group_rows), jnp.int32)
        for k in range(DOCS):
            begin = jnp.where(place[None] >= ends[:, k : k + 1], ends[:, k : k + 1], begin)
        position = (place[None] - begin).reshape(-1, 1).astype(F32)
        lane = jnp.arange(LANES)
        half = ROT // 2
        freq = 10000.0 ** (-(2.0 * (lane % half).astype(F32)) / ROT)
        angle = position * freq[None]
        cosine = jnp.where(lane < ROT, jnp.cos(angle), 1.0)
        sine = jnp.sin(angle)
        turns = (cosine, jnp.where(lane < half, -sine, 0.0), jnp.where((lane >= half) & (lane < ROT), sine, 0.0))

        def feed(c, weights):
            bias = bias_fc1[:, starts[c] : starts[c] + sizes[c]]
            return feed_call(arrays, weights, gain_two, shift_two, ratio_two, bias)

        shift = (t * own_rows).astype(jnp.int32).reshape(1)
        done = []
        for k, weights in enumerate(full):
            if done:
                weights = [after(weights[0], done[-1][7])] + weights[1:]
            if k == 2:
                p = attention_call(
                    lengths, shift, arrays, weights, gain_one, shift_one, ratio_one, bias_qkv, turns
                )
            else:
                p = feed(k if k < 2 else k - 1, weights)
            done.append(p)
        attn = done[2]
        feeds = done[:2] + done[3:]
        acts, outs = [p[0] for p in done], [p[3] for p in done]
        grads, ins = [p[1] for p in done], [p[2] for p in done]
        back = reduce_face(join_call(grads, ins, False), join_call(grads, ins, True))
        summed = reduce_face(join_call(acts, outs, False), join_call(acts, outs, True))
        names = [p[7] for p in done] + [None] * 8
        reduced = [reduce_outer(p[4], p[5], names[k + 2 : k + 5]) for k, p in enumerate(done)]

        output = (input_own + blocks(summed + bias_out, back_table, o)).astype(BF)
        pulled = blocks(back, back_table, o)
        along = jnp.mean(pulled * unit_float, axis=-1, keepdims=True)
        level = jnp.mean(pulled, axis=-1, keepdims=True)
        term = rstd * (pulled - level - unit_float * along)
        input_grad = (cotangent.astype(F32) + term).astype(BF)

        own_sums = jnp.concatenate([attn[6], sum(p[6] for p in feeds)], axis=0)
        own_sums = blocks(own_sums, back_table, o)
        own_sums = jnp.concatenate([own_sums, jnp.sum(cotangent, axis=0, dtype=F32)[None]], axis=0)
        own_sums = own_sums.reshape(5, total, piece).transpose(1, 0, 2).reshape(total, 5 * piece)
        share = dp // INNER

        def spread(v, n):
            held = jnp.zeros((dp, tensor, n), F32)
            return lax.dynamic_update_slice(held, v.reshape(share, 1, n), (i * share, t, 0)).reshape(total, n)

        tail = jnp.concatenate(
            [own_sums, spread(attn[7], nq), spread(jnp.concatenate([p[7] for p in feeds], axis=1), nf)], axis=1
        )
        pad = -tail.shape[1] % 128
        tail = jnp.concatenate([tail, jnp.zeros((total, pad), F32)], axis=1)
        tail = jnp.sum(lax.all_to_all(tail, AXES, split_axis=0, concat_axis=0, tiled=True), axis=0)
        cuts = [tail[j * piece : (j + 1) * piece] for j in range(5)]
        b_qkv_grad = tail[at : at + nq]
        b_fc1_grad = tail[at + nq : at + nq + nf]

        final = [swap_ring(r) for r in reduced]
        attn_grad = final[2]
        feed_grads = final[:2] + final[3:]
        w_qkv_grad = attn_grad[:, :qkv_own].reshape(INNER * qkv_own, strip).T.astype(F32)
        w_dense_grad = attn_grad[:, qkv_own:].reshape(INNER * ctx, strip).astype(F32)
        w_fc1_grad = jnp.concatenate([g[:, :n] for g, n in zip(feed_grads, sizes)], axis=1)
        w_fc1_grad = w_fc1_grad.reshape(INNER * hidden_own, strip).T.astype(F32)
        w_fc2_grad = jnp.concatenate([g[:, n:] for g, n in zip(feed_grads, sizes)], axis=1)
        w_fc2_grad = w_fc2_grad.reshape(INNER * hidden_own, strip).astype(F32)
        return (
            output, input_grad, cuts[0], cuts[1], cuts[2], cuts[3], w_qkv_grad, b_qkv_grad, w_dense_grad, cuts[4],
            w_fc1_grad, b_fc1_grad, w_fc2_grad, cuts[4],
        )

    return per_device


def solution(mesh):
    rows = P(("dp", "tensor"), None)
    vector = P(("dp", "tensor"))
    crossed = P(("tensor", "dp"))
    wide = P("dp", "tensor")
    tall = P("tensor", "dp")
    return jax.shard_map(
        make(mesh.shape["dp"], mesh.shape["tensor"]),
        mesh=mesh,
        in_specs=(rows, P("dp", None), vector, vector, vector, vector, wide, crossed, tall, vector, wide, crossed,
                  tall, vector, rows),
        out_specs=(rows, rows, vector, vector, vector, vector, wide, crossed, tall, vector, wide, crossed, tall,
                   vector),
        check_vma=False,
    )
```

```python
import functools
import math

import jax
import jax.numpy as jnp
from jax import lax
from jax.experimental import pallas as pl
from jax.experimental.pallas import tpu as pltpu
from jax.sharding import PartitionSpec as P

HD = 256
ROT = 64
DOCS = 3
EPSILON = 1e-05
INNER = 4
LANES = 128
AXES = ("dp", "tensor")
BF = jnp.bfloat16
F32 = jnp.float32
NT = ((1,), (1,))
NN = ((1,), (0,))
TN = ((0,), (0,))
VMEM_LIMIT = 56 * 2**20
STEPS = 4


ORDER = (
    "p1", "p0", "g1", "p2", "g0", "p3", "g2", "own", "g3", "h1", "h0", "sm", "p4", "h2", "i1", "h3", "xt", "c",
    "i0", "j1", "g4", "vec", "i2", "j0", "i3", "b", "tc", "h4", "bc", "K0", "r0", "K1", "i4", "j3", "j2", "r1",
    "KA", "r2", "u0", "j4", "u1", "K4", "r3", "r4", "v0", "JB", "v1", "JO", "u2", "kB", "w0", "CB", "kO", "u3",
    "z0", "v2", "CO", "DB", "tail", "v3", "u4", "w2", "tz", "w1", "DO", "z2", "EO", "v4", "w3", "EB", "z1", "w4",
    "z3", "z4",
)

NOTHING = pl.CostEstimate(flops=0, bytes_accessed=0, transcendentals=0)
SCALARS = pl.BlockSpec(memory_space=pltpu.SMEM)
ANYWHERE = pl.BlockSpec(memory_space=pl.ANY)
VECTORS = pl.BlockSpec(memory_space=pltpu.VMEM)

OUTER, INSIDE, SIDE, SPOT, DOC_ROW = 0, 1, 2, 3, 7


def dot(a, b, dims):
    return lax.dot_general(a, b, (dims, ((), ())), preferred_element_type=F32)


def shaped(shape, dtype=BF):
    return jax.ShapeDtypeStruct(shape, dtype)


def whole(shape):
    return pl.BlockSpec(shape, lambda *_: (0,) * len(shape), pipeline_mode=pl.Buffered(1))


def run_kernel(kernel, outs, in_specs, out_specs, args, name, grid=(), scratch=(), aliases=None, vmem=None):
    return pl.pallas_call(
        kernel,
        grid=grid,
        out_shape=outs,
        in_specs=in_specs,
        out_specs=out_specs,
        scratch_shapes=scratch,
        input_output_aliases=aliases or {},
        compiler_params=pltpu.CompilerParams(vmem_limit_bytes=vmem),
        cost_estimate=NOTHING,
        name=name,
    )(*args)


def gate_kernel(*refs):
    pass


class Line:
    def __init__(self):
        self.mark = jnp.zeros((8, LANES), F32)

    def __call__(self, *arrays):
        held = (*arrays, self.mark)
        *held, self.mark = run_kernel(
            gate_kernel, [shaped(v.shape, v.dtype) for v in held], [ANYWHERE] * len(held), [ANYWHERE] * len(held),
            held, "gate", aliases={n: n for n in range(len(held))},
        )
        return held[0] if len(held) == 1 else held


def spot(place, b, width):
    return pl.ds(pl.multiple_of(place[SPOT + b] * width, width), width)


def places(axis, shape, count, shift):
    at = lax.broadcasted_iota(jnp.int32, shape, axis) + shift
    return jnp.where(at >= count, at - count, at)


def full_lanes(n):
    return n + -n % LANES


def take_weights(parts, gain_ref, dests):
    both, far, passed = parts
    for b in range(16):
        lanes = slice(b * LANES, (b + 1) * LANES)
        block = both[b].astype(F32) if b < 8 else far[b - 8].astype(F32) + passed[b - 8].astype(F32)
        for lo, hi, to, at, gained in dests:
            rows = block[lo:hi]
            to[at : at + hi - lo, lanes] = (rows * gain_ref[:, lanes] if gained else rows).astype(BF)


def give_grads(acc1, acc2, col, gain_ref, shift_ref, w1, to1, to2, norm_ref):
    for b in range(16):
        lanes = slice(b * LANES, (b + 1) * LANES)
        gain = gain_ref[:, lanes]
        m = acc1[:, lanes]
        w = w1[:, lanes].astype(F32)
        for (own, rest, at), v in ((to1, m * gain + col[...] * shift_ref[:, lanes]), (to2, acc2[:, lanes])):
            to, k = (own, b) if b < 4 else (rest, b - 4)
            to[k, at : at + v.shape[0]] = v.astype(BF)
        norm_ref[0:1, lanes] = jnp.sum(w * m, axis=0, keepdims=True) / gain
        norm_ref[1:2, lanes] = jnp.sum(w * col[...], axis=0, keepdims=True) / gain


def stream(step, pieces, unit_buf, cot_buf, sems):
    rows = pieces[0].shape[1]
    steps = len(pieces) // 2

    def copies(s):
        made = []
        for k in (2 * s, 2 * s + 1):
            for n, buffer in enumerate((unit_buf, cot_buf)):
                to = buffer.at[s % 2, pl.ds((k % 2) * rows, rows)]
                made.append(pltpu.make_async_copy(pieces[k].at[n], to, sems.at[s % 2, len(made)]))
        return made

    def begin(s):
        for c in copies(s):
            c.start()

    def arrive():
        for s in range(steps):
            @pl.when(step == s)
            def _(s=s):
                if s + 1 < steps:
                    begin(s + 1)
                for c in copies(s):
                    c.wait()

    return begin, arrive


def stream_scratch(rows, width):
    return [pltpu.VMEM((2, rows, width), BF), pltpu.VMEM((2, rows, width), BF), pltpu.SemaphoreType.DMA((2, 4))]


def feed_kernel(cols, split, *refs):
    pieces, parts, refs = refs[:8], refs[8:11], refs[11:]
    gain_ref, shift_ref, ratio_ref, bias_ref = refs[:4]
    hidden_ref, pre_grad_ref, w1, w2, norm_ref, sum_ref = refs[4:10]
    grads, refs = refs[10 : 10 + 2 * split], refs[10 + 2 * split :]
    acc1, acc2, col, row, unit_buf, cot_buf, sems = refs
    step = pl.program_id(0)
    begin, arrive = stream(step, pieces, unit_buf, cot_buf, sems)

    @pl.when(step == 0)
    def _():
        begin(0)
        take_weights(parts, gain_ref, ((0, cols, w1, 0, True), (cols, 2 * cols, w2, 0, False)))
        row[...] = jnp.sum(dot(ratio_ref[...], w1[...], NT), axis=0, keepdims=True) + bias_ref[...]
        acc1[...] = jnp.zeros_like(acc1)
        acc2[...] = jnp.zeros_like(acc2)
        col[...] = jnp.zeros_like(col)
        sum_ref[...] = jnp.zeros_like(sum_ref)

    arrive()
    slot = lax.rem(step, 2)
    unit = unit_buf[slot]
    cot = cot_buf[slot]
    pre = dot(unit, w1[...], NT) + row[...]
    back = dot(cot, w2[...], NT)
    phi = 0.5 * (1.0 + lax.erf(pre * (1.0 / math.sqrt(2.0))))
    slope = phi + pre * (jnp.exp(-0.5 * pre * pre) * (1.0 / math.sqrt(2.0 * math.pi)))
    hidden = (pre * phi).astype(BF)
    pre_grad = (back * slope).astype(BF)
    hidden_ref[...] = hidden
    pre_grad_ref[...] = pre_grad
    acc1[...] += dot(pre_grad, unit, TN)
    acc2[...] += dot(hidden, cot, TN)
    col[...] += dot(pre_grad, jnp.ones((pre_grad.shape[0], LANES), BF), TN)
    sum_ref[...] += jnp.sum(pre_grad.astype(F32), axis=0, keepdims=True)

    @pl.when(step == pl.num_programs(0) - 1)
    def _():
        to1 = (*grads[:2], 0)
        to2 = (*grads[2:], 0) if split == 2 else (*grads[:2], cols)
        give_grads(acc1, acc2, col, gain_ref, shift_ref, w1, to1, to2, norm_ref)


def chunk_call(kernel, name, pieces, extra_in, extra_specs, sets, vectors, cols, others, split):
    _, part, width = pieces[0].shape
    block, rows = 2 * part, 8 * part
    per_row = lambda n: pl.BlockSpec((block, n), lambda r: (r, 0))
    shapes = [
        shaped((rows, others)), shaped((rows, cols)), shaped((cols, width)), shaped((others, width)),
        shaped((2, width), F32), shaped((1, cols), F32),
    ]
    specs = [per_row(others), per_row(cols)] + [whole(s.shape) for s in shapes[2:]]
    for n in (cols, others) if split == 2 else (cols + others,):
        shapes += [shaped((4, n, LANES)), shaped((12, n, LANES))]
    specs += [whole(s.shape) for s in shapes[6:]]
    weights = [w for s in sets for w in s]
    return run_kernel(
        kernel, shapes,
        [ANYWHERE] * 8 + [whole(w.shape) for w in weights] + [whole(v.shape) for v in vectors] + extra_specs,
        specs, (*pieces, *weights, *vectors, *extra_in), name, grid=(rows // block,),
        scratch=[
            pltpu.VMEM((cols, width), F32), pltpu.VMEM((others, width), F32), pltpu.VMEM((cols, LANES), F32),
            pltpu.VMEM((1, cols), F32),
        ]
        + stream_scratch(block, width),
        vmem=VMEM_LIMIT,
    )


def attention_kernel(cols, *refs):
    pieces, refs = refs[:8], refs[8:]
    set_one, set_two, refs = refs[:3], refs[3:6], refs[6:]
    gain_ref, shift_ref, ratio_ref, bias_ref, lengths, place, cos_ref, sin_up_ref, sin_down_ref = refs[:9]
    mixed_ref, qkv_grad_ref, w1, w2, norm_ref, sum_ref, own_ref, rest_ref = refs[9:17]
    acc1, acc2, col, row, unit_buf, cot_buf, sems = refs[17:]
    group = pl.program_id(0)
    begin, arrive = stream(group, pieces, unit_buf, cot_buf, sems)

    @pl.when(group == 0)
    def _():
        begin(0)
        take_weights(set_one, gain_ref, ((0, 2 * HD, w1, 0, True),))
        take_weights(set_two, gain_ref, ((0, HD, w1, 2 * HD, True), (HD, 2 * HD, w2, 0, False)))
        row[...] = jnp.sum(dot(ratio_ref[...], w1[...], NT), axis=0, keepdims=True) + bias_ref[...]
        acc1[...] = jnp.zeros_like(acc1)
        acc2[...] = jnp.zeros_like(acc2)
        col[...] = jnp.zeros_like(col)
        sum_ref[...] = jnp.zeros_like(sum_ref)

    arrive()
    slot = lax.rem(group, 2)
    unit = unit_buf[slot]
    cot = cot_buf[slot]
    count = unit.shape[0]
    cosine, sin_up, sin_down = cos_ref[...], sin_up_ref[...], sin_down_ref[...]
    half = ROT // 2

    def turn(u):
        p = u[:, :LANES]
        p = p * cosine + pltpu.roll(p, LANES - half, 1) * sin_up + pltpu.roll(p, half, 1) * sin_down
        return jnp.concatenate([p, u[:, LANES:]], axis=1)

    def unturn(u):
        p = u[:, :LANES]
        p = p * cosine + pltpu.roll(p * sin_up, half, 1) + pltpu.roll(p * sin_down, LANES - half, 1)
        return jnp.concatenate([p, u[:, LANES:]], axis=1)

    qkv = dot(unit, w1[...], NT) + row[...]
    query = turn(qkv[:, :HD]).astype(BF)
    key = turn(qkv[:, HD : 2 * HD]).astype(BF)
    value = qkv[:, 2 * HD :].astype(BF)
    back = dot(cot, w2[...], NT).astype(BF)

    shift = place[SIDE] * (count // 2)
    at = places(0, (count, 1), count, shift)
    to = places(1, (1, count), count, shift)
    end, seg_at, seg_to = 0, jnp.zeros_like(at), jnp.zeros_like(to)
    for k in range(DOCS):
        end = end + lengths[group, k]
        seg_at = seg_at + jnp.where(at >= end, 1, 0)
        seg_to = seg_to + jnp.where(to >= end, 1, 0)
    seg_at = jnp.where(seg_at == DOCS, DOCS + at, seg_at)
    seg_to = jnp.where(seg_to == DOCS, DOCS + to, seg_to)
    visible = (seg_at == seg_to) & (to <= at)

    scale = 1.0 / math.sqrt(HD)
    scores = jnp.where(visible, dot(query, key, NT) * scale, -1e30)
    expo = jnp.exp(scores - jnp.max(scores, axis=1, keepdims=True))
    probs = expo / jnp.sum(expo, axis=1, keepdims=True)
    low = probs.astype(BF)
    mixed = dot(low, value, NN).astype(BF)
    value_grad = dot(low, back, TN)
    probs_grad = dot(back, value, NT)
    inner = jnp.sum(probs * probs_grad, axis=1, keepdims=True)
    score_grad = (probs * (probs_grad - inner)).astype(BF)
    query_grad = unturn(dot(score_grad, key, NN) * scale)
    key_grad = unturn(dot(score_grad, query, TN) * scale)
    qkv_grad = jnp.concatenate([query_grad, key_grad, value_grad], axis=1).astype(BF)
    mixed_ref[...] = mixed
    qkv_grad_ref[...] = qkv_grad
    acc1[...] += dot(qkv_grad, unit, TN)
    acc2[...] += dot(mixed, cot, TN)
    col[...] += dot(qkv_grad, jnp.ones((count, LANES), BF), TN)
    sum_ref[...] += jnp.sum(qkv_grad.astype(F32), axis=0, keepdims=True)

    @pl.when(group == pl.num_programs(0) - 1)
    def _():
        give_grads(acc1, acc2, col, gain_ref, shift_ref, w1, (own_ref, rest_ref, 0), (own_ref, rest_ref, cols), norm_ref)


def join_kernel(n, *refs):
    total = dot(refs[0][...], refs[n][...], NN)
    for j in range(1, n):
        total += dot(refs[j][...], refs[n + j][...], NN)
    refs[2 * n][...] = total.astype(BF)


def join_call(acts, weights, sent):
    rows, width = acts[0].shape[0], weights[0].shape[1]
    block = rows // 8
    first = 2 if sent else 0
    return run_kernel(
        functools.partial(join_kernel, len(acts)),
        shaped((rows // 2, width)),
        [pl.BlockSpec((block, a.shape[1]), lambda r: (4 * (r // 2) + r % 2 + first, 0)) for a in acts]
        + [whole(w.shape) for w in weights],
        pl.BlockSpec((block, width), lambda r: (r, 0)),
        (*acts, *weights),
        "join",
        grid=(4,),
        vmem=VMEM_LIMIT,
    )


def own_kernel(place, x_ref, cot_ref, out_ref, sum_ref):
    x = x_ref[...].astype(F32)
    centred = x - jnp.mean(x, axis=1, keepdims=True)
    spread = jnp.mean(centred * centred, axis=1, keepdims=True)
    unit = (centred * lax.rsqrt(spread + EPSILON)).astype(BF)
    width = x.shape[1] // 4
    for b in range(4):
        out_ref[0, :, spot(place, b, width)] = unit[:, b * width : (b + 1) * width]
        out_ref[1, :, spot(place, b, width)] = cot_ref[:, b * width : (b + 1) * width]

    @pl.when(pl.program_id(0) == 0)
    def _():
        sum_ref[...] = jnp.zeros_like(sum_ref)

    sum_ref[...] += jnp.sum(cot_ref[...].astype(F32), axis=0, keepdims=True)


def own_call(place, x, cot):
    rows, width = x.shape
    spec = pl.BlockSpec((rows // STEPS, width), lambda r: (r, 0))
    return run_kernel(
        own_kernel, [shaped((2, rows, width)), shaped((1, width), F32)], [SCALARS, spec, spec],
        [pl.BlockSpec((2, rows // STEPS, width), lambda r: (0, r, 0)), pl.BlockSpec((1, width), lambda r: (0, 0))],
        (place, x, cot), "own", grid=(STEPS,),
    )


def part_specs(parts, strip):
    specs = []
    for cross, n, first, every in parts:
        if cross:
            specs.append(pl.BlockSpec((strip, n), functools.partial(lambda f, e, k: (0, k * e + f), first, every)))
        else:
            specs.append(pl.BlockSpec((n, strip), functools.partial(lambda f, e, k: (k * e + f, 0), first, every)))
    return specs


def piece_kernel(parts, *refs):
    out_ref, at = refs[-1], 0
    for (cross, n, *_), ref in zip(parts, refs):
        out_ref[0, at : at + n] = ref[...].astype(F32).T.astype(BF) if cross else ref[...]
        at += n


def piece_call(arrays, parts, strip):
    n = sum(p[1] for p in parts)
    return run_kernel(
        functools.partial(piece_kernel, parts), shaped((INNER, n, strip)), part_specs(parts, strip),
        pl.BlockSpec((1, n, strip), lambda k: (k, 0, 0)), arrays, "piece", grid=(INNER,),
    )


def unpiece_kernel(parts, *refs):
    v_ref, outs, at = refs[0], refs[-len(parts) :], 0
    for (cross, n, *_), ref in zip(parts, outs):
        v = v_ref[0, at : at + n].astype(F32)
        ref[...] = v.T if cross else v
        at += n


def unpiece_call(v, shapes, parts, held):
    _, n, strip = v.shape
    held = [h for h in held if h is not None]
    return run_kernel(
        functools.partial(unpiece_kernel, parts), [shaped(s, F32) for s in shapes],
        [pl.BlockSpec((1, n, strip), lambda k: (k, 0, 0))] + [ANYWHERE] * len(held),
        part_specs(parts, strip), (v, *held), "unpiece", grid=(INNER,),
        aliases={1 + k: k for k in range(len(held))},
    )


def cat_kernel(a, b, out):
    out[0] = a[...]
    out[1] = b[...]


def cat_call(a, b):
    n = a.shape[0] // 2
    spec = pl.BlockSpec((n,) + a.shape[1:], lambda k: (k, 0, 0))
    out = run_kernel(
        cat_kernel, shaped((2,) + a.shape), [spec, spec],
        pl.BlockSpec((2, n) + a.shape[1:], lambda k: (0, k, 0, 0)), (a, b), "cat", grid=(2,),
    )
    return out.reshape((8,) + a.shape[1:])


def vectors_kernel(piece, nq, nf, share, tensor, place, small, g1, s1, g2, s2, r1, r2, out_bias, bq, bf, lengths):
    total = small.shape[0]
    per = total // 4
    width = per * piece

    def lay(to, b, k, where):
        part = small[b * per : (b + 1) * per, k * piece : (k + 1) * piece]
        to[:, where] = jnp.concatenate([part[r : r + 1] for r in range(per)], axis=1)

    for b in range(4):
        for k, to in enumerate((g1, s1, g2, s2)):
            lay(to, b, k, spot(place, b, width))
        lay(out_bias, b, 4, slice(b * width, (b + 1) * width))
    for gain, shift, ratio in ((g1, s1, r1), (g2, s2, r2)):
        v = shift[...] / gain[...]
        high = v.astype(BF).astype(F32)
        ratio[...] = jnp.concatenate([high, v - high, jnp.zeros((14, v.shape[1]), F32)], axis=0).astype(BF)
    at = 5 * piece
    for k in range(share):
        row = small[pl.ds((place[INSIDE] * share + k) * tensor + place[SIDE], 1), :]
        bq[:, k * nq : (k + 1) * nq] = row[:, at : at + nq]
        bf[:, k * nf : (k + 1) * nf] = row[:, at + nq : at + nq + nf]
    for g in range(INNER):
        row = small[pl.ds(place[DOC_ROW + g], 1), :]
        docs = row[:, at + nq + nf : at + nq + nf + LANES]
        lengths[g : g + 1] = (docs + 0.5).astype(jnp.int32)


def turns_kernel(own_rows, place, lengths, cos_ref, up_ref, down_ref):
    count = cos_ref.shape[0]
    group = pl.program_id(0)
    at = places(0, (count, 1), count, place[SIDE] * own_rows)
    end, begin = 0, jnp.zeros_like(at)
    for k in range(DOCS):
        end = end + lengths[group, k]
        begin = jnp.where(at >= end, end, begin)
    half = ROT // 2
    lane = lax.broadcasted_iota(jnp.int32, (1, LANES), 1)
    step = jnp.where(lane >= half, lane - half, lane).astype(F32)
    freq = jnp.exp(step * (-2.0 * math.log(10000.0) / ROT))
    angle = (at - begin).astype(F32) * freq
    sine = jnp.sin(angle)
    cos_ref[...] = jnp.where(lane < ROT, jnp.cos(angle), 1.0)
    up_ref[...] = jnp.where(lane < half, -sine, 0.0)
    down_ref[...] = jnp.where((lane >= half) & (lane < ROT), sine, 0.0)


def sum_kernel(*refs):
    total = refs[0][...].astype(F32)
    for r in refs[1:-1]:
        total += r[...].astype(F32)
    refs[-1][...] = total.astype(BF)


def sum_call(parts, firsts, count):
    shape = (4,) + parts[0].shape[1:]
    return run_kernel(
        sum_kernel,
        shaped((count,) + shape[1:]),
        [pl.BlockSpec(shape, functools.partial(lambda f, k: (k + f, 0, 0), f // 4)) for f in firsts],
        pl.BlockSpec(shape, lambda k: (k, 0, 0)),
        parts,
        "sum",
        grid=(count // 4,),
        vmem=VMEM_LIMIT,
    )


def core_kernel(kt, kx, kb, ot, ox, ob, x1, t1):
    half = kt.shape[1] // 2
    add = lambda a, b, cut: (a[:, cut].astype(F32) + b[:, cut].astype(F32)).astype(BF)
    left, right = slice(0, half), slice(half, 2 * half)
    x1[:, left] = add(kb, ob, left)
    x1[:, right] = add(kx, ox, left)
    t1[:, left] = add(kb, ob, right)
    t1[:, right] = add(kt, ot, right)


def cross_kernel(kt, kx, ot, ox, x1, t1, t2, x2):
    half = kt.shape[1] // 2
    left, right = slice(0, half), slice(half, 2 * half)
    add = lambda a, b, c: (a.astype(F32) + b.astype(F32) + c.astype(F32)).astype(BF)
    t2[...] = add(kt[:, left], ot[:, left], x1[:, left])
    x2[...] = add(kx[:, right], ox[:, right], t1[:, left])


def face_sum(place, kept, other, x1, t1, t2, x2, natural):
    half = kept.shape[1] // 2
    left, right = slice(0, half), slice(half, 2 * half)
    natural[:, left] = kept[:, left].astype(F32) + other[:, left].astype(F32) + x1[:, right].astype(F32) + t2[...].astype(F32)
    natural[:, right] = (
        kept[:, right].astype(F32) + other[:, right].astype(F32) + t1[:, right].astype(F32) + x2[...].astype(F32)
    )
    return jnp.concatenate([natural[:, spot(place, b, half // 2)] for b in range(4)], axis=1)


def output_kernel(place, x_ref, bias_ref, kept, other, x1, t1, t2, x2, out_ref, natural):
    total = face_sum(place, kept, other, x1, t1, t2, x2, natural) + bias_ref[...] + x_ref[...].astype(F32)
    out_ref[...] = total.astype(BF)


def input_grad_kernel(place, x_ref, cot_ref, kept, other, x1, t1, t2, x2, out_ref, natural):
    pulled = face_sum(place, kept, other, x1, t1, t2, x2, natural)
    x = x_ref[...].astype(F32)
    centred = x - jnp.mean(x, axis=1, keepdims=True)
    rstd = lax.rsqrt(jnp.mean(centred * centred, axis=1, keepdims=True) + EPSILON)
    unit = centred * rstd
    along = jnp.mean(pulled * unit, axis=1, keepdims=True)
    level = jnp.mean(pulled, axis=1, keepdims=True)
    out_ref[...] = (cot_ref[...].astype(F32) + rstd * (pulled - level - unit * along)).astype(BF)


def own_rows_call(kernel, place, rows_in, row_in, sums, name):
    rows, width = rows_in[0].shape
    block = rows // STEPS
    spec = pl.BlockSpec((block, width), lambda r: (r, 0))
    half = pl.BlockSpec((block, width // 2), lambda r: (r, 0))
    vector = pl.BlockSpec((1, width), lambda r: (0, 0))
    return run_kernel(
        kernel, shaped((rows, width)),
        [SCALARS] + [spec] * len(rows_in) + [vector] * len(row_in) + [spec] * 4 + [half] * 2,
        spec, (place, *rows_in, *row_in, *sums), name, grid=(STEPS,), scratch=[pltpu.VMEM((block, width), F32)],
    )


def tail_kernel(piece, nq, nf, share, tensor, place, n_attn, n0, n1, n2, sum_q, f0, f1, f2, cot_sum, tail):
    total = tail.shape[0]
    per = total // 4
    width = per * piece
    tail[...] = jnp.zeros_like(tail)

    def lay(k, b, row):
        rows = jnp.concatenate([row[:, r * piece : (r + 1) * piece] for r in range(per)], axis=0)
        tail[b * per : (b + 1) * per, k * piece : (k + 1) * piece] = rows

    for b in range(4):
        at = spot(place, b, width)
        attn = n_attn[:, at]
        feeds = n0[:, at] + n1[:, at] + n2[:, at]
        for k, row in enumerate((attn[0:1], attn[1:2], feeds[0:1], feeds[1:2])):
            lay(k, b, row)
        lay(4, b, cot_sum[:, b * width : (b + 1) * width])
    hidden = jnp.concatenate([f0[...], f1[...], f2[...]], axis=1)
    query = sum_q[...]
    at = full_lanes(5 * piece)
    rest = jnp.zeros((1, full_lanes(nq + nf) - nq - nf), F32)
    line = lax.broadcasted_iota(jnp.int32, (total, 1), 0)
    below = jnp.zeros((total, full_lanes(nq + nf)), F32)
    for k in range(share):
        row = (place[INSIDE] * share + k) * tensor + place[SIDE]
        both = [query[:, k * nq : (k + 1) * nq], hidden[:, k * nf : (k + 1) * nf]]
        both = jnp.concatenate(both + [rest] if rest.shape[1] else both, axis=1)
        below = jnp.where(line == row, both, below)
    tail[:, at:] = below


def make(dp, tensor):
    outer = dp // INNER
    face = INNER * tensor
    total = dp * tensor
    short = outer == 4

    def permute(v, pairs):
        return lax.ppermute(v, AXES, pairs)

    def flip(v, k):
        return permute(v, [(l, l ^ k) for l in range(total)])

    def hop(v, moves):
        return permute(v, [(a * face + f, b * face + f) for a, b in moves for f in range(face)])

    column_groups = [[o * face + f for o in range(outer)] for f in range(face)]
    ring_groups = [[o * face + i * tensor + t for i in range(INNER)] for o in range(outer) for t in range(tensor)]
    towards_middle = [(0, 1), (3, 2)]
    across_middle = [(1, 2), (2, 1)]
    towards_ends = [(1, 0), (2, 3)]

    back_table = [[0, 1, 2, 3], [1, 0, 2, 3], [3, 2, 0, 1], [3, 2, 1, 0]]

    def swap_ring(v):
        return lax.all_to_all(v, AXES, split_axis=0, concat_axis=0, tiled=True, axis_index_groups=ring_groups)

    def swap_all(v):
        return lax.all_to_all(v, AXES, split_axis=0, concat_axis=0, tiled=True)

    class Gather:
        def __init__(self, v):
            if not short:
                every = lax.all_gather(v, AXES, axis=0, tiled=True, axis_index_groups=column_groups)
                n = v.shape[1]
                every = every.transpose(1, 0, 2).reshape(n, 16, LANES).transpose(1, 0, 2)
                self.parts = [every[:8], every[8:], jnp.zeros_like(every[8:])]
                return
            self.own = v
            self.near = flip(v, face)

        def near_came(self, line):
            if short:
                self.own, near = line(self.own, self.near)
                self.both = line(cat_call(self.own, near))
                self.far = hop(self.both, across_middle)

        def far_came(self, line):
            if short:
                self.far = line(self.far)
                self.passed = hop(self.far, towards_ends)

        def passed_came(self, line):
            if short:
                self.parts = list(line(self.both, self.far, self.passed))

    class Reduce:
        def __init__(self, line, own, rest):
            if not short:
                v = jnp.concatenate([own, rest], axis=0)
                v = v.transpose(1, 0, 2).reshape(v.shape[1], dp, -1).transpose(1, 0, 2)
                self.total = lax.psum_scatter(
                    v, AXES, scatter_dimension=0, tiled=True, axis_index_groups=column_groups
                )
                return
            self.own, self.rest = line(own, rest)
            self.first = hop(self.rest, towards_middle)

        def first_came(self, line):
            if short:
                self.rest, self.first = line(self.rest, self.first)
                far = line(sum_call((self.rest, self.first), (4, 4), 8))
                self.second = hop(far, across_middle)

        def second_came(self, line):
            if short:
                self.rest, self.second = line(self.rest, self.second)
                near = line(sum_call((self.rest, self.second), (0, 4), 4))
                self.third = hop(near, towards_ends)

        def third_came(self, line):
            if short:
                self.third = line(self.third)
                self.total = sum_call((self.own, self.first, self.second, self.third), (0, 0, 0, 0), 4)
            self.total = line(self.total)
            self.final = swap_ring(self.total)

    class FaceReduce:
        def __init__(self, sent):
            self.other = flip(sent, 2)

        def core_came(self, line):
            self.kept, self.other = line(self.kept, self.other)
            self.rows, self.width = self.kept.shape[0] // 4, self.kept.shape[1]
            spec = pl.BlockSpec((self.rows // STEPS, self.width), lambda r: (r, 0))
            x1, t1 = run_kernel(
                core_kernel, [shaped((self.rows, self.width))] * 2, self.block_specs(1, 2, 3) * 2, [spec] * 2,
                (self.kept,) * 3 + (self.other,) * 3, "core", grid=(STEPS,),
            )
            x1, t1 = line(x1, t1)
            self.x1, self.t1 = flip(x1, 4), flip(t1, 1)

        def block_specs(self, *blocks):
            block = self.rows // STEPS
            return [
                pl.BlockSpec((block, self.width), functools.partial(lambda k, r: (k * STEPS + r, 0), k)) for k in blocks
            ]

        def first_came(self, line):
            self.x1, self.t1 = line(self.x1, self.t1)
            rows, width = self.rows, self.width
            spec = pl.BlockSpec((rows // STEPS, width), lambda r: (r, 0))
            half = pl.BlockSpec((rows // STEPS, width // 2), lambda r: (r, 0))
            t2, x2 = run_kernel(
                cross_kernel, [shaped((rows, width // 2))] * 2, self.block_specs(1, 2) * 2 + [spec] * 2, [half] * 2,
                (self.kept, self.kept, self.other, self.other, self.x1, self.t1), "cross", grid=(STEPS,),
            )
            t2, x2 = line(t2, x2)
            self.t2, self.x2 = flip(t2, 1), flip(x2, 4)

        def second_came(self, line):
            self.t2, self.x2 = line(self.t2, self.x2)
            return self.kept, self.other, self.x1, self.t1, self.t2, self.x2

    def per_device(
        layer_input, doc_lengths, ln1_gain, ln1_bias, ln2_gain, ln2_bias, w_qkv, b_qkv, w_dense, b_dense,
        w_fc1, b_fc1, w_fc2, b_fc2, cotangent,
    ):
        d, t = lax.axis_index("dp"), lax.axis_index("tensor")
        o, i = d // INNER, d % INNER
        own_rows, width = layer_input.shape
        rows, group_rows = own_rows * face, own_rows * tensor
        strip = width // dp
        hidden_own = w_fc1.shape[1] // INNER
        qkv_own = w_qkv.shape[1] // INNER
        quarter = hidden_own // 4
        piece, nq, nf = width // total, b_qkv.shape[0], b_fc1.shape[0]
        share = dp // INNER
        line = Line()
        if short:
            spots = jnp.array(back_table, jnp.int32)[o]
        else:
            spots = jnp.arange(4, dtype=jnp.int32)
        doc_rows = (o * INNER + (i ^ jnp.arange(INNER, dtype=jnp.int32))) * tensor
        place = jnp.concatenate([jnp.stack([o, i, t]).astype(jnp.int32), spots, doc_rows.astype(jnp.int32)])

        forms = [
            ((w_fc1, w_fc2), ((True, quarter, 0, 4), (False, quarter, 0, 4))),
            ((w_fc1, w_fc2), ((True, quarter, 1, 4), (False, quarter, 1, 4))),
            ((w_qkv, w_qkv), ((True, HD, 0, 3), (True, HD, 1, 3))),
            ((w_qkv, w_dense), ((True, HD, 2, 3), (False, HD, 0, 1))),
            ((w_fc1, w_fc2), ((True, 2 * quarter, 1, 2), (False, 2 * quarter, 1, 2))),
        ]
        s = {}
        steps = {}

        def own():
            s["own"], s["cot_sum"] = own_call(place, *line(layer_input, cotangent))
            s["own"] = line(s["own"])
            s["t"], s["x"], s["c"] = flip(s["own"], 1), flip(s["own"], 4), flip(s["own"], 2)

        def own_c():
            s["c"] = line(s["c"])

        def own_xt():
            s["x"], s["t"] = line(s["x"], s["t"])
            s["b"], s["tc"], s["xc"] = flip(s["x"], 1), flip(s["t"], 2), flip(s["x"], 2)

        def own_tc():
            s["tc"], s["xc"] = line(s["tc"], s["xc"])

        def own_b():
            s["b"] = line(s["b"])
            s["bc"] = flip(s["b"], 2)

        def own_bc():
            s["bc"] = line(s["bc"])

        steps.update({"own": own, "c": own_c, "xt": own_xt, "tc": own_tc, "b": own_b, "bc": own_bc})

        def small():
            v = jnp.concatenate(
                [ln1_gain, ln1_bias, ln2_gain, ln2_bias, b_dense + b_fc2, b_qkv.astype(F32), b_fc1.astype(F32),
                 doc_lengths[0].astype(F32), jnp.zeros((LANES - DOCS,), F32)]
            )
            s["small"] = swap_all(line(jnp.broadcast_to(v[None], (total, v.shape[0]))))

        def vectors():
            v = line(s["small"]).reshape(total, -1)
            row, fine = shaped((1, width), F32), shaped((16, width))
            *s["vec"], s["bias_q"], s["bias_f"], s["lengths"] = run_kernel(
                functools.partial(vectors_kernel, piece, nq, nf, share, tensor),
                [row] * 4 + [fine] * 2 + [row, shaped((1, qkv_own), F32), shaped((1, hidden_own), F32),
                                          shaped((INNER, LANES), jnp.int32)],
                [SCALARS, VECTORS], [VECTORS] * 10, (place, v), "vectors",
            )
            turn_spec = pl.BlockSpec((group_rows, LANES), lambda g: (g, 0))
            turns = run_kernel(
                functools.partial(turns_kernel, own_rows), [shaped((rows, LANES), F32)] * 3, [SCALARS] * 2,
                [turn_spec] * 3, (place, s["lengths"]), "turns", grid=(INNER,),
            )
            s["turns"] = line(*turns)

        steps.update({"sm": small, "vec": vectors})
        gathers, done, sums = {}, {}, {}

        def gather_steps(k):
            def p():
                arrays, parts = forms[k]
                s[f"ring{k}"] = swap_ring(line(piece_call(arrays, parts, strip)))

            def g():
                gathers[k] = Gather(line(s[f"ring{k}"]))

            steps.update({
                f"p{k}": p, f"g{k}": g, f"h{k}": lambda: gathers[k].near_came(line),
                f"i{k}": lambda: gathers[k].far_came(line), f"j{k}": lambda: gathers[k].passed_came(line),
            })

        for k in range(5):
            gather_steps(k)

        def pieces():
            return [s[n] for n in ("own", "t", "c", "tc", "x", "b", "xc", "bc")]

        def feed(k, first, count):
            def run():
                gain, shift, ratio = s["vec"][2], s["vec"][3], s["vec"][5]
                bias = s["bias_f"][:, first * quarter : (first + count) * quarter]
                cols, split = count * quarter, count
                parts = gathers[k].parts
                parts[0] = line(parts[0])
                done[k] = list(chunk_call(
                    functools.partial(feed_kernel, cols, split), "feed", pieces(), (), [], [parts],
                    (gain, shift, ratio, bias), cols, cols, split,
                ))
                done[k][5] = line(done[k][5])

            return run

        def attention():
            gain, shift, ratio = s["vec"][0], s["vec"][1], s["vec"][4]
            one, two = gathers[2].parts, gathers[3].parts
            one[0] = line(one[0])
            turn_spec = pl.BlockSpec((group_rows, LANES), lambda r: (r, 0))
            done[2] = list(chunk_call(
                functools.partial(attention_kernel, qkv_own), "attention", pieces(),
                (s["lengths"], place, *s["turns"]), [SCALARS, SCALARS] + [turn_spec] * 3, [one, two],
                (gain, shift, ratio, s["bias_q"]), qkv_own, HD, 1,
            ))
            done[2][5] = line(done[2][5])

        steps.update({"K0": feed(0, 0, 1), "K1": feed(1, 1, 1), "KA": attention, "K4": feed(4, 2, 2)})

        def reduce_steps(k, chunk, at):
            def r():
                sums[k] = Reduce(line, *done[chunk][at : at + 2])

            def z():
                final = line(sums[k].final)
                if k == 2:
                    s["qkv"], s["dense"] = line(*unpiece_call(
                        final, (w_qkv.shape, w_dense.shape), ((True, qkv_own, 0, 1), (False, HD, 0, 1)), ()
                    ))
                elif k < 2:
                    s["fc1"], s["fc2"] = line(*unpiece_call(
                        final, (w_fc1.shape, w_fc2.shape), forms[k][1], (s.get("fc1"), s.get("fc2"))
                    ))
                else:
                    name, w, form = (("fc1", w_fc1, 0), ("fc2", w_fc2, 1))[k - 3]
                    s[name] = line(*unpiece_call(final, (w.shape,), forms[4][1][form : form + 1], (s[name],)))

            steps.update({
                f"r{k}": r, f"u{k}": lambda: sums[k].first_came(line), f"v{k}": lambda: sums[k].second_came(line),
                f"w{k}": lambda: sums[k].third_came(line), f"z{k}": z,
            })

        for k, chunk, at in ((0, 0, 6), (1, 1, 6), (2, 2, 6), (3, 4, 6), (4, 4, 8)):
            reduce_steps(k, chunk, at)

        def face_steps(name, act, weight, finish):
            def parts():
                chunks = [done[k] for k in (0, 1, 2, 4)]
                return [c[act] for c in chunks], [c[weight] for c in chunks]

            def sent():
                acts, weights = parts()
                acts[0] = line(acts[0])
                s["face" + name] = FaceReduce(line(join_call(acts, weights, True)))

            def kept():
                acts, weights = parts()
                acts[0] = line(acts[0])
                s["face" + name].kept = line(join_call(acts, weights, False))

            steps.update({
                "J" + name: sent, "k" + name: kept, "C" + name: lambda: s["face" + name].core_came(line),
                "D" + name: lambda: s["face" + name].first_came(line),
                "E" + name: lambda: finish(s["face" + name].second_came(line)),
            })

        def finish_back(sums_in):
            s["input_grad"] = line(
                own_rows_call(input_grad_kernel, place, (layer_input, cotangent), (), sums_in, "input_grad")
            )

        def finish_out(sums_in):
            s["output"] = line(own_rows_call(output_kernel, place, (layer_input,), (s["vec"][6],), sums_in, "output"))

        face_steps("B", 1, 2, finish_back)
        face_steps("O", 0, 3, finish_out)

        def tail():
            feeds = [done[k] for k in (0, 1, 4)]
            v = run_kernel(
                functools.partial(tail_kernel, piece, nq, nf, share, tensor),
                shaped((total, full_lanes(5 * piece) + full_lanes(nq + nf)), F32), [SCALARS] + [VECTORS] * 9, VECTORS,
                (place, done[2][4], *[p[4] for p in feeds], done[2][5], *[p[5] for p in feeds], s["cot_sum"]), "tail",
            )
            s["tail"] = swap_all(line(v))

        def tail_came():
            s["tail"] = jnp.sum(line(s["tail"]), axis=0)

        steps.update({"tail": tail, "tz": tail_came})
        for name in ORDER:
            steps[name]()

        tail_row = s["tail"]
        cuts = [tail_row[j * piece : (j + 1) * piece] for j in range(5)]
        at = full_lanes(5 * piece)
        return (
            s["output"], s["input_grad"], cuts[0], cuts[1], cuts[2], cuts[3], s["qkv"], tail_row[at : at + nq],
            s["dense"], cuts[4], s["fc1"], tail_row[at + nq : at + nq + nf], s["fc2"], cuts[4],
        )

    return per_device


def solution(mesh):
    rows = P(("dp", "tensor"), None)
    vector = P(("dp", "tensor"))
    crossed = P(("tensor", "dp"))
    wide = P("dp", "tensor")
    tall = P("tensor", "dp")
    return jax.shard_map(
        make(mesh.shape["dp"], mesh.shape["tensor"]),
        mesh=mesh,
        in_specs=(rows, P("dp", None), vector, vector, vector, vector, wide, crossed, tall, vector, wide, crossed,
                  tall, vector, rows),
        out_specs=(rows, rows, vector, vector, vector, vector, wide, crossed, tall, vector, wide, crossed, tall,
                   vector),
        check_vma=False,
    )
```

```python
import functools
import math

import jax
import jax.numpy as jnp
from jax import lax
from jax.experimental import pallas as pl
from jax.experimental.pallas import tpu as pltpu
from jax.sharding import PartitionSpec as P

HD = 256
ROT = 64
DOCS = 3
EPSILON = 1e-05
INNER = 4
LANES = 128
AXES = ("dp", "tensor")
BF = jnp.bfloat16
F32 = jnp.float32
NT = ((1,), (1,))
NN = ((1,), (0,))
TN = ((0,), (0,))
VMEM = 63 * 2**20
STEPS = 4


ORDER = (
    "p0", "p2", "g0", "g2", "own", "h0", "h1", "sm", "i0", "c", "h2", "h3", "sw", "xt", "i1", "vec", "j0", "p4",
    "b", "j1", "i2", "g4", "bc", "tc", "K0", "r0", "i3", "h4", "K1", "i4", "j2", "j3", "r1", "KA", "r2", "u0", "j4",
    "u1", "K4", "r3", "r4", "v0", "JB", "v1", "JO", "u2", "kB", "w0", "CB", "kO", "u3", "z0", "v2", "CO", "DB",
    "tail", "v3", "u4", "w2", "tz", "w1", "DO", "z2", "EO", "v4", "w3", "EB", "z1", "w4", "z3", "z4",
)

NOTHING = pl.CostEstimate(flops=0, bytes_accessed=0, transcendentals=0)
SCALARS = pl.BlockSpec(memory_space=pltpu.SMEM)
ANYWHERE = pl.BlockSpec(memory_space=pl.ANY)
VECTORS = pl.BlockSpec(memory_space=pltpu.VMEM)

OUTER, INSIDE, SIDE, SPOT, DOC_ROW = 0, 1, 2, 3, 7


def dot(a, b, dims):
    return lax.dot_general(a, b, (dims, ((), ())), preferred_element_type=F32)


def shaped(shape, dtype=BF):
    return jax.ShapeDtypeStruct(shape, dtype)


def whole(shape):
    return pl.BlockSpec(shape, lambda *_: (0,) * len(shape), pipeline_mode=pl.Buffered(1))


def run_kernel(
    kernel, outs, in_specs, out_specs, args, name, grid=(), scratch=(), aliases=None, line=None
):
    one = not isinstance(outs, (list, tuple))
    outs, out_specs = ([outs], [out_specs]) if one else (list(outs), list(out_specs))
    in_specs, args, aliases, inner = list(in_specs), list(args), dict(aliases or {}), kernel
    if line is not None:
        n, m = len(args), len(outs)
        aliases[n] = m
        in_specs.append(ANYWHERE)
        out_specs.append(ANYWHERE)
        args.append(line.mark)
        outs.append(shaped(line.mark.shape, line.mark.dtype))

        def inner(*refs):
            kernel(*refs[:n], *refs[n + 1 : n + 1 + m], *refs[n + 2 + m :])

    got = pl.pallas_call(
        inner,
        grid=grid,
        out_shape=outs,
        in_specs=in_specs,
        out_specs=out_specs,
        scratch_shapes=scratch,
        input_output_aliases=aliases,
        compiler_params=pltpu.CompilerParams(vmem_limit_bytes=VMEM),
        cost_estimate=NOTHING,
        name=name,
    )(*args)
    if line is not None:
        *got, line.mark = got
    return got[0] if one else got


def gate_kernel(*refs):
    pass


class Line:
    def __init__(self):
        self.mark = jnp.zeros((8, LANES), F32)

    def __call__(self, *arrays):
        held = (*arrays, self.mark)
        *held, self.mark = run_kernel(
            gate_kernel, [shaped(v.shape, v.dtype) for v in held], [ANYWHERE] * len(held), [ANYWHERE] * len(held),
            held, "gate", aliases={n: n for n in range(len(held))},
        )
        return held[0] if len(held) == 1 else held


def spot(place, b, width):
    return pl.ds(pl.multiple_of(place[SPOT + b] * width, width), width)


def places(axis, shape, count, shift):
    at = lax.broadcasted_iota(jnp.int32, shape, axis) + shift
    return jnp.where(at >= count, at - count, at)


def full_lanes(n):
    return n + -n % LANES


def take_weights(parts, gain_ref, dests):
    both, far, passed = parts
    for b in range(16):
        lanes = slice(b * LANES, (b + 1) * LANES)
        block = both[b].astype(F32) if b < 8 else far[b - 8].astype(F32) + passed[b - 8].astype(F32)
        for lo, hi, to, at, gained in dests:
            rows = block[lo:hi]
            to[at : at + hi - lo, lanes] = (rows * gain_ref[:, lanes] if gained else rows).astype(BF)


def give_grads(blocks, acc1, acc2, col, gain_ref, shift_ref, w1, to1, to2, norm_ref):
    for b in blocks:
        lanes = slice(b * LANES, (b + 1) * LANES)
        gain = gain_ref[:, lanes]
        m = acc1[:, lanes]
        w = w1[:, lanes].astype(F32)
        for (own, rest, at), v in ((to1, m * gain + col[...] * shift_ref[:, lanes]), (to2, acc2[:, lanes])):
            to, k = (own, b) if b < 4 else (rest, b - 4)
            to[k, at : at + v.shape[0]] = v.astype(BF)
        norm_ref[0:1, lanes] = jnp.sum(w * m, axis=0, keepdims=True) / gain
        norm_ref[1:2, lanes] = jnp.sum(w * col[...], axis=0, keepdims=True) / gain


def add_grads(step, grad, unit, act, cot, acc1, acc2, col, sum_ref, finish):
    col[...] += dot(grad, jnp.ones((grad.shape[0], LANES), BF), TN)
    sum_ref[...] += jnp.sum(grad.astype(F32), axis=0, keepdims=True)
    last = pl.num_programs(0) - 1

    @pl.when(step < last)
    def _():
        acc1[...] += dot(grad, unit, TN)
        acc2[...] += dot(act, cot, TN)

    @pl.when(step == last)
    def _():
        width = unit.shape[1] // 4
        for part in range(4):
            lanes = slice(part * width, (part + 1) * width)
            acc1[:, lanes] += dot(grad, unit[:, lanes], TN)
            acc2[:, lanes] += dot(act, cot[:, lanes], TN)
            finish(range(4 * part, 4 * part + 4))


def stream(step, pieces, unit_buf, cot_buf, sems):
    blocks = [(p.at[0], p.at[1]) for p in pieces[:6]] + [(pieces[6], pieces[7]), (pieces[8], pieces[9])]
    blocks = [blocks[k] for k in (0, 1, 2, 3, 4, 6, 5, 7)]
    rows = pieces[0].shape[1]
    steps = len(blocks) // 2

    def copies(s):
        made = []
        for k in (2 * s, 2 * s + 1):
            for n, buffer in enumerate((unit_buf, cot_buf)):
                to = buffer.at[s % 2, pl.ds((k % 2) * rows, rows)]
                made.append(pltpu.make_async_copy(blocks[k][n], to, sems.at[s % 2, len(made)]))
        return made

    def begin(s):
        for c in copies(s):
            c.start()

    def arrive():
        for s in range(steps):
            @pl.when(step == s)
            def _(s=s):
                if s + 1 < steps:
                    begin(s + 1)
                for c in copies(s):
                    c.wait()

    return begin, arrive


def stream_scratch(rows, width):
    return [pltpu.VMEM((2, rows, width), BF), pltpu.VMEM((2, rows, width), BF), pltpu.SemaphoreType.DMA((2, 4))]


def feed_kernel(cols, split, sets, *refs):
    pieces, parts, refs = refs[:10], refs[10 : 10 + 3 * sets], refs[10 + 3 * sets :]
    gain_ref, shift_ref, ratio_ref, bias_ref = refs[:4]
    hidden_ref, pre_grad_ref, w1, w2, norm_ref, sum_ref = refs[4:10]
    grads, refs = refs[10 : 10 + 2 * split], refs[10 + 2 * split :]
    acc1, acc2, col, row, unit_buf, cot_buf, sems = refs
    step = pl.program_id(0)
    begin, arrive = stream(step, pieces, unit_buf, cot_buf, sems)

    @pl.when(step == 0)
    def _():
        begin(0)
        n = cols // sets
        for k in range(sets):
            take_weights(parts[3 * k : 3 * k + 3], gain_ref, ((0, n, w1, k * n, True), (n, 2 * n, w2, k * n, False)))
        row[...] = jnp.sum(dot(ratio_ref[...], w1[...], NT), axis=0, keepdims=True) + bias_ref[...]
        acc1[...] = jnp.zeros_like(acc1)
        acc2[...] = jnp.zeros_like(acc2)
        col[...] = jnp.zeros_like(col)
        sum_ref[...] = jnp.zeros_like(sum_ref)

    arrive()
    slot = lax.rem(step, 2)
    unit = unit_buf[slot]
    cot = cot_buf[slot]
    pre = dot(unit, w1[...], NT) + row[...]
    back = dot(cot, w2[...], NT)
    phi = 0.5 * (1.0 + lax.erf(pre * (1.0 / math.sqrt(2.0))))
    slope = phi + pre * (jnp.exp(-0.5 * pre * pre) * (1.0 / math.sqrt(2.0 * math.pi)))
    hidden = (pre * phi).astype(BF)
    pre_grad = (back * slope).astype(BF)
    hidden_ref[...] = hidden
    pre_grad_ref[...] = pre_grad
    to1 = (*grads[:2], 0)
    to2 = (*grads[2:], 0) if split == 2 else (*grads[:2], cols)
    finish = lambda blocks: give_grads(blocks, acc1, acc2, col, gain_ref, shift_ref, w1, to1, to2, norm_ref)
    add_grads(step, pre_grad, unit, hidden, cot, acc1, acc2, col, sum_ref, finish)


def chunk_call(line, kernel, name, pieces, extra_in, extra_specs, sets, vectors, cols, others, split):
    _, part, width = pieces[0].shape
    block, rows = 2 * part, 8 * part
    per_row = lambda n: pl.BlockSpec((block, n), lambda r: (r, 0))
    shapes = [
        shaped((rows, others)), shaped((rows, cols)), shaped((cols, width)), shaped((others, width)),
        shaped((2, width), F32), shaped((1, cols), F32),
    ]
    specs = [per_row(others), per_row(cols)] + [whole(s.shape) for s in shapes[2:]]
    for n in (cols, others) if split == 2 else (cols + others,):
        shapes += [shaped((4, n, LANES)), shaped((12, n, LANES))]
    specs += [whole(s.shape) for s in shapes[6:]]
    weights = [w for s in sets for w in s]
    return run_kernel(
        kernel, shapes,
        [ANYWHERE] * 10 + [whole(w.shape) for w in weights] + [whole(v.shape) for v in vectors] + extra_specs,
        specs, (*pieces, *weights, *vectors, *extra_in), name, grid=(rows // block,),
        scratch=[
            pltpu.VMEM((cols, width), F32), pltpu.VMEM((others, width), F32), pltpu.VMEM((cols, LANES), F32),
            pltpu.VMEM((1, cols), F32),
        ]
        + stream_scratch(block, width),
        line=line,
    )


def attention_kernel(cols, *refs):
    pieces, refs = refs[:10], refs[10:]
    set_one, set_two, refs = refs[:3], refs[3:6], refs[6:]
    gain_ref, shift_ref, ratio_ref, bias_ref, lengths, place, cos_ref, sin_up_ref, sin_down_ref = refs[:9]
    mixed_ref, qkv_grad_ref, w1, w2, norm_ref, sum_ref, own_ref, rest_ref = refs[9:17]
    acc1, acc2, col, row, unit_buf, cot_buf, sems = refs[17:]
    group = pl.program_id(0)
    begin, arrive = stream(group, pieces, unit_buf, cot_buf, sems)

    @pl.when(group == 0)
    def _():
        begin(0)
        take_weights(set_one, gain_ref, ((0, 2 * HD, w1, 0, True),))
        take_weights(set_two, gain_ref, ((0, HD, w1, 2 * HD, True), (HD, 2 * HD, w2, 0, False)))
        row[...] = jnp.sum(dot(ratio_ref[...], w1[...], NT), axis=0, keepdims=True) + bias_ref[...]
        acc1[...] = jnp.zeros_like(acc1)
        acc2[...] = jnp.zeros_like(acc2)
        col[...] = jnp.zeros_like(col)
        sum_ref[...] = jnp.zeros_like(sum_ref)

    arrive()
    slot = lax.rem(group, 2)
    unit = unit_buf[slot]
    cot = cot_buf[slot]
    count = unit.shape[0]
    cosine, sin_up, sin_down = cos_ref[...], sin_up_ref[...], sin_down_ref[...]
    half = ROT // 2

    def turn(u):
        p = u[:, :LANES]
        p = p * cosine + pltpu.roll(p, LANES - half, 1) * sin_up + pltpu.roll(p, half, 1) * sin_down
        return jnp.concatenate([p, u[:, LANES:]], axis=1)

    def unturn(u):
        p = u[:, :LANES]
        p = p * cosine + pltpu.roll(p * sin_up, half, 1) + pltpu.roll(p * sin_down, LANES - half, 1)
        return jnp.concatenate([p, u[:, LANES:]], axis=1)

    qkv = dot(unit, w1[...], NT) + row[...]
    query = turn(qkv[:, :HD]).astype(BF)
    key = turn(qkv[:, HD : 2 * HD]).astype(BF)
    value = qkv[:, 2 * HD :].astype(BF)
    back = dot(cot, w2[...], NT).astype(BF)

    shift = place[SIDE] * (count // 2)
    at = places(0, (count, 1), count, shift)
    to = places(1, (1, count), count, shift)
    end, seg_at, seg_to = 0, jnp.zeros_like(at), jnp.zeros_like(to)
    for k in range(DOCS):
        end = end + lengths[group, k]
        seg_at = seg_at + jnp.where(at >= end, 1, 0)
        seg_to = seg_to + jnp.where(to >= end, 1, 0)
    seg_at = jnp.where(seg_at == DOCS, DOCS + at, seg_at)
    seg_to = jnp.where(seg_to == DOCS, DOCS + to, seg_to)
    visible = (seg_at == seg_to) & (to <= at)

    scale = 1.0 / math.sqrt(HD)
    scores = jnp.where(visible, dot(query, key, NT) * scale, -1e30)
    expo = jnp.exp(scores - jnp.max(scores, axis=1, keepdims=True))
    probs = expo / jnp.sum(expo, axis=1, keepdims=True)
    low = probs.astype(BF)
    mixed = dot(low, value, NN).astype(BF)
    value_grad = dot(low, back, TN)
    probs_grad = dot(back, value, NT)
    inner = jnp.sum(probs * probs_grad, axis=1, keepdims=True)
    score_grad = (probs * (probs_grad - inner)).astype(BF)
    query_grad = unturn(dot(score_grad, key, NN) * scale)
    key_grad = unturn(dot(score_grad, query, TN) * scale)
    qkv_grad = jnp.concatenate([query_grad, key_grad, value_grad], axis=1).astype(BF)
    mixed_ref[...] = mixed
    qkv_grad_ref[...] = qkv_grad
    to1, to2 = (own_ref, rest_ref, 0), (own_ref, rest_ref, cols)
    finish = lambda blocks: give_grads(blocks, acc1, acc2, col, gain_ref, shift_ref, w1, to1, to2, norm_ref)
    add_grads(group, qkv_grad, unit, mixed, cot, acc1, acc2, col, sum_ref, finish)


def join_kernel(n, *refs):
    total = dot(refs[0][...], refs[n][...], NN)
    for j in range(1, n):
        total += dot(refs[j][...], refs[n + j][...], NN)
    refs[2 * n][...] = total.astype(BF)


def join_call(line, acts, weights, sent):
    rows, width = acts[0].shape[0], weights[0].shape[1]
    block = rows // 4
    first = 1 if sent else 0
    return run_kernel(
        functools.partial(join_kernel, len(acts)),
        shaped((rows // 2, width)),
        [pl.BlockSpec((block, a.shape[1]), lambda r: (2 * r + first, 0)) for a in acts]
        + [whole(w.shape) for w in weights],
        pl.BlockSpec((block, width), lambda r: (r, 0)),
        (*acts, *weights),
        "join",
        grid=(2,),
        line=line,
    )


def own_kernel(place, x_ref, cot_ref, out_ref, sum_ref):
    x = x_ref[...].astype(F32)
    centred = x - jnp.mean(x, axis=1, keepdims=True)
    spread = jnp.mean(centred * centred, axis=1, keepdims=True)
    unit = (centred * lax.rsqrt(spread + EPSILON)).astype(BF)
    width = x.shape[1] // 4
    for b in range(4):
        out_ref[0, :, spot(place, b, width)] = unit[:, b * width : (b + 1) * width]
        out_ref[1, :, spot(place, b, width)] = cot_ref[:, b * width : (b + 1) * width]

    @pl.when(pl.program_id(0) == 0)
    def _():
        sum_ref[...] = jnp.zeros_like(sum_ref)

    sum_ref[...] += jnp.sum(cot_ref[...].astype(F32), axis=0, keepdims=True)


def own_call(line, place, x, cot):
    rows, width = x.shape
    spec = pl.BlockSpec((rows // STEPS, width), lambda r: (r, 0))
    return run_kernel(
        own_kernel, [shaped((2, rows, width)), shaped((1, width), F32)], [SCALARS, spec, spec],
        [pl.BlockSpec((2, rows // STEPS, width), lambda r: (0, r, 0)), pl.BlockSpec((1, width), lambda r: (0, 0))],
        (place, x, cot), "own", grid=(STEPS,), line=line,
    )


def part_specs(parts, strip):
    specs = []
    for cross, n, first, every in parts:
        if cross:
            specs.append(pl.BlockSpec((strip, n), functools.partial(lambda f, e, k: (0, k * e + f), first, every)))
        else:
            specs.append(pl.BlockSpec((n, strip), functools.partial(lambda f, e, k: (k * e + f, 0), first, every)))
    return specs


def piece_kernel(parts, *refs):
    out_ref, at = refs[-1], 0
    for (cross, n, *_), ref in zip(parts, refs):
        out_ref[0, at : at + n] = ref[...].astype(F32).T.astype(BF) if cross else ref[...]
        at += n


def piece_call(line, arrays, parts, strip):
    n = sum(p[1] for p in parts)
    return run_kernel(
        functools.partial(piece_kernel, parts), shaped((INNER, n, strip)), part_specs(parts, strip),
        pl.BlockSpec((1, n, strip), lambda k: (k, 0, 0)), arrays, "piece", grid=(INNER,),
        line=line,
    )


def unpiece_kernel(parts, *refs):
    count = len(parts)
    v_ref, refs = refs[0], refs[-2 * count - 3 :]
    outs, helds, buffer, sems, into = refs[:count], refs[count : 2 * count], refs[-3], refs[-2], refs[-1]
    copies = []
    loads = [pltpu.make_async_copy(v_ref.at[k], buffer.at[k], into.at[k]) for k in range(INNER)]
    for load in loads:
        load.start()
    for k in range(INNER):
        at = 0
        loads[k].wait()
        for c, ((cross, n, first, every), out, held) in enumerate(zip(parts, outs, helds)):
            v = buffer[k, at : at + n].astype(F32)
            held[k] = v.T if cross else v
            where = pl.ds((k * every + first) * n, n)
            copies.append(pltpu.make_async_copy(held.at[k], out.at[:, where] if cross else out.at[where], sems.at[c, k]))
            copies[-1].start()
            at += n
    for c in copies:
        c.wait()


def unpiece_call(line, v, shapes, parts, held):
    strip = v.shape[2]
    held = [h for h in held if h is not None]
    return run_kernel(
        functools.partial(unpiece_kernel, parts), [shaped(s, F32) for s in shapes],
        [ANYWHERE] * (1 + len(held)), [ANYWHERE] * len(shapes), (v, *held), "unpiece",
        scratch=[pltpu.VMEM((INNER, strip, n) if cross else (INNER, n, strip), F32) for cross, n, _, _ in parts]
        + [pltpu.VMEM(v.shape, BF), pltpu.SemaphoreType.DMA((len(parts), INNER)), pltpu.SemaphoreType.DMA((INNER,))],
        aliases={1 + k: k for k in range(len(held))}, line=line,
    )


def cat_kernel(a, b, out):
    out[0] = a[...]
    out[1] = b[...]


def cat_call(line, a, b, cols, at):
    n = a.shape[0] // 2
    shape = a.shape[:1] + (cols,) + a.shape[2:]
    spec = pl.BlockSpec((n,) + shape[1:], lambda k: (k, at, 0))
    out = run_kernel(
        cat_kernel, shaped((2,) + shape), [spec, spec],
        pl.BlockSpec((2, n) + shape[1:], lambda k: (0, k, 0, 0)), (a, b), "cat", grid=(2,), line=line,
    )
    return out.reshape((8,) + shape[1:])


def vectors_kernel(piece, nq, nf, share, tensor, place, small, g1, s1, g2, s2, r1, r2, out_bias, bq, bf, lengths):
    total = small.shape[0]
    per = total // 4
    width = per * piece

    def lay(to, b, k, where):
        part = small[b * per : (b + 1) * per, k * piece : (k + 1) * piece]
        to[:, where] = jnp.concatenate([part[r : r + 1] for r in range(per)], axis=1)

    for b in range(4):
        for k, to in enumerate((g1, s1, g2, s2)):
            lay(to, b, k, spot(place, b, width))
        lay(out_bias, b, 4, slice(b * width, (b + 1) * width))
    for gain, shift, ratio in ((g1, s1, r1), (g2, s2, r2)):
        v = shift[...] / gain[...]
        high = v.astype(BF).astype(F32)
        ratio[...] = jnp.concatenate([high, v - high, jnp.zeros((14, v.shape[1]), F32)], axis=0).astype(BF)
    at = 5 * piece
    for k in range(share):
        row = small[pl.ds((place[INSIDE] * share + k) * tensor + place[SIDE], 1), :]
        bq[:, k * nq : (k + 1) * nq] = row[:, at : at + nq]
        bf[:, k * nf : (k + 1) * nf] = row[:, at + nq : at + nq + nf]
    for g in range(INNER):
        row = small[pl.ds(place[DOC_ROW + g], 1), :]
        docs = row[:, at + nq + nf : at + nq + nf + LANES]
        lengths[g : g + 1] = (docs + 0.5).astype(jnp.int32)


def turns_kernel(own_rows, place, lengths, cos_ref, up_ref, down_ref):
    count = cos_ref.shape[0]
    group = pl.program_id(0)
    at = places(0, (count, 1), count, place[SIDE] * own_rows)
    end, begin = 0, jnp.zeros_like(at)
    for k in range(DOCS):
        end = end + lengths[group, k]
        begin = jnp.where(at >= end, end, begin)
    half = ROT // 2
    lane = lax.broadcasted_iota(jnp.int32, (1, LANES), 1)
    step = jnp.where(lane >= half, lane - half, lane).astype(F32)
    freq = jnp.exp(step * (-2.0 * math.log(10000.0) / ROT))
    angle = (at - begin).astype(F32) * freq
    sine = jnp.sin(angle)
    cos_ref[...] = jnp.where(lane < ROT, jnp.cos(angle), 1.0)
    up_ref[...] = jnp.where(lane < half, -sine, 0.0)
    down_ref[...] = jnp.where((lane >= half) & (lane < ROT), sine, 0.0)


def sum_kernel(*refs):
    total = refs[0][...].astype(F32)
    for r in refs[1:-1]:
        total += r[...].astype(F32)
    refs[-1][...] = total.astype(BF)


def sum_call(line, parts, firsts, count):
    n = count // 2
    shape = (n,) + parts[0].shape[1:]
    return run_kernel(
        sum_kernel, shaped((count,) + shape[1:]),
        [pl.BlockSpec(shape, functools.partial(lambda f, k: (k + f, 0, 0), f // n)) for f in firsts],
        pl.BlockSpec(shape, lambda k: (k, 0, 0)), parts, "sum", grid=(2,), line=line,
    )


def core_kernel(kt, kx, kb, ot, ox, ob, x1, t1):
    half = kt.shape[1] // 2
    add = lambda a, b, cut: (a[:, cut].astype(F32) + b[:, cut].astype(F32)).astype(BF)
    left, right = slice(0, half), slice(half, 2 * half)
    x1[:, left] = add(kb, ob, left)
    x1[:, right] = add(kx, ox, left)
    t1[:, left] = add(kb, ob, right)
    t1[:, right] = add(kt, ot, right)


def cross_kernel(kt, kx, ot, ox, x1, t1, t2, x2):
    half = kt.shape[1] // 2
    left, right = slice(0, half), slice(half, 2 * half)
    add = lambda a, b, c: (a.astype(F32) + b.astype(F32) + c.astype(F32)).astype(BF)
    t2[...] = add(kt[:, left], ot[:, left], x1[:, left])
    x2[...] = add(kx[:, right], ox[:, right], t1[:, left])


def face_sum(place, kept, other, x1, t1, t2, x2, natural):
    half = kept.shape[1] // 2
    left, right = slice(0, half), slice(half, 2 * half)
    natural[:, left] = kept[:, left].astype(F32) + other[:, left].astype(F32) + x1[:, right].astype(F32) + t2[...].astype(F32)
    natural[:, right] = (
        kept[:, right].astype(F32) + other[:, right].astype(F32) + t1[:, right].astype(F32) + x2[...].astype(F32)
    )
    return jnp.concatenate([natural[:, spot(place, b, half // 2)] for b in range(4)], axis=1)


def output_kernel(place, x_ref, bias_ref, kept, other, x1, t1, t2, x2, out_ref, natural):
    total = face_sum(place, kept, other, x1, t1, t2, x2, natural) + bias_ref[...] + x_ref[...].astype(F32)
    out_ref[...] = total.astype(BF)


def input_grad_kernel(place, x_ref, cot_ref, kept, other, x1, t1, t2, x2, out_ref, natural):
    pulled = face_sum(place, kept, other, x1, t1, t2, x2, natural)
    x = x_ref[...].astype(F32)
    centred = x - jnp.mean(x, axis=1, keepdims=True)
    rstd = lax.rsqrt(jnp.mean(centred * centred, axis=1, keepdims=True) + EPSILON)
    unit = centred * rstd
    along = jnp.mean(pulled * unit, axis=1, keepdims=True)
    level = jnp.mean(pulled, axis=1, keepdims=True)
    out_ref[...] = (cot_ref[...].astype(F32) + rstd * (pulled - level - unit * along)).astype(BF)


def own_rows_call(line, kernel, place, rows_in, row_in, sums, name):
    rows, width = rows_in[0].shape
    block = rows // STEPS
    spec = pl.BlockSpec((block, width), lambda r: (r, 0))
    half = pl.BlockSpec((block, width // 2), lambda r: (r, 0))
    vector = pl.BlockSpec((1, width), lambda r: (0, 0))
    return run_kernel(
        kernel, shaped((rows, width)),
        [SCALARS] + [spec] * len(rows_in) + [vector] * len(row_in) + [spec] * 4 + [half] * 2,
        spec, (place, *rows_in, *row_in, *sums), name, grid=(STEPS,), scratch=[pltpu.VMEM((block, width), F32)],
        line=line,
    )


def tail_kernel(piece, nq, nf, share, tensor, place, n_attn, n0, n1, n2, sum_q, f0, f1, f2, cot_sum, tail):
    total = tail.shape[0]
    per = total // 4
    width = per * piece
    tail[...] = jnp.zeros_like(tail)

    def lay(k, b, row):
        rows = jnp.concatenate([row[:, r * piece : (r + 1) * piece] for r in range(per)], axis=0)
        tail[b * per : (b + 1) * per, k * piece : (k + 1) * piece] = rows

    for b in range(4):
        at = spot(place, b, width)
        attn = n_attn[:, at]
        feeds = n0[:, at] + n1[:, at] + n2[:, at]
        for k, row in enumerate((attn[0:1], attn[1:2], feeds[0:1], feeds[1:2])):
            lay(k, b, row)
        lay(4, b, cot_sum[:, b * width : (b + 1) * width])
    hidden = jnp.concatenate([f0[...], f1[...], f2[...]], axis=1)
    query = sum_q[...]
    at = full_lanes(5 * piece)
    rest = jnp.zeros((1, full_lanes(nq + nf) - nq - nf), F32)
    line = lax.broadcasted_iota(jnp.int32, (total, 1), 0)
    below = jnp.zeros((total, full_lanes(nq + nf)), F32)
    for k in range(share):
        row = (place[INSIDE] * share + k) * tensor + place[SIDE]
        both = [query[:, k * nq : (k + 1) * nq], hidden[:, k * nf : (k + 1) * nf]]
        both = jnp.concatenate(both + [rest] if rest.shape[1] else both, axis=1)
        below = jnp.where(line == row, both, below)
    tail[:, at:] = below


def make(dp, tensor):
    outer = dp // INNER
    face = INNER * tensor
    total = dp * tensor
    short = outer == 4

    def permute(v, pairs):
        return lax.ppermute(v.reshape(-1, v.shape[-1]), AXES, pairs).reshape(v.shape)

    def flip(v, k):
        return permute(v, [(l, l ^ k) for l in range(total)])

    def hop(v, moves):
        return permute(v, [(a * face + f, b * face + f) for a, b in moves for f in range(face)])

    column_groups = [[o * face + f for o in range(outer)] for f in range(face)]
    ring_groups = [[o * face + i * tensor + t for i in range(INNER)] for o in range(outer) for t in range(tensor)]
    towards_middle = [(0, 1), (3, 2)]
    across_middle = [(1, 2), (2, 1)]
    towards_ends = [(1, 0), (2, 3)]

    back_table = [[0, 1, 2, 3], [1, 0, 2, 3], [3, 2, 0, 1], [3, 2, 1, 0]]

    def swap_ring(v):
        return lax.all_to_all(v, AXES, split_axis=0, concat_axis=0, tiled=True, axis_index_groups=ring_groups)

    def swap_all(v):
        return lax.all_to_all(v, AXES, split_axis=0, concat_axis=0, tiled=True)

    class Near:
        def __init__(self, v):
            self.own = v
            self.near = flip(v, face) if short else None

    class Gather:
        def __init__(self, line, v, cols, at):
            if not short:
                own = v.own[:, at * cols : (at + 1) * cols]
                every = lax.all_gather(own, AXES, axis=0, tiled=True, axis_index_groups=column_groups)
                every = every.transpose(1, 0, 2).reshape(cols, 16, LANES).transpose(1, 0, 2)
                self.parts = [every[:8], every[8:], jnp.zeros_like(every[8:])]
                return
            self.both = cat_call(line, v.own, v.near, cols, at)
            self.far = hop(self.both, across_middle)

        def far_came(self, line):
            if short:
                self.far = line(self.far)
                self.passed = hop(self.far, towards_ends)

        def passed_came(self, line):
            if short:
                self.passed = line(self.passed)
                self.parts = [self.both, self.far, self.passed]

    class Reduce:
        def __init__(self, line, own, rest):
            if not short:
                v = jnp.concatenate([own, rest], axis=0)
                v = v.transpose(1, 0, 2).reshape(v.shape[1], dp, -1).transpose(1, 0, 2)
                self.total = lax.psum_scatter(
                    v, AXES, scatter_dimension=0, tiled=True, axis_index_groups=column_groups
                )
                return
            self.own, self.rest = own, line(rest)
            self.first = hop(self.rest, towards_middle)

        def first_came(self, line):
            if short:
                far = sum_call(line, (self.rest, self.first), (4, 4), 8)
                self.second = hop(far, across_middle)

        def second_came(self, line):
            if short:
                near = sum_call(line, (self.rest, self.second), (0, 4), 4)
                self.third = hop(near, towards_ends)

        def third_came(self, line):
            if short:
                self.total = sum_call(line, (self.own, self.first, self.second, self.third), (0, 0, 0, 0), 4)
            self.final = swap_ring(self.total)

    class FaceReduce:
        def __init__(self, sent):
            self.other = flip(sent, 2)

        def core_came(self, line):
            self.rows, self.width = self.kept.shape[0] // 4, self.kept.shape[1]
            spec = pl.BlockSpec((self.rows // STEPS, self.width), lambda r: (r, 0))
            x1, t1 = run_kernel(
                core_kernel, [shaped((self.rows, self.width))] * 2, self.block_specs(1, 2, 3) * 2, [spec] * 2,
                (self.kept,) * 3 + (self.other,) * 3, "core", grid=(STEPS,), line=line,
            )
            self.x1, self.t1 = flip(x1, 4), flip(t1, 1)

        def block_specs(self, *blocks):
            block = self.rows // STEPS
            return [
                pl.BlockSpec((block, self.width), functools.partial(lambda k, r: (k * STEPS + r, 0), k)) for k in blocks
            ]

        def first_came(self, line):
            rows, width = self.rows, self.width
            spec = pl.BlockSpec((rows // STEPS, width), lambda r: (r, 0))
            half = pl.BlockSpec((rows // STEPS, width // 2), lambda r: (r, 0))
            t2, x2 = run_kernel(
                cross_kernel, [shaped((rows, width // 2))] * 2, self.block_specs(1, 2) * 2 + [spec] * 2, [half] * 2,
                (self.kept, self.kept, self.other, self.other, self.x1, self.t1), "cross", grid=(STEPS,), line=line,
            )
            self.t2, self.x2 = flip(t2, 1), flip(x2, 4)

        def second_came(self):
            return self.kept, self.other, self.x1, self.t1, self.t2, self.x2

    def per_device(
        layer_input, doc_lengths, ln1_gain, ln1_bias, ln2_gain, ln2_bias, w_qkv, b_qkv, w_dense, b_dense,
        w_fc1, b_fc1, w_fc2, b_fc2, cotangent,
    ):
        d, t = lax.axis_index("dp"), lax.axis_index("tensor")
        o, i = d // INNER, d % INNER
        own_rows, width = layer_input.shape
        rows, group_rows = own_rows * face, own_rows * tensor
        strip = width // dp
        hidden_own = w_fc1.shape[1] // INNER
        qkv_own = w_qkv.shape[1] // INNER
        quarter = hidden_own // 4
        piece, nq, nf = width // total, b_qkv.shape[0], b_fc1.shape[0]
        share = dp // INNER
        line = Line()
        if short:
            spots = jnp.array(back_table, jnp.int32)[o]
        else:
            spots = jnp.arange(4, dtype=jnp.int32)
        doc_rows = (o * INNER + (i ^ jnp.arange(INNER, dtype=jnp.int32))) * tensor
        place = jnp.concatenate([jnp.stack([o, i, t]).astype(jnp.int32), spots, doc_rows.astype(jnp.int32)])

        forms = {
            0: ((w_fc1, w_fc2) * 2, tuple((cross, quarter, k, 4) for k in (0, 1) for cross in (True, False))),
            2: ((w_qkv,) * 3 + (w_dense,), tuple((True, HD, k, 3) for k in (0, 1, 2)) + ((False, HD, 0, 1),)),
            4: ((w_fc1, w_fc2), ((True, 2 * quarter, 1, 2), (False, 2 * quarter, 1, 2))),
        }
        cuts_of = {0: (0, 2 * quarter, 0), 1: (0, 2 * quarter, 1), 2: (2, 2 * HD, 0), 3: (2, 2 * HD, 1), 4: (4, 4 * quarter, 0)}
        s = {}
        steps = {}

        def own():
            s["own"], s["cot_sum"] = own_call(line, place, layer_input, cotangent)
            s["t"], s["x"], s["c"] = flip(s["own"], 1), flip(s["own"], 4), flip(s["own"], 2)

        def own_c():
            s["c"] = line(s["c"])

        def own_xt():
            s["x"], s["t"] = line(s["x"], s["t"])
            s["bu"], s["bv"] = flip(s["x"][0], 1), flip(s["t"][1], 4)
            s["tc"], s["xc"] = flip(s["t"], 2), flip(s["x"], 2)

        def own_tc():
            s["tc"], s["xc"] = line(s["tc"], s["xc"])

        def own_b():
            s["bu"], s["bv"] = line(s["bu"], s["bv"])
            s["buc"], s["bvc"] = flip(s["bu"], 2), flip(s["bv"], 2)

        def own_bc():
            s["buc"], s["bvc"] = line(s["buc"], s["bvc"])

        steps.update({"own": own, "c": own_c, "xt": own_xt, "tc": own_tc, "b": own_b, "bc": own_bc})

        def small():
            v = jnp.concatenate(
                [ln1_gain, ln1_bias, ln2_gain, ln2_bias, b_dense + b_fc2, b_qkv.astype(F32), b_fc1.astype(F32),
                 doc_lengths[0].astype(F32), jnp.zeros((LANES - DOCS,), F32)]
            )
            s["small"] = swap_all(line(jnp.broadcast_to(v[None], (total, v.shape[0]))))

        def small_came():
            s["small"] = line(s["small"])

        def vectors():
            v = s["small"].reshape(total, -1)
            row, fine = shaped((1, width), F32), shaped((16, width))
            *s["vec"], s["bias_q"], s["bias_f"], s["lengths"] = run_kernel(
                functools.partial(vectors_kernel, piece, nq, nf, share, tensor),
                [row] * 4 + [fine] * 2 + [row, shaped((1, qkv_own), F32), shaped((1, hidden_own), F32),
                                          shaped((INNER, LANES), jnp.int32)],
                [SCALARS, VECTORS], [VECTORS] * 10, (place, v), "vectors", line=line,
            )
            turn_spec = pl.BlockSpec((group_rows, LANES), lambda g: (g, 0))
            s["turns"] = run_kernel(
                functools.partial(turns_kernel, own_rows), [shaped((rows, LANES), F32)] * 3, [SCALARS] * 2,
                [turn_spec] * 3, (place, s["lengths"]), "turns", grid=(INNER,), line=line,
            )

        steps.update({"sm": small, "sw": small_came, "vec": vectors})
        nears, gathers, done, sums = {}, {}, {}, {}

        def near_steps(k):
            def p():
                arrays, parts = forms[k]
                s[f"ring{k}"] = swap_ring(piece_call(line, arrays, parts, strip))

            def g():
                nears[k] = Near(line(s[f"ring{k}"]))

            steps.update({f"p{k}": p, f"g{k}": g})

        def gather_steps(k):
            def h():
                of, cols, at = cuts_of[k]
                gathers[k] = Gather(line, nears[of], cols, at)

            steps.update({
                f"h{k}": h, f"i{k}": lambda: gathers[k].far_came(line), f"j{k}": lambda: gathers[k].passed_came(line),
            })

        for k in forms:
            near_steps(k)
        for k in cuts_of:
            gather_steps(k)

        def pieces():
            return [s[n] for n in ("own", "t", "c", "tc", "x", "xc", "bu", "bv", "buc", "bvc")]

        def feed(k, first, split, sets):
            def run():
                gain, shift, ratio = s["vec"][2], s["vec"][3], s["vec"][5]
                cols = split * quarter
                bias = s["bias_f"][:, first * quarter : first * quarter + cols]
                done[k] = chunk_call(
                    line, functools.partial(feed_kernel, cols, split, len(sets)), "feed", pieces(), (), [],
                    [gathers[j].parts for j in sets], (gain, shift, ratio, bias), cols, cols, split,
                )

            return run

        def attention():
            gain, shift, ratio = s["vec"][0], s["vec"][1], s["vec"][4]
            one, two = gathers[2].parts, gathers[3].parts
            turn_spec = pl.BlockSpec((group_rows, LANES), lambda r: (r, 0))
            done[2] = chunk_call(
                line, functools.partial(attention_kernel, qkv_own), "attention", pieces(),
                (s["lengths"], place, *s["turns"]), [SCALARS, SCALARS] + [turn_spec] * 3, [one, two],
                (gain, shift, ratio, s["bias_q"]), qkv_own, HD, 1,
            )

        steps.update({"K0": feed(0, 0, 1, (0,)), "K1": feed(1, 1, 1, (1,)), "KA": attention, "K4": feed(4, 2, 2, (4,))})

        def reduce_steps(k, chunk, at):
            def r():
                sums[k] = Reduce(line, *done[chunk][at : at + 2])

            def z():
                final = sums[k].final
                if k == 2:
                    s["qkv"], s["dense"] = unpiece_call(
                        line, final, (w_qkv.shape, w_dense.shape), ((True, qkv_own, 0, 1), (False, HD, 0, 1)), ()
                    )
                elif k < 2:
                    s["fc1"], s["fc2"] = unpiece_call(
                        line, final, (w_fc1.shape, w_fc2.shape), forms[0][1][2 * k : 2 * k + 2], (s.get("fc1"), s.get("fc2"))
                    )
                else:
                    name, w, form = (("fc1", w_fc1, 0), ("fc2", w_fc2, 1))[k - 3]
                    s[name], = unpiece_call(line, final, (w.shape,), forms[4][1][form : form + 1], (s[name],))

            steps.update({
                f"r{k}": r, f"u{k}": lambda: sums[k].first_came(line), f"v{k}": lambda: sums[k].second_came(line),
                f"w{k}": lambda: sums[k].third_came(line), f"z{k}": z,
            })

        for k, chunk, at in ((0, 0, 6), (1, 1, 6), (2, 2, 6), (3, 4, 6), (4, 4, 8)):
            reduce_steps(k, chunk, at)

        def face_steps(name, act, weight, finish):
            def parts():
                chunks = [done[k] for k in (0, 1, 2, 4)]
                return [c[act] for c in chunks], [c[weight] for c in chunks]

            def sent():
                s["face" + name] = FaceReduce(join_call(line, *parts(), True))

            def kept():
                s["face" + name].kept = join_call(line, *parts(), False)

            steps.update({
                "J" + name: sent, "k" + name: kept, "C" + name: lambda: s["face" + name].core_came(line),
                "D" + name: lambda: s["face" + name].first_came(line),
                "E" + name: lambda: finish(s["face" + name].second_came()),
            })

        def finish_back(sums_in):
            s["input_grad"] = own_rows_call(
                line, input_grad_kernel, place, (layer_input, cotangent), (), sums_in, "input_grad"
            )

        def finish_out(sums_in):
            s["output"] = own_rows_call(line, output_kernel, place, (layer_input,), (s["vec"][6],), sums_in, "output")

        face_steps("B", 1, 2, finish_back)
        face_steps("O", 0, 3, finish_out)

        def tail():
            feeds = [done[k] for k in (0, 1, 4)]
            v = run_kernel(
                functools.partial(tail_kernel, piece, nq, nf, share, tensor),
                shaped((total, full_lanes(5 * piece) + full_lanes(nq + nf)), F32), [SCALARS] + [VECTORS] * 9, VECTORS,
                (place, done[2][4], *[p[4] for p in feeds], done[2][5], *[p[5] for p in feeds], s["cot_sum"]), "tail", line=line,
            )
            s["tail"] = swap_all(v)

        def tail_came():
            s["tail"] = jnp.sum(line(s["tail"]), axis=0)

        steps.update({"tail": tail, "tz": tail_came})
        for name in ORDER:
            steps[name]()

        tail_row = s["tail"]
        cuts = [tail_row[j * piece : (j + 1) * piece] for j in range(5)]
        at = full_lanes(5 * piece)
        return (
            s["output"], s["input_grad"], cuts[0], cuts[1], cuts[2], cuts[3], s["qkv"], tail_row[at : at + nq],
            s["dense"], cuts[4], s["fc1"], tail_row[at + nq : at + nq + nf], s["fc2"], cuts[4],
        )

    return per_device


def solution(mesh):
    rows = P(("dp", "tensor"), None)
    vector = P(("dp", "tensor"))
    crossed = P(("tensor", "dp"))
    wide = P("dp", "tensor")
    tall = P("tensor", "dp")
    return jax.shard_map(
        make(mesh.shape["dp"], mesh.shape["tensor"]),
        mesh=mesh,
        in_specs=(rows, P("dp", None), vector, vector, vector, vector, wide, crossed, tall, vector, wide, crossed,
                  tall, vector, rows),
        out_specs=(rows, rows, vector, vector, vector, vector, wide, crossed, tall, vector, wide, crossed, tall,
                   vector),
        check_vma=False,
    )
```

```python
import functools
import math

import jax
import jax.numpy as jnp
from jax import lax
from jax.experimental import pallas as pl
from jax.experimental.pallas import tpu as pltpu
from jax.sharding import PartitionSpec as P

HD = 256
ROT = 64
DOCS = 3
EPSILON = 1e-05
INNER = 4
LANES = 128
AXES = ("dp", "tensor")
BF = jnp.bfloat16
F32 = jnp.float32
NT = ((1,), (1,))
NN = ((1,), (0,))
TN = ((0,), (0,))
VMEM = 63 * 2**20
STEPS = 4


ORDER = (
    "p0", "p2", "g0", "g2", "own", "h0", "h1", "sm", "i0", "c", "h2", "h3", "sw", "xt", "i1", "vec", "j0", "p4",
    "b", "j1", "i2", "g4", "bc", "tc", "K0", "r0", "i3", "h4", "K1", "i4", "j2", "j3", "r1", "KA", "r2", "u0", "j4",
    "u1", "K4", "r3", "r4", "v0", "JB", "v1", "JO", "u2", "kB", "w0", "CB", "kO", "u3", "z0", "v2", "CO", "DB",
    "tail", "v3", "u4", "w2", "tz", "w1", "DO", "z2", "EO", "v4", "w3", "EB", "z1", "w4", "z3", "z4",
)

NOTHING = pl.CostEstimate(flops=0, bytes_accessed=0, transcendentals=0)
SCALARS = pl.BlockSpec(memory_space=pltpu.SMEM)
ANYWHERE = pl.BlockSpec(memory_space=pl.ANY)
VECTORS = pl.BlockSpec(memory_space=pltpu.VMEM)

OUTER, INSIDE, SIDE, SPOT, DOC_ROW = 0, 1, 2, 3, 7


def dot(a, b, dims):
    return lax.dot_general(a, b, (dims, ((), ())), preferred_element_type=F32)


def shaped(shape, dtype=BF):
    return jax.ShapeDtypeStruct(shape, dtype)


def whole(shape):
    return pl.BlockSpec(shape, lambda *_: (0,) * len(shape), pipeline_mode=pl.Buffered(1))


def run_kernel(
    kernel, outs, in_specs, out_specs, args, name, grid=(), scratch=(), aliases=None, line=None
):
    one = not isinstance(outs, (list, tuple))
    outs, out_specs = ([outs], [out_specs]) if one else (list(outs), list(out_specs))
    in_specs, args, aliases, inner = list(in_specs), list(args), dict(aliases or {}), kernel
    if line is not None:
        n, m = len(args), len(outs)
        aliases[n] = m
        in_specs.append(ANYWHERE)
        out_specs.append(ANYWHERE)
        args.append(line.mark)
        outs.append(shaped(line.mark.shape, line.mark.dtype))

        def inner(*refs):
            kernel(*refs[:n], *refs[n + 1 : n + 1 + m], *refs[n + 2 + m :])

    got = pl.pallas_call(
        inner,
        grid=grid,
        out_shape=outs,
        in_specs=in_specs,
        out_specs=out_specs,
        scratch_shapes=scratch,
        input_output_aliases=aliases,
        compiler_params=pltpu.CompilerParams(vmem_limit_bytes=VMEM),
        cost_estimate=NOTHING,
        name=name,
    )(*args)
    if line is not None:
        *got, line.mark = got
    return got[0] if one else got


def gate_kernel(*refs):
    pass


class Line:
    def __init__(self):
        self.mark = jnp.zeros((8, LANES), F32)

    def __call__(self, *arrays):
        held = (*arrays, self.mark)
        *held, self.mark = run_kernel(
            gate_kernel, [shaped(v.shape, v.dtype) for v in held], [ANYWHERE] * len(held), [ANYWHERE] * len(held),
            held, "gate", aliases={n: n for n in range(len(held))},
        )
        return held[0] if len(held) == 1 else held


def spot(place, b, width):
    return pl.ds(pl.multiple_of(place[SPOT + b] * width, width), width)


def places(axis, shape, count, shift):
    at = lax.broadcasted_iota(jnp.int32, shape, axis) + shift
    return jnp.where(at >= count, at - count, at)


def full_lanes(n):
    return n + -n % LANES


def take_weights(parts, gain_ref, dests):
    both, far, passed = parts
    for b in range(16):
        lanes = slice(b * LANES, (b + 1) * LANES)
        block = both[b].astype(F32) if b < 8 else far[b - 8].astype(F32) + passed[b - 8].astype(F32)
        for lo, hi, to, at, gained in dests:
            rows = block[lo:hi]
            to[at : at + hi - lo, lanes] = (rows * gain_ref[:, lanes] if gained else rows).astype(BF)


def give_grads(blocks, acc1, acc2, col, gain_ref, shift_ref, w1, to1, to2, norm_ref):
    for b in blocks:
        lanes = slice(b * LANES, (b + 1) * LANES)
        gain = gain_ref[:, lanes]
        m = acc1[:, lanes]
        w = w1[:, lanes].astype(F32)
        for (own, rest, at), v in ((to1, m * gain + col[...] * shift_ref[:, lanes]), (to2, acc2[:, lanes])):
            to, k = (own, b) if b < 4 else (rest, b - 4)
            to[k, at : at + v.shape[0]] = v.astype(BF)
        norm_ref[0:1, lanes] = jnp.sum(w * m, axis=0, keepdims=True) / gain
        norm_ref[1:2, lanes] = jnp.sum(w * col[...], axis=0, keepdims=True) / gain


def add_grads(step, grad, unit, act, cot, acc1, acc2, col, sum_ref, finish):
    col[...] += dot(grad, jnp.ones((grad.shape[0], LANES), BF), TN)
    sum_ref[...] += jnp.sum(grad.astype(F32), axis=0, keepdims=True)
    last = pl.num_programs(0) - 1

    @pl.when(step < last)
    def _():
        acc1[...] += dot(grad, unit, TN)
        acc2[...] += dot(act, cot, TN)

    @pl.when(step == last)
    def _():
        width = unit.shape[1] // 4
        for part in range(4):
            lanes = slice(part * width, (part + 1) * width)
            acc1[:, lanes] += dot(grad, unit[:, lanes], TN)
            acc2[:, lanes] += dot(act, cot[:, lanes], TN)
            finish(range(4 * part, 4 * part + 4))


def stream(step, pieces, unit_buf, cot_buf, sems):
    blocks = [(p.at[0], p.at[1]) for p in pieces[:6]] + [(pieces[6], pieces[7]), (pieces[8], pieces[9])]
    blocks = [blocks[k] for k in (0, 1, 2, 3, 4, 6, 5, 7)]
    rows = pieces[0].shape[1]
    steps = len(blocks) // 2

    def copies(s):
        made = []
        for k in (2 * s, 2 * s + 1):
            for n, buffer in enumerate((unit_buf, cot_buf)):
                to = buffer.at[s % 2, pl.ds((k % 2) * rows, rows)]
                made.append(pltpu.make_async_copy(blocks[k][n], to, sems.at[s % 2, len(made)]))
        return made

    def begin(s):
        for c in copies(s):
            c.start()

    def arrive():
        for s in range(steps):
            @pl.when(step == s)
            def _(s=s):
                if s + 1 < steps:
                    begin(s + 1)
                for c in copies(s):
                    c.wait()

    return begin, arrive


def stream_scratch(rows, width):
    return [pltpu.VMEM((2, rows, width), BF), pltpu.VMEM((2, rows, width), BF), pltpu.SemaphoreType.DMA((2, 4))]


def feed_kernel(cols, split, sets, *refs):
    pieces, parts, refs = refs[:10], refs[10 : 10 + 3 * sets], refs[10 + 3 * sets :]
    gain_ref, shift_ref, ratio_ref, bias_ref = refs[:4]
    hidden_ref, pre_grad_ref, w1, w2, norm_ref, sum_ref = refs[4:10]
    grads, refs = refs[10 : 10 + 2 * split], refs[10 + 2 * split :]
    acc1, acc2, col, row, unit_buf, cot_buf, sems = refs
    step = pl.program_id(0)
    begin, arrive = stream(step, pieces, unit_buf, cot_buf, sems)

    @pl.when(step == 0)
    def _():
        begin(0)
        n = cols // sets
        for k in range(sets):
            take_weights(parts[3 * k : 3 * k + 3], gain_ref, ((0, n, w1, k * n, True), (n, 2 * n, w2, k * n, False)))
        row[...] = jnp.sum(dot(ratio_ref[...], w1[...], NT), axis=0, keepdims=True) + bias_ref[...]
        acc1[...] = jnp.zeros_like(acc1)
        acc2[...] = jnp.zeros_like(acc2)
        col[...] = jnp.zeros_like(col)
        sum_ref[...] = jnp.zeros_like(sum_ref)

    arrive()
    slot = lax.rem(step, 2)
    unit = unit_buf[slot]
    cot = cot_buf[slot]
    pre = dot(unit, w1[...], NT) + row[...]
    back = dot(cot, w2[...], NT)
    phi = 0.5 * (1.0 + lax.erf(pre * (1.0 / math.sqrt(2.0))))
    slope = phi + pre * (jnp.exp(-0.5 * pre * pre) * (1.0 / math.sqrt(2.0 * math.pi)))
    hidden = (pre * phi).astype(BF)
    pre_grad = (back * slope).astype(BF)
    hidden_ref[...] = hidden
    pre_grad_ref[...] = pre_grad
    to1 = (*grads[:2], 0)
    to2 = (*grads[2:], 0) if split == 2 else (*grads[:2], cols)
    finish = lambda blocks: give_grads(blocks, acc1, acc2, col, gain_ref, shift_ref, w1, to1, to2, norm_ref)
    add_grads(step, pre_grad, unit, hidden, cot, acc1, acc2, col, sum_ref, finish)


def chunk_call(line, kernel, name, pieces, extra_in, extra_specs, sets, vectors, cols, others, split):
    _, part, width = pieces[0].shape
    block, rows = 2 * part, 8 * part
    per_row = lambda n: pl.BlockSpec((block, n), lambda r: (r, 0))
    shapes = [
        shaped((rows, others)), shaped((rows, cols)), shaped((cols, width)), shaped((others, width)),
        shaped((2, width), F32), shaped((1, cols), F32),
    ]
    specs = [per_row(others), per_row(cols)] + [whole(s.shape) for s in shapes[2:]]
    for n in (cols, others) if split == 2 else (cols + others,):
        shapes += [shaped((4, n, LANES)), shaped((12, n, LANES))]
    specs += [whole(s.shape) for s in shapes[6:]]
    weights = [w for s in sets for w in s]
    return run_kernel(
        kernel, shapes,
        [ANYWHERE] * 10 + [whole(w.shape) for w in weights] + [whole(v.shape) for v in vectors] + extra_specs,
        specs, (*pieces, *weights, *vectors, *extra_in), name, grid=(rows // block,),
        scratch=[
            pltpu.VMEM((cols, width), F32), pltpu.VMEM((others, width), F32), pltpu.VMEM((cols, LANES), F32),
            pltpu.VMEM((1, cols), F32),
        ]
        + stream_scratch(block, width),
        line=line,
    )


def attention_kernel(cols, *refs):
    pieces, refs = refs[:10], refs[10:]
    set_one, set_two, refs = refs[:3], refs[3:6], refs[6:]
    gain_ref, shift_ref, ratio_ref, bias_ref, lengths, place, cos_ref, sin_up_ref, sin_down_ref = refs[:9]
    mixed_ref, qkv_grad_ref, w1, w2, norm_ref, sum_ref, own_ref, rest_ref = refs[9:17]
    acc1, acc2, col, row, unit_buf, cot_buf, sems = refs[17:]
    group = pl.program_id(0)
    begin, arrive = stream(group, pieces, unit_buf, cot_buf, sems)

    @pl.when(group == 0)
    def _():
        begin(0)
        take_weights(set_one, gain_ref, ((0, 2 * HD, w1, 0, True),))
        take_weights(set_two, gain_ref, ((0, HD, w1, 2 * HD, True), (HD, 2 * HD, w2, 0, False)))
        row[...] = jnp.sum(dot(ratio_ref[...], w1[...], NT), axis=0, keepdims=True) + bias_ref[...]
        acc1[...] = jnp.zeros_like(acc1)
        acc2[...] = jnp.zeros_like(acc2)
        col[...] = jnp.zeros_like(col)
        sum_ref[...] = jnp.zeros_like(sum_ref)

    arrive()
    slot = lax.rem(group, 2)
    unit = unit_buf[slot]
    cot = cot_buf[slot]
    count = unit.shape[0]
    cosine, sin_up, sin_down = cos_ref[...], sin_up_ref[...], sin_down_ref[...]
    half = ROT // 2

    def turn(u):
        p = u[:, :LANES]
        p = p * cosine + pltpu.roll(p, LANES - half, 1) * sin_up + pltpu.roll(p, half, 1) * sin_down
        return jnp.concatenate([p, u[:, LANES:]], axis=1)

    def unturn(u):
        p = u[:, :LANES]
        p = p * cosine + pltpu.roll(p * sin_up, half, 1) + pltpu.roll(p * sin_down, LANES - half, 1)
        return jnp.concatenate([p, u[:, LANES:]], axis=1)

    qkv = dot(unit, w1[...], NT) + row[...]
    query = turn(qkv[:, :HD]).astype(BF)
    key = turn(qkv[:, HD : 2 * HD]).astype(BF)
    value = qkv[:, 2 * HD :].astype(BF)
    back = dot(cot, w2[...], NT).astype(BF)

    shift = place[SIDE] * (count // 2)
    at = places(0, (count, 1), count, shift)
    to = places(1, (1, count), count, shift)
    end, seg_at, seg_to = 0, jnp.zeros_like(at), jnp.zeros_like(to)
    for k in range(DOCS):
        end = end + lengths[group, k]
        seg_at = seg_at + jnp.where(at >= end, 1, 0)
        seg_to = seg_to + jnp.where(to >= end, 1, 0)
    seg_at = jnp.where(seg_at == DOCS, DOCS + at, seg_at)
    seg_to = jnp.where(seg_to == DOCS, DOCS + to, seg_to)
    visible = (seg_at == seg_to) & (to <= at)

    scale = 1.0 / math.sqrt(HD)
    scores = jnp.where(visible, dot(query, key, NT) * scale, -1e30)
    expo = jnp.exp(scores - jnp.max(scores, axis=1, keepdims=True))
    probs = expo / jnp.sum(expo, axis=1, keepdims=True)
    low = probs.astype(BF)
    mixed = dot(low, value, NN).astype(BF)
    value_grad = dot(low, back, TN)
    probs_grad = dot(back, value, NT)
    inner = jnp.sum(probs * probs_grad, axis=1, keepdims=True)
    score_grad = (probs * (probs_grad - inner)).astype(BF)
    query_grad = unturn(dot(score_grad, key, NN) * scale)
    key_grad = unturn(dot(score_grad, query, TN) * scale)
    qkv_grad = jnp.concatenate([query_grad, key_grad, value_grad], axis=1).astype(BF)
    mixed_ref[...] = mixed
    qkv_grad_ref[...] = qkv_grad
    to1, to2 = (own_ref, rest_ref, 0), (own_ref, rest_ref, cols)
    finish = lambda blocks: give_grads(blocks, acc1, acc2, col, gain_ref, shift_ref, w1, to1, to2, norm_ref)
    add_grads(group, qkv_grad, unit, mixed, cot, acc1, acc2, col, sum_ref, finish)


def join_kernel(n, *refs):
    acts = [r[...].reshape(-1, r.shape[-1]) for r in refs[:n]]
    total = dot(acts[0], refs[n][...], NN)
    for j in range(1, n):
        total += dot(acts[j], refs[n + j][...], NN)
    refs[2 * n][...] = total.astype(BF)


def join_call(line, acts, weights, sent):
    rows, width = acts[0].shape[0], weights[0].shape[1]
    block, part = rows // 4, width // 4
    first = 1 if sent else 0
    acts = [a.reshape(2, 2, block, a.shape[1]) for a in acts]
    return run_kernel(
        functools.partial(join_kernel, len(acts)),
        shaped((rows // 2, width)),
        [pl.BlockSpec((2, None) + a.shape[2:], lambda c: (0, first, 0, 0), pipeline_mode=pl.Buffered(1)) for a in acts]
        + [pl.BlockSpec((w.shape[0], part), lambda c: (0, c)) for w in weights],
        pl.BlockSpec((rows // 2, part), lambda c: (0, c)),
        (*acts, *weights),
        "join",
        grid=(4,),
        line=line,
    )


def own_kernel(place, x_ref, cot_ref, out_ref, sum_ref):
    x = x_ref[...].astype(F32)
    centred = x - jnp.mean(x, axis=1, keepdims=True)
    spread = jnp.mean(centred * centred, axis=1, keepdims=True)
    unit = (centred * lax.rsqrt(spread + EPSILON)).astype(BF)
    width = x.shape[1] // 4
    for b in range(4):
        out_ref[0, :, spot(place, b, width)] = unit[:, b * width : (b + 1) * width]
        out_ref[1, :, spot(place, b, width)] = cot_ref[:, b * width : (b + 1) * width]

    @pl.when(pl.program_id(0) == 0)
    def _():
        sum_ref[...] = jnp.zeros_like(sum_ref)

    sum_ref[...] += jnp.sum(cot_ref[...].astype(F32), axis=0, keepdims=True)


def own_call(line, place, x, cot):
    rows, width = x.shape
    spec = pl.BlockSpec((rows // STEPS, width), lambda r: (r, 0))
    return run_kernel(
        own_kernel, [shaped((2, rows, width)), shaped((1, width), F32)], [SCALARS, spec, spec],
        [pl.BlockSpec((2, rows // STEPS, width), lambda r: (0, r, 0)), pl.BlockSpec((1, width), lambda r: (0, 0))],
        (place, x, cot), "own", grid=(STEPS,), line=line,
    )


def part_specs(parts, strip):
    specs = []
    for cross, n, first, every in parts:
        if cross:
            specs.append(pl.BlockSpec((strip, n), functools.partial(lambda f, e, k: (0, k * e + f), first, every)))
        else:
            specs.append(pl.BlockSpec((n, strip), functools.partial(lambda f, e, k: (k * e + f, 0), first, every)))
    return specs


def piece_kernel(parts, *refs):
    out_ref, at = refs[-1], 0
    for (cross, n, *_), ref in zip(parts, refs):
        out_ref[0, at : at + n] = ref[...].astype(F32).T.astype(BF) if cross else ref[...]
        at += n


def piece_call(line, arrays, parts, strip):
    n = sum(p[1] for p in parts)
    return run_kernel(
        functools.partial(piece_kernel, parts), shaped((INNER, n, strip)), part_specs(parts, strip),
        pl.BlockSpec((1, n, strip), lambda k: (k, 0, 0)), arrays, "piece", grid=(INNER,),
        line=line,
    )


def unpiece_kernel(parts, *refs):
    count = len(parts)
    v_ref, refs = refs[0], refs[-2 * count - 3 :]
    outs, helds, buffer, sems, into = refs[:count], refs[count : 2 * count], refs[-3], refs[-2], refs[-1]
    copies = []
    loads = [pltpu.make_async_copy(v_ref.at[k], buffer.at[k], into.at[k]) for k in range(INNER)]
    for load in loads:
        load.start()
    for k in range(INNER):
        at = 0
        loads[k].wait()
        for c, ((cross, n, first, every), out, held) in enumerate(zip(parts, outs, helds)):
            v = buffer[k, at : at + n].astype(F32)
            held[k] = v.T if cross else v
            where = pl.ds((k * every + first) * n, n)
            copies.append(pltpu.make_async_copy(held.at[k], out.at[:, where] if cross else out.at[where], sems.at[c, k]))
            copies[-1].start()
            at += n
    for c in copies:
        c.wait()


def unpiece_call(line, v, shapes, parts, held):
    strip = v.shape[2]
    held = [h for h in held if h is not None]
    return run_kernel(
        functools.partial(unpiece_kernel, parts), [shaped(s, F32) for s in shapes],
        [ANYWHERE] * (1 + len(held)), [ANYWHERE] * len(shapes), (v, *held), "unpiece",
        scratch=[pltpu.VMEM((INNER, strip, n) if cross else (INNER, n, strip), F32) for cross, n, _, _ in parts]
        + [pltpu.VMEM(v.shape, BF), pltpu.SemaphoreType.DMA((len(parts), INNER)), pltpu.SemaphoreType.DMA((INNER,))],
        aliases={1 + k: k for k in range(len(held))}, line=line,
    )


def cat_kernel(a, b, out):
    out[0] = a[...]
    out[1] = b[...]


def cat_call(line, a, b, cols, at):
    n = a.shape[0] // 2
    shape = a.shape[:1] + (cols,) + a.shape[2:]
    spec = pl.BlockSpec((n,) + shape[1:], lambda k: (k, at, 0))
    out = run_kernel(
        cat_kernel, shaped((2,) + shape), [spec, spec],
        pl.BlockSpec((2, n) + shape[1:], lambda k: (0, k, 0, 0)), (a, b), "cat", grid=(2,), line=line,
    )
    return out.reshape((8,) + shape[1:])


def vectors_kernel(piece, nq, nf, share, tensor, place, small, g1, s1, g2, s2, r1, r2, out_bias, bq, bf, lengths):
    total = small.shape[0]
    per = total // 4
    width = per * piece

    def lay(to, b, k, where):
        part = small[b * per : (b + 1) * per, k * piece : (k + 1) * piece]
        to[:, where] = jnp.concatenate([part[r : r + 1] for r in range(per)], axis=1)

    for b in range(4):
        for k, to in enumerate((g1, s1, g2, s2)):
            lay(to, b, k, spot(place, b, width))
        lay(out_bias, b, 4, slice(b * width, (b + 1) * width))
    for gain, shift, ratio in ((g1, s1, r1), (g2, s2, r2)):
        v = shift[...] / gain[...]
        high = v.astype(BF).astype(F32)
        ratio[...] = jnp.concatenate([high, v - high, jnp.zeros((14, v.shape[1]), F32)], axis=0).astype(BF)
    at = 5 * piece
    for k in range(share):
        row = small[pl.ds((place[INSIDE] * share + k) * tensor + place[SIDE], 1), :]
        bq[:, k * nq : (k + 1) * nq] = row[:, at : at + nq]
        bf[:, k * nf : (k + 1) * nf] = row[:, at + nq : at + nq + nf]
    for g in range(INNER):
        row = small[pl.ds(place[DOC_ROW + g], 1), :]
        docs = row[:, at + nq + nf : at + nq + nf + LANES]
        lengths[g : g + 1] = (docs + 0.5).astype(jnp.int32)


def turns_kernel(own_rows, place, lengths, cos_ref, up_ref, down_ref):
    count = cos_ref.shape[0]
    group = pl.program_id(0)
    at = places(0, (count, 1), count, place[SIDE] * own_rows)
    end, begin = 0, jnp.zeros_like(at)
    for k in range(DOCS):
        end = end + lengths[group, k]
        begin = jnp.where(at >= end, end, begin)
    half = ROT // 2
    lane = lax.broadcasted_iota(jnp.int32, (1, LANES), 1)
    step = jnp.where(lane >= half, lane - half, lane).astype(F32)
    freq = jnp.exp(step * (-2.0 * math.log(10000.0) / ROT))
    angle = (at - begin).astype(F32) * freq
    sine = jnp.sin(angle)
    cos_ref[...] = jnp.where(lane < ROT, jnp.cos(angle), 1.0)
    up_ref[...] = jnp.where(lane < half, -sine, 0.0)
    down_ref[...] = jnp.where((lane >= half) & (lane < ROT), sine, 0.0)


def sum_kernel(*refs):
    total = refs[0][...].astype(F32)
    for r in refs[1:-1]:
        total += r[...].astype(F32)
    refs[-1][...] = total.astype(BF)


def sum_call(line, parts, firsts, count):
    n = count // 2
    shape = (n,) + parts[0].shape[1:]
    return run_kernel(
        sum_kernel, shaped((count,) + shape[1:]),
        [pl.BlockSpec(shape, functools.partial(lambda f, k: (k + f, 0, 0), f // n)) for f in firsts],
        pl.BlockSpec(shape, lambda k: (k, 0, 0)), parts, "sum", grid=(2,), line=line,
    )


def core_kernel(kt, kx, kb, ot, ox, ob, x1, t1):
    half = kb.shape[1] // 2
    add = lambda a, b: (a.astype(F32) + b.astype(F32)).astype(BF)
    x1[:, :half] = add(kb[:, :half], ob[:, :half])
    x1[:, half:] = add(kx[...], ox[...])
    t1[:, :half] = add(kb[:, half:], ob[:, half:])
    t1[:, half:] = add(kt[...], ot[...])


def cross_kernel(kt, kx, ot, ox, x1, t1, t2, x2):
    add = lambda a, b, c: (a[...].astype(F32) + b[...].astype(F32) + c[...].astype(F32)).astype(BF)
    t2[...] = add(kt, ot, x1)
    x2[...] = add(kx, ox, t1)


def face_sum(place, kept, other, x1, t1, t2, x2, natural):
    half = kept.shape[1] // 2
    left, right = slice(0, half), slice(half, 2 * half)
    natural[:, left] = kept[:, left].astype(F32) + other[:, left].astype(F32) + x1[...].astype(F32) + t2[...].astype(F32)
    natural[:, right] = kept[:, right].astype(F32) + other[:, right].astype(F32) + t1[...].astype(F32) + x2[...].astype(F32)
    return jnp.concatenate([natural[:, spot(place, b, half // 2)] for b in range(4)], axis=1)


def output_kernel(place, x_ref, bias_ref, kept, other, x1, t1, t2, x2, out_ref, natural):
    total = face_sum(place, kept, other, x1, t1, t2, x2, natural) + bias_ref[...] + x_ref[...].astype(F32)
    out_ref[...] = total.astype(BF)


def input_grad_kernel(place, x_ref, cot_ref, kept, other, x1, t1, t2, x2, out_ref, natural):
    pulled = face_sum(place, kept, other, x1, t1, t2, x2, natural)
    x = x_ref[...].astype(F32)
    centred = x - jnp.mean(x, axis=1, keepdims=True)
    rstd = lax.rsqrt(jnp.mean(centred * centred, axis=1, keepdims=True) + EPSILON)
    unit = centred * rstd
    along = jnp.mean(pulled * unit, axis=1, keepdims=True)
    level = jnp.mean(pulled, axis=1, keepdims=True)
    out_ref[...] = (cot_ref[...].astype(F32) + rstd * (pulled - level - unit * along)).astype(BF)


def own_rows_call(line, kernel, place, rows_in, row_in, sums, name):
    rows, width = rows_in[0].shape
    block = rows // STEPS
    spec = pl.BlockSpec((block, width), lambda r: (r, 0))
    half = pl.BlockSpec((block, width // 2), lambda r: (r, 0))
    second = pl.BlockSpec((block, width // 2), lambda r: (r, 1))
    vector = pl.BlockSpec((1, width), lambda r: (0, 0))
    return run_kernel(
        kernel, shaped((rows, width)),
        [SCALARS] + [spec] * len(rows_in) + [vector] * len(row_in) + [spec] * 2 + [second] * 2 + [half] * 2,
        spec, (place, *rows_in, *row_in, *sums), name, grid=(STEPS,), scratch=[pltpu.VMEM((block, width), F32)],
        line=line,
    )


def tail_kernel(piece, nq, nf, share, tensor, place, n_attn, n0, n1, n2, sum_q, f0, f1, f2, cot_sum, tail):
    total = tail.shape[0]
    per = total // 4
    width = per * piece
    tail[...] = jnp.zeros_like(tail)

    def lay(k, b, row):
        rows = jnp.concatenate([row[:, r * piece : (r + 1) * piece] for r in range(per)], axis=0)
        tail[b * per : (b + 1) * per, k * piece : (k + 1) * piece] = rows

    for b in range(4):
        at = spot(place, b, width)
        attn = n_attn[:, at]
        feeds = n0[:, at] + n1[:, at] + n2[:, at]
        for k, row in enumerate((attn[0:1], attn[1:2], feeds[0:1], feeds[1:2])):
            lay(k, b, row)
        lay(4, b, cot_sum[:, b * width : (b + 1) * width])
    hidden = jnp.concatenate([f0[...], f1[...], f2[...]], axis=1)
    query = sum_q[...]
    at = full_lanes(5 * piece)
    rest = jnp.zeros((1, full_lanes(nq + nf) - nq - nf), F32)
    line = lax.broadcasted_iota(jnp.int32, (total, 1), 0)
    below = jnp.zeros((total, full_lanes(nq + nf)), F32)
    for k in range(share):
        row = (place[INSIDE] * share + k) * tensor + place[SIDE]
        both = [query[:, k * nq : (k + 1) * nq], hidden[:, k * nf : (k + 1) * nf]]
        both = jnp.concatenate(both + [rest] if rest.shape[1] else both, axis=1)
        below = jnp.where(line == row, both, below)
    tail[:, at:] = below


def make(dp, tensor):
    outer = dp // INNER
    face = INNER * tensor
    total = dp * tensor
    short = outer == 4

    def permute(v, pairs):
        return lax.ppermute(v.reshape(-1, v.shape[-1]), AXES, pairs).reshape(v.shape)

    def flip(v, k):
        return permute(v, [(l, l ^ k) for l in range(total)])

    def hop(v, moves):
        return permute(v, [(a * face + f, b * face + f) for a, b in moves for f in range(face)])

    column_groups = [[o * face + f for o in range(outer)] for f in range(face)]
    ring_groups = [[o * face + i * tensor + t for i in range(INNER)] for o in range(outer) for t in range(tensor)]
    towards_middle = [(0, 1), (3, 2)]
    across_middle = [(1, 2), (2, 1)]
    towards_ends = [(1, 0), (2, 3)]

    back_table = [[0, 1, 2, 3], [1, 0, 2, 3], [3, 2, 0, 1], [3, 2, 1, 0]]

    def swap_ring(v):
        return lax.all_to_all(v, AXES, split_axis=0, concat_axis=0, tiled=True, axis_index_groups=ring_groups)

    def swap_all(v):
        return lax.all_to_all(v, AXES, split_axis=0, concat_axis=0, tiled=True)

    class Near:
        def __init__(self, v):
            self.own = v
            self.near = flip(v, face) if short else None

    class Gather:
        def __init__(self, line, v, cols, at):
            if not short:
                own = v.own[:, at * cols : (at + 1) * cols]
                every = lax.all_gather(own, AXES, axis=0, tiled=True, axis_index_groups=column_groups)
                every = every.transpose(1, 0, 2).reshape(cols, 16, LANES).transpose(1, 0, 2)
                self.parts = [every[:8], every[8:], jnp.zeros_like(every[8:])]
                return
            self.both = cat_call(line, v.own, v.near, cols, at)
            self.far = hop(self.both, across_middle)

        def far_came(self, line):
            if short:
                self.far = line(self.far)
                self.passed = hop(self.far, towards_ends)

        def passed_came(self, line):
            if short:
                self.passed = line(self.passed)
                self.parts = [self.both, self.far, self.passed]

    class Reduce:
        def __init__(self, line, own, rest):
            if not short:
                v = jnp.concatenate([own, rest], axis=0)
                v = v.transpose(1, 0, 2).reshape(v.shape[1], dp, -1).transpose(1, 0, 2)
                self.total = lax.psum_scatter(
                    v, AXES, scatter_dimension=0, tiled=True, axis_index_groups=column_groups
                )
                return
            self.own, self.rest = own, line(rest)
            self.first = hop(self.rest, towards_middle)

        def first_came(self, line):
            if short:
                far = sum_call(line, (self.rest, self.first), (4, 4), 8)
                self.second = hop(far, across_middle)

        def second_came(self, line):
            if short:
                near = sum_call(line, (self.rest, self.second), (0, 4), 4)
                self.third = hop(near, towards_ends)

        def third_came(self, line):
            if short:
                self.total = sum_call(line, (self.own, self.first, self.second, self.third), (0, 0, 0, 0), 4)
            self.final = swap_ring(self.total)

    class FaceReduce:
        def __init__(self, sent):
            self.other = flip(sent, 2)

        def core_came(self, line):
            self.rows, self.width = self.kept.shape[0] // 4, self.kept.shape[1]
            spec = pl.BlockSpec((self.rows // STEPS, self.width), lambda r: (r, 0))
            x1, t1 = run_kernel(
                core_kernel, [shaped((self.rows, self.width))] * 2, self.block_specs((1, 1), (2, 0), (3, None)) * 2, [spec] * 2,
                (self.kept,) * 3 + (self.other,) * 3, "core", grid=(STEPS,), line=line,
            )
            self.x1, self.t1 = flip(x1, 4), flip(t1, 1)

        def block_specs(self, *blocks):
            block = self.rows // STEPS
            return [
                pl.BlockSpec(
                    (block, self.width if half is None else self.width // 2),
                    functools.partial(lambda k, h, r: (k * STEPS + r, h), k, half or 0),
                )
                for k, half in blocks
            ]

        def first_came(self, line):
            rows, width = self.rows, self.width
            half = pl.BlockSpec((rows // STEPS, width // 2), lambda r: (r, 0))
            t2, x2 = run_kernel(
                cross_kernel, [shaped((rows, width // 2))] * 2, self.block_specs((1, 0), (2, 1)) * 2 + [half] * 2, [half] * 2,
                (self.kept, self.kept, self.other, self.other, self.x1, self.t1), "cross", grid=(STEPS,), line=line,
            )
            self.t2, self.x2 = flip(t2, 1), flip(x2, 4)

        def second_came(self):
            return self.kept, self.other, self.x1, self.t1, self.t2, self.x2

    def per_device(
        layer_input, doc_lengths, ln1_gain, ln1_bias, ln2_gain, ln2_bias, w_qkv, b_qkv, w_dense, b_dense,
        w_fc1, b_fc1, w_fc2, b_fc2, cotangent,
    ):
        d, t = lax.axis_index("dp"), lax.axis_index("tensor")
        o, i = d // INNER, d % INNER
        own_rows, width = layer_input.shape
        rows, group_rows = own_rows * face, own_rows * tensor
        strip = width // dp
        hidden_own = w_fc1.shape[1] // INNER
        qkv_own = w_qkv.shape[1] // INNER
        quarter = hidden_own // 4
        piece, nq, nf = width // total, b_qkv.shape[0], b_fc1.shape[0]
        share = dp // INNER
        line = Line()
        if short:
            spots = jnp.array(back_table, jnp.int32)[o]
        else:
            spots = jnp.arange(4, dtype=jnp.int32)
        doc_rows = (o * INNER + (i ^ jnp.arange(INNER, dtype=jnp.int32))) * tensor
        place = jnp.concatenate([jnp.stack([o, i, t]).astype(jnp.int32), spots, doc_rows.astype(jnp.int32)])

        forms = {
            0: ((w_fc1, w_fc2) * 2, tuple((cross, quarter, k, 4) for k in (0, 1) for cross in (True, False))),
            2: ((w_qkv,) * 3 + (w_dense,), tuple((True, HD, k, 3) for k in (0, 1, 2)) + ((False, HD, 0, 1),)),
            4: ((w_fc1, w_fc2), ((True, 2 * quarter, 1, 2), (False, 2 * quarter, 1, 2))),
        }
        cuts_of = {0: (0, 2 * quarter, 0), 1: (0, 2 * quarter, 1), 2: (2, 2 * HD, 0), 3: (2, 2 * HD, 1), 4: (4, 4 * quarter, 0)}
        s = {}
        steps = {}

        def own():
            s["own"], s["cot_sum"] = own_call(line, place, layer_input, cotangent)
            s["t"], s["x"], s["c"] = flip(s["own"], 1), flip(s["own"], 4), flip(s["own"], 2)

        def own_c():
            s["c"] = line(s["c"])

        def own_xt():
            s["x"], s["t"] = line(s["x"], s["t"])
            s["bu"], s["bv"] = flip(s["x"][0], 1), flip(s["t"][1], 4)
            s["tc"], s["xc"] = flip(s["t"], 2), flip(s["x"], 2)

        def own_tc():
            s["tc"], s["xc"] = line(s["tc"], s["xc"])

        def own_b():
            s["bu"], s["bv"] = line(s["bu"], s["bv"])
            s["buc"], s["bvc"] = flip(s["bu"], 2), flip(s["bv"], 2)

        def own_bc():
            s["buc"], s["bvc"] = line(s["buc"], s["bvc"])

        steps.update({"own": own, "c": own_c, "xt": own_xt, "tc": own_tc, "b": own_b, "bc": own_bc})

        def small():
            v = jnp.concatenate(
                [ln1_gain, ln1_bias, ln2_gain, ln2_bias, b_dense + b_fc2, b_qkv.astype(F32), b_fc1.astype(F32),
                 doc_lengths[0].astype(F32), jnp.zeros((LANES - DOCS,), F32)]
            )
            s["small"] = swap_all(line(jnp.broadcast_to(v[None], (total, v.shape[0]))))

        def small_came():
            s["small"] = line(s["small"])

        def vectors():
            v = s["small"].reshape(total, -1)
            row, fine = shaped((1, width), F32), shaped((16, width))
            *s["vec"], s["bias_q"], s["bias_f"], s["lengths"] = run_kernel(
                functools.partial(vectors_kernel, piece, nq, nf, share, tensor),
                [row] * 4 + [fine] * 2 + [row, shaped((1, qkv_own), F32), shaped((1, hidden_own), F32),
                                          shaped((INNER, LANES), jnp.int32)],
                [SCALARS, VECTORS], [VECTORS] * 10, (place, v), "vectors", line=line,
            )
            turn_spec = pl.BlockSpec((group_rows, LANES), lambda g: (g, 0))
            s["turns"] = run_kernel(
                functools.partial(turns_kernel, own_rows), [shaped((rows, LANES), F32)] * 3, [SCALARS] * 2,
                [turn_spec] * 3, (place, s["lengths"]), "turns", grid=(INNER,), line=line,
            )

        steps.update({"sm": small, "sw": small_came, "vec": vectors})
        nears, gathers, done, sums = {}, {}, {}, {}

        def near_steps(k):
            def p():
                arrays, parts = forms[k]
                s[f"ring{k}"] = swap_ring(piece_call(line, arrays, parts, strip))

            def g():
                nears[k] = Near(line(s[f"ring{k}"]))

            steps.update({f"p{k}": p, f"g{k}": g})

        def gather_steps(k):
            def h():
                of, cols, at = cuts_of[k]
                gathers[k] = Gather(line, nears[of], cols, at)

            steps.update({
                f"h{k}": h, f"i{k}": lambda: gathers[k].far_came(line), f"j{k}": lambda: gathers[k].passed_came(line),
            })

        for k in forms:
            near_steps(k)
        for k in cuts_of:
            gather_steps(k)

        def pieces():
            return [s[n] for n in ("own", "t", "c", "tc", "x", "xc", "bu", "bv", "buc", "bvc")]

        def feed(k, first, split, sets):
            def run():
                gain, shift, ratio = s["vec"][2], s["vec"][3], s["vec"][5]
                cols = split * quarter
                bias = s["bias_f"][:, first * quarter : first * quarter + cols]
                done[k] = chunk_call(
                    line, functools.partial(feed_kernel, cols, split, len(sets)), "feed", pieces(), (), [],
                    [gathers[j].parts for j in sets], (gain, shift, ratio, bias), cols, cols, split,
                )

            return run

        def attention():
            gain, shift, ratio = s["vec"][0], s["vec"][1], s["vec"][4]
            one, two = gathers[2].parts, gathers[3].parts
            turn_spec = pl.BlockSpec((group_rows, LANES), lambda r: (r, 0))
            done[2] = chunk_call(
                line, functools.partial(attention_kernel, qkv_own), "attention", pieces(),
                (s["lengths"], place, *s["turns"]), [SCALARS, SCALARS] + [turn_spec] * 3, [one, two],
                (gain, shift, ratio, s["bias_q"]), qkv_own, HD, 1,
            )

        steps.update({"K0": feed(0, 0, 1, (0,)), "K1": feed(1, 1, 1, (1,)), "KA": attention, "K4": feed(4, 2, 2, (4,))})

        def reduce_steps(k, chunk, at):
            def r():
                sums[k] = Reduce(line, *done[chunk][at : at + 2])

            def z():
                final = sums[k].final
                if k == 2:
                    s["qkv"], s["dense"] = unpiece_call(
                        line, final, (w_qkv.shape, w_dense.shape), ((True, qkv_own, 0, 1), (False, HD, 0, 1)), ()
                    )
                elif k < 2:
                    s["fc1"], s["fc2"] = unpiece_call(
                        line, final, (w_fc1.shape, w_fc2.shape), forms[0][1][2 * k : 2 * k + 2], (s.get("fc1"), s.get("fc2"))
                    )
                else:
                    name, w, form = (("fc1", w_fc1, 0), ("fc2", w_fc2, 1))[k - 3]
                    s[name], = unpiece_call(line, final, (w.shape,), forms[4][1][form : form + 1], (s[name],))

            steps.update({
                f"r{k}": r, f"u{k}": lambda: sums[k].first_came(line), f"v{k}": lambda: sums[k].second_came(line),
                f"w{k}": lambda: sums[k].third_came(line), f"z{k}": z,
            })

        for k, chunk, at in ((0, 0, 6), (1, 1, 6), (2, 2, 6), (3, 4, 6), (4, 4, 8)):
            reduce_steps(k, chunk, at)

        def face_steps(name, act, weight, finish):
            def parts():
                chunks = [done[k] for k in (0, 1, 2, 4)]
                return [c[act] for c in chunks], [c[weight] for c in chunks]

            def sent():
                s["face" + name] = FaceReduce(join_call(line, *parts(), True))

            def kept():
                s["face" + name].kept = join_call(line, *parts(), False)

            steps.update({
                "J" + name: sent, "k" + name: kept, "C" + name: lambda: s["face" + name].core_came(line),
                "D" + name: lambda: s["face" + name].first_came(line),
                "E" + name: lambda: finish(s["face" + name].second_came()),
            })

        def finish_back(sums_in):
            s["input_grad"] = own_rows_call(
                line, input_grad_kernel, place, (layer_input, cotangent), (), sums_in, "input_grad"
            )

        def finish_out(sums_in):
            s["output"] = own_rows_call(line, output_kernel, place, (layer_input,), (s["vec"][6],), sums_in, "output")

        face_steps("B", 1, 2, finish_back)
        face_steps("O", 0, 3, finish_out)

        def tail():
            feeds = [done[k] for k in (0, 1, 4)]
            v = run_kernel(
                functools.partial(tail_kernel, piece, nq, nf, share, tensor),
                shaped((total, full_lanes(5 * piece) + full_lanes(nq + nf)), F32), [SCALARS] + [VECTORS] * 9, VECTORS,
                (place, done[2][4], *[p[4] for p in feeds], done[2][5], *[p[5] for p in feeds], s["cot_sum"]), "tail", line=line,
            )
            s["tail"] = swap_all(v)

        def tail_came():
            s["tail"] = jnp.sum(line(s["tail"]), axis=0)

        steps.update({"tail": tail, "tz": tail_came})
        for name in ORDER:
            steps[name]()

        tail_row = s["tail"]
        cuts = [tail_row[j * piece : (j + 1) * piece] for j in range(5)]
        at = full_lanes(5 * piece)
        return (
            s["output"], s["input_grad"], cuts[0], cuts[1], cuts[2], cuts[3], s["qkv"], tail_row[at : at + nq],
            s["dense"], cuts[4], s["fc1"], tail_row[at + nq : at + nq + nf], s["fc2"], cuts[4],
        )

    return per_device


def solution(mesh):
    rows = P(("dp", "tensor"), None)
    vector = P(("dp", "tensor"))
    crossed = P(("tensor", "dp"))
    wide = P("dp", "tensor")
    tall = P("tensor", "dp")
    return jax.shard_map(
        make(mesh.shape["dp"], mesh.shape["tensor"]),
        mesh=mesh,
        in_specs=(rows, P("dp", None), vector, vector, vector, vector, wide, crossed, tall, vector, wide, crossed,
                  tall, vector, rows),
        out_specs=(rows, rows, vector, vector, vector, vector, wide, crossed, tall, vector, wide, crossed, tall,
                   vector),
        check_vma=False,
    )
```

```python
import functools
import math

import jax
import jax.numpy as jnp
from jax import lax
from jax.experimental import pallas as pl
from jax.experimental.pallas import tpu as pltpu
from jax.sharding import PartitionSpec as P

HD = 256
ROT = 64
DOCS = 3
EPSILON = 1e-05
INNER = 4
LANES = 128
AXES = ("dp", "tensor")
BF = jnp.bfloat16
F32 = jnp.float32
NT = ((1,), (1,))
NN = ((1,), (0,))
TN = ((0,), (0,))
VMEM = 63 * 2**20
STEPS = 4


ORDER = (
    "p0", "p2", "g0", "g2", "own", "h0", "h1", "sm", "i0", "c", "h2", "h3", "sw", "xt", "i1", "vec", "j0", "p4",
    "b", "j1", "i2", "g4", "bc", "tc", "K0", "r0", "i3", "h4", "K1", "i4", "j2", "j3", "r1", "KA", "r2", "u0", "j4",
    "u1", "K4", "r3", "r4", "v0", "JB", "v1", "JO", "u2", "kB", "w0", "CB", "kO", "u3", "z0", "v2", "CO", "DB",
    "tail", "v3", "u4", "w2", "tz", "w1", "DO", "z2", "EO", "v4", "w3", "EB", "z1", "w4", "z3", "z4",
)

NOTHING = pl.CostEstimate(flops=0, bytes_accessed=0, transcendentals=0)
SCALARS = pl.BlockSpec(memory_space=pltpu.SMEM)
ANYWHERE = pl.BlockSpec(memory_space=pl.ANY)
VECTORS = pl.BlockSpec(memory_space=pltpu.VMEM)

OUTER, INSIDE, SIDE, SPOT, DOC_ROW = 0, 1, 2, 3, 7


def dot(a, b, dims):
    return lax.dot_general(a, b, (dims, ((), ())), preferred_element_type=F32)


def shaped(shape, dtype=BF):
    return jax.ShapeDtypeStruct(shape, dtype)


def whole(shape):
    return pl.BlockSpec(shape, lambda *_: (0,) * len(shape), pipeline_mode=pl.Buffered(1))


def run_kernel(
    kernel, outs, in_specs, out_specs, args, name, grid=(), scratch=(), aliases=None, line=None
):
    one = not isinstance(outs, (list, tuple))
    outs, out_specs = ([outs], [out_specs]) if one else (list(outs), list(out_specs))
    in_specs, args, aliases, inner = list(in_specs), list(args), dict(aliases or {}), kernel
    if line is not None:
        n, m = len(args), len(outs)
        aliases[n] = m
        in_specs.append(ANYWHERE)
        out_specs.append(ANYWHERE)
        args.append(line.mark)
        outs.append(shaped(line.mark.shape, line.mark.dtype))

        def inner(*refs):
            kernel(*refs[:n], *refs[n + 1 : n + 1 + m], *refs[n + 2 + m :])

    got = pl.pallas_call(
        inner,
        grid=grid,
        out_shape=outs,
        in_specs=in_specs,
        out_specs=out_specs,
        scratch_shapes=scratch,
        input_output_aliases=aliases,
        compiler_params=pltpu.CompilerParams(vmem_limit_bytes=VMEM),
        cost_estimate=NOTHING,
        name=name,
    )(*args)
    if line is not None:
        *got, line.mark = got
    return got[0] if one else got


def gate_kernel(*refs):
    pass


class Line:
    def __init__(self):
        self.mark = jnp.zeros((8, LANES), F32)

    def __call__(self, *arrays):
        held = (*arrays, self.mark)
        *held, self.mark = run_kernel(
            gate_kernel, [shaped(v.shape, v.dtype) for v in held], [ANYWHERE] * len(held), [ANYWHERE] * len(held),
            held, "gate", aliases={n: n for n in range(len(held))},
        )
        return held[0] if len(held) == 1 else held


def spot(place, b, width):
    return pl.ds(pl.multiple_of(place[SPOT + b] * width, width), width)


def places(axis, shape, count, shift):
    at = lax.broadcasted_iota(jnp.int32, shape, axis) + shift
    return jnp.where(at >= count, at - count, at)


def full_lanes(n):
    return n + -n % LANES


def take_weights(parts, gain_ref, dests):
    both, far, passed = parts
    for b in range(16):
        lanes = slice(b * LANES, (b + 1) * LANES)
        block = both[b].astype(F32) if b < 8 else far[b - 8].astype(F32) + passed[b - 8].astype(F32)
        for lo, hi, to, at, gained in dests:
            rows = block[lo:hi]
            to[at : at + hi - lo, lanes] = (rows * gain_ref[:, lanes] if gained else rows).astype(BF)


def give_grads(blocks, acc1, acc2, col, gain_ref, shift_ref, w1, to1, to2, norm_ref):
    for b in blocks:
        lanes = slice(b * LANES, (b + 1) * LANES)
        gain = gain_ref[:, lanes]
        m = acc1[:, lanes]
        w = w1[:, lanes].astype(F32)
        for (own, rest, at), v in ((to1, m * gain + col[...] * shift_ref[:, lanes]), (to2, acc2[:, lanes])):
            to, k = (own, b) if b < 4 else (rest, b - 4)
            to[k, at : at + v.shape[0]] = v.astype(BF)
        norm_ref[0:1, lanes] = jnp.sum(w * m, axis=0, keepdims=True) / gain
        norm_ref[1:2, lanes] = jnp.sum(w * col[...], axis=0, keepdims=True) / gain


def add_grads(step, grad, unit, act, cot, acc1, acc2, col, sum_ref, finish):
    col[...] += dot(grad, jnp.ones((grad.shape[0], LANES), BF), TN)
    sum_ref[...] += jnp.sum(grad.astype(F32), axis=0, keepdims=True)
    last = pl.num_programs(0) - 1

    @pl.when(step < last)
    def _():
        acc1[...] += dot(grad, unit, TN)
        acc2[...] += dot(act, cot, TN)

    @pl.when(step == last)
    def _():
        width = unit.shape[1] // 4
        for part in range(4):
            lanes = slice(part * width, (part + 1) * width)
            acc1[:, lanes] += dot(grad, unit[:, lanes], TN)
            acc2[:, lanes] += dot(act, cot[:, lanes], TN)
            finish(range(4 * part, 4 * part + 4))


def stream(step, pieces, unit_buf, cot_buf, sems):
    blocks = [(p.at[0], p.at[1]) for p in pieces[:6]] + [(pieces[6], pieces[7]), (pieces[8], pieces[9])]
    blocks = [blocks[k] for k in (0, 1, 2, 3, 4, 6, 5, 7)]
    rows = pieces[0].shape[1]
    steps = len(blocks) // 2

    def copies(s):
        made = []
        for k in (2 * s, 2 * s + 1):
            for n, buffer in enumerate((unit_buf, cot_buf)):
                to = buffer.at[s % 2, pl.ds((k % 2) * rows, rows)]
                made.append(pltpu.make_async_copy(blocks[k][n], to, sems.at[s % 2, len(made)]))
        return made

    def begin(s):
        for c in copies(s):
            c.start()

    def arrive():
        for s in range(steps):
            @pl.when(step == s)
            def _(s=s):
                if s + 1 < steps:
                    begin(s + 1)
                for c in copies(s):
                    c.wait()

    return begin, arrive


def stream_scratch(rows, width):
    return [pltpu.VMEM((2, rows, width), BF), pltpu.VMEM((2, rows, width), BF), pltpu.SemaphoreType.DMA((2, 4))]


def feed_kernel(cols, split, sets, *refs):
    pieces, parts, refs = refs[:10], refs[10 : 10 + 3 * sets], refs[10 + 3 * sets :]
    gain_ref, shift_ref, ratio_ref, bias_ref = refs[:4]
    hidden_ref, pre_grad_ref, w1, w2, norm_ref, sum_ref = refs[4:10]
    grads, refs = refs[10 : 10 + 2 * split], refs[10 + 2 * split :]
    acc1, acc2, col, row, unit_buf, cot_buf, sems = refs
    step = pl.program_id(0)
    begin, arrive = stream(step, pieces, unit_buf, cot_buf, sems)

    @pl.when(step == 0)
    def _():
        begin(0)
        n = cols // sets
        for k in range(sets):
            take_weights(parts[3 * k : 3 * k + 3], gain_ref, ((0, n, w1, k * n, True), (n, 2 * n, w2, k * n, False)))
        row[...] = jnp.sum(dot(ratio_ref[...], w1[...], NT), axis=0, keepdims=True) + bias_ref[...]
        acc1[...] = jnp.zeros_like(acc1)
        acc2[...] = jnp.zeros_like(acc2)
        col[...] = jnp.zeros_like(col)
        sum_ref[...] = jnp.zeros_like(sum_ref)

    arrive()
    slot = lax.rem(step, 2)
    unit = unit_buf[slot]
    cot = cot_buf[slot]
    pre = dot(unit, w1[...], NT) + row[...]
    back = dot(cot, w2[...], NT)
    phi = 0.5 * (1.0 + lax.erf(pre * (1.0 / math.sqrt(2.0))))
    slope = phi + pre * (jnp.exp(-0.5 * pre * pre) * (1.0 / math.sqrt(2.0 * math.pi)))
    hidden = (pre * phi).astype(BF)
    pre_grad = (back * slope).astype(BF)
    hidden_ref[...] = hidden
    pre_grad_ref[...] = pre_grad
    to1 = (*grads[:2], 0)
    to2 = (*grads[2:], 0) if split == 2 else (*grads[:2], cols)
    finish = lambda blocks: give_grads(blocks, acc1, acc2, col, gain_ref, shift_ref, w1, to1, to2, norm_ref)
    add_grads(step, pre_grad, unit, hidden, cot, acc1, acc2, col, sum_ref, finish)


def chunk_call(line, kernel, name, pieces, extra_in, extra_specs, sets, vectors, cols, others, split):
    _, part, width = pieces[0].shape
    block, rows = 2 * part, 8 * part
    per_row = lambda n: pl.BlockSpec((block, n), lambda r: (r, 0))
    shapes = [
        shaped((rows, others)), shaped((rows, cols)), shaped((cols, width)), shaped((others, width)),
        shaped((2, width), F32), shaped((1, cols), F32),
    ]
    specs = [per_row(others), per_row(cols)] + [whole(s.shape) for s in shapes[2:]]
    for n in (cols, others) if split == 2 else (cols + others,):
        shapes += [shaped((4, n, LANES)), shaped((12, n, LANES))]
    specs += [whole(s.shape) for s in shapes[6:]]
    weights = [w for s in sets for w in s]
    return run_kernel(
        kernel, shapes,
        [ANYWHERE] * 10 + [whole(w.shape) for w in weights] + [whole(v.shape) for v in vectors] + extra_specs,
        specs, (*pieces, *weights, *vectors, *extra_in), name, grid=(rows // block,),
        scratch=[
            pltpu.VMEM((cols, width), F32), pltpu.VMEM((others, width), F32), pltpu.VMEM((cols, LANES), F32),
            pltpu.VMEM((1, cols), F32),
        ]
        + stream_scratch(block, width),
        line=line,
    )


def attention_kernel(cols, *refs):
    pieces, refs = refs[:10], refs[10:]
    set_one, set_two, refs = refs[:3], refs[3:6], refs[6:]
    gain_ref, shift_ref, ratio_ref, bias_ref, lengths, place, cos_ref, sin_up_ref, sin_down_ref = refs[:9]
    mixed_ref, qkv_grad_ref, w1, w2, norm_ref, sum_ref, own_ref, rest_ref = refs[9:17]
    acc1, acc2, col, row, unit_buf, cot_buf, sems = refs[17:]
    group = pl.program_id(0)
    begin, arrive = stream(group, pieces, unit_buf, cot_buf, sems)

    @pl.when(group == 0)
    def _():
        begin(0)
        take_weights(set_one, gain_ref, ((0, 2 * HD, w1, 0, True),))
        take_weights(set_two, gain_ref, ((0, HD, w1, 2 * HD, True), (HD, 2 * HD, w2, 0, False)))
        row[...] = jnp.sum(dot(ratio_ref[...], w1[...], NT), axis=0, keepdims=True) + bias_ref[...]
        acc1[...] = jnp.zeros_like(acc1)
        acc2[...] = jnp.zeros_like(acc2)
        col[...] = jnp.zeros_like(col)
        sum_ref[...] = jnp.zeros_like(sum_ref)

    arrive()
    slot = lax.rem(group, 2)
    unit = unit_buf[slot]
    cot = cot_buf[slot]
    count = unit.shape[0]
    cosine, sin_up, sin_down = cos_ref[...], sin_up_ref[...], sin_down_ref[...]
    half = ROT // 2

    def turn(u):
        p = u[:, :LANES]
        p = p * cosine + pltpu.roll(p, LANES - half, 1) * sin_up + pltpu.roll(p, half, 1) * sin_down
        return jnp.concatenate([p, u[:, LANES:]], axis=1)

    def unturn(u):
        p = u[:, :LANES]
        p = p * cosine + pltpu.roll(p * sin_up, half, 1) + pltpu.roll(p * sin_down, LANES - half, 1)
        return jnp.concatenate([p, u[:, LANES:]], axis=1)

    qkv = dot(unit, w1[...], NT) + row[...]
    query = turn(qkv[:, :HD]).astype(BF)
    key = turn(qkv[:, HD : 2 * HD]).astype(BF)
    value = qkv[:, 2 * HD :].astype(BF)
    back = dot(cot, w2[...], NT).astype(BF)

    shift = place[SIDE] * (count // 2)
    at = places(0, (count, 1), count, shift)
    to = places(1, (1, count), count, shift)
    end, seg_at, seg_to = 0, jnp.zeros_like(at), jnp.zeros_like(to)
    for k in range(DOCS):
        end = end + lengths[group, k]
        seg_at = seg_at + jnp.where(at >= end, 1, 0)
        seg_to = seg_to + jnp.where(to >= end, 1, 0)
    seg_at = jnp.where(seg_at == DOCS, DOCS + at, seg_at)
    seg_to = jnp.where(seg_to == DOCS, DOCS + to, seg_to)
    visible = (seg_at == seg_to) & (to <= at)

    scale = 1.0 / math.sqrt(HD)
    query = query * jnp.asarray(scale, BF)
    scores = jnp.where(visible, dot(query, key, NT), -1e30)
    expo = jnp.exp(scores - jnp.max(scores, axis=1, keepdims=True))
    probs = expo * (1.0 / jnp.sum(expo, axis=1, keepdims=True))
    low = probs.astype(BF)
    mixed = dot(low, value, NN).astype(BF)
    value_grad = dot(low, back, TN)
    probs_grad = dot(back, value, NT)
    inner = jnp.sum(probs * probs_grad, axis=1, keepdims=True)
    score_grad = (probs * (probs_grad - inner)).astype(BF)
    query_grad = unturn(dot(score_grad, key, NN) * scale)
    key_grad = unturn(dot(score_grad, query, TN))
    qkv_grad = jnp.concatenate([query_grad, key_grad, value_grad], axis=1).astype(BF)
    mixed_ref[...] = mixed
    qkv_grad_ref[...] = qkv_grad
    to1, to2 = (own_ref, rest_ref, 0), (own_ref, rest_ref, cols)
    finish = lambda blocks: give_grads(blocks, acc1, acc2, col, gain_ref, shift_ref, w1, to1, to2, norm_ref)
    add_grads(group, qkv_grad, unit, mixed, cot, acc1, acc2, col, sum_ref, finish)


def join_kernel(n, *refs):
    acts = [r[...].reshape(-1, r.shape[-1]) for r in refs[:n]]
    total = dot(acts[0], refs[n][...], NN)
    for j in range(1, n):
        total += dot(acts[j], refs[n + j][...], NN)
    refs[2 * n][...] = total.astype(BF)


def join_call(line, acts, weights, sent):
    rows, width = acts[0].shape[0], weights[0].shape[1]
    block, part = rows // 4, width // 4
    first = 1 if sent else 0
    acts = [a.reshape(2, 2, block, a.shape[1]) for a in acts]
    return run_kernel(
        functools.partial(join_kernel, len(acts)),
        shaped((rows // 2, width)),
        [pl.BlockSpec((2, None) + a.shape[2:], lambda c: (0, first, 0, 0), pipeline_mode=pl.Buffered(1)) for a in acts]
        + [pl.BlockSpec((w.shape[0], part), lambda c: (0, c)) for w in weights],
        pl.BlockSpec((rows // 2, part), lambda c: (0, c)),
        (*acts, *weights),
        "join",
        grid=(4,),
        line=line,
    )


def own_kernel(place, x_ref, cot_ref, out_ref, sum_ref):
    x = x_ref[...].astype(F32)
    centred = x - jnp.mean(x, axis=1, keepdims=True)
    spread = jnp.mean(centred * centred, axis=1, keepdims=True)
    unit = (centred * lax.rsqrt(spread + EPSILON)).astype(BF)
    width = x.shape[1] // 4
    for b in range(4):
        out_ref[0, :, spot(place, b, width)] = unit[:, b * width : (b + 1) * width]
        out_ref[1, :, spot(place, b, width)] = cot_ref[:, b * width : (b + 1) * width]

    @pl.when(pl.program_id(0) == 0)
    def _():
        sum_ref[...] = jnp.zeros_like(sum_ref)

    sum_ref[...] += jnp.sum(cot_ref[...].astype(F32), axis=0, keepdims=True)


def own_call(line, place, x, cot):
    rows, width = x.shape
    spec = pl.BlockSpec((rows // STEPS, width), lambda r: (r, 0))
    return run_kernel(
        own_kernel, [shaped((2, rows, width)), shaped((1, width), F32)], [SCALARS, spec, spec],
        [pl.BlockSpec((2, rows // STEPS, width), lambda r: (0, r, 0)), pl.BlockSpec((1, width), lambda r: (0, 0))],
        (place, x, cot), "own", grid=(STEPS,), line=line,
    )


def part_specs(parts, strip):
    specs = []
    for cross, n, first, every in parts:
        if cross:
            specs.append(pl.BlockSpec((strip, n), functools.partial(lambda f, e, k: (0, k * e + f), first, every)))
        else:
            specs.append(pl.BlockSpec((n, strip), functools.partial(lambda f, e, k: (k * e + f, 0), first, every)))
    return specs


def piece_kernel(parts, *refs):
    out_ref, at = refs[-1], 0
    for (cross, n, *_), ref in zip(parts, refs):
        out_ref[0, at : at + n] = ref[...].astype(F32).T.astype(BF) if cross else ref[...]
        at += n


def piece_call(line, arrays, parts, strip):
    n = sum(p[1] for p in parts)
    return run_kernel(
        functools.partial(piece_kernel, parts), shaped((INNER, n, strip)), part_specs(parts, strip),
        pl.BlockSpec((1, n, strip), lambda k: (k, 0, 0)), arrays, "piece", grid=(INNER,),
        line=line,
    )


def unpiece_kernel(parts, *refs):
    count = len(parts)
    v_ref, refs = refs[0], refs[-2 * count - 3 :]
    outs, helds, buffer, sems, into = refs[:count], refs[count : 2 * count], refs[-3], refs[-2], refs[-1]
    copies = []
    loads = [pltpu.make_async_copy(v_ref.at[k], buffer.at[k], into.at[k]) for k in range(INNER)]
    for load in loads:
        load.start()
    for k in range(INNER):
        at = 0
        loads[k].wait()
        for c, ((cross, n, first, every), out, held) in enumerate(zip(parts, outs, helds)):
            v = buffer[k, at : at + n].astype(F32)
            held[k] = v.T if cross else v
            where = pl.ds((k * every + first) * n, n)
            copies.append(pltpu.make_async_copy(held.at[k], out.at[:, where] if cross else out.at[where], sems.at[c, k]))
            copies[-1].start()
            at += n
    for c in copies:
        c.wait()


def unpiece_call(line, v, shapes, parts, held):
    strip = v.shape[2]
    held = [h for h in held if h is not None]
    return run_kernel(
        functools.partial(unpiece_kernel, parts), [shaped(s, F32) for s in shapes],
        [ANYWHERE] * (1 + len(held)), [ANYWHERE] * len(shapes), (v, *held), "unpiece",
        scratch=[pltpu.VMEM((INNER, strip, n) if cross else (INNER, n, strip), F32) for cross, n, _, _ in parts]
        + [pltpu.VMEM(v.shape, BF), pltpu.SemaphoreType.DMA((len(parts), INNER)), pltpu.SemaphoreType.DMA((INNER,))],
        aliases={1 + k: k for k in range(len(held))}, line=line,
    )


def cat_kernel(a, b, out):
    out[0] = a[...]
    out[1] = b[...]


def cat_call(line, a, b, cols, at):
    n = a.shape[0] // 2
    shape = a.shape[:1] + (cols,) + a.shape[2:]
    spec = pl.BlockSpec((n,) + shape[1:], lambda k: (k, at, 0))
    out = run_kernel(
        cat_kernel, shaped((2,) + shape), [spec, spec],
        pl.BlockSpec((2, n) + shape[1:], lambda k: (0, k, 0, 0)), (a, b), "cat", grid=(2,), line=line,
    )
    return out.reshape((8,) + shape[1:])


def vectors_kernel(piece, nq, nf, share, tensor, place, small, g1, s1, g2, s2, r1, r2, out_bias, bq, bf, lengths):
    total = small.shape[0]
    per = total // 4
    width = per * piece

    def lay(to, b, k, where):
        part = small[b * per : (b + 1) * per, k * piece : (k + 1) * piece]
        to[:, where] = jnp.concatenate([part[r : r + 1] for r in range(per)], axis=1)

    for b in range(4):
        for k, to in enumerate((g1, s1, g2, s2)):
            lay(to, b, k, spot(place, b, width))
        lay(out_bias, b, 4, slice(b * width, (b + 1) * width))
    for gain, shift, ratio in ((g1, s1, r1), (g2, s2, r2)):
        v = shift[...] / gain[...]
        high = v.astype(BF).astype(F32)
        ratio[...] = jnp.concatenate([high, v - high, jnp.zeros((14, v.shape[1]), F32)], axis=0).astype(BF)
    at = 5 * piece
    for k in range(share):
        row = small[pl.ds((place[INSIDE] * share + k) * tensor + place[SIDE], 1), :]
        bq[:, k * nq : (k + 1) * nq] = row[:, at : at + nq]
        bf[:, k * nf : (k + 1) * nf] = row[:, at + nq : at + nq + nf]
    for g in range(INNER):
        row = small[pl.ds(place[DOC_ROW + g], 1), :]
        docs = row[:, at + nq + nf : at + nq + nf + LANES]
        lengths[g : g + 1] = (docs + 0.5).astype(jnp.int32)


def turns_kernel(own_rows, place, lengths, cos_ref, up_ref, down_ref):
    count = cos_ref.shape[0]
    group = pl.program_id(0)
    at = places(0, (count, 1), count, place[SIDE] * own_rows)
    end, begin = 0, jnp.zeros_like(at)
    for k in range(DOCS):
        end = end + lengths[group, k]
        begin = jnp.where(at >= end, end, begin)
    half = ROT // 2
    lane = lax.broadcasted_iota(jnp.int32, (1, LANES), 1)
    step = jnp.where(lane >= half, lane - half, lane).astype(F32)
    freq = jnp.exp(step * (-2.0 * math.log(10000.0) / ROT))
    angle = (at - begin).astype(F32) * freq
    sine = jnp.sin(angle)
    cos_ref[...] = jnp.where(lane < ROT, jnp.cos(angle), 1.0)
    up_ref[...] = jnp.where(lane < half, -sine, 0.0)
    down_ref[...] = jnp.where((lane >= half) & (lane < ROT), sine, 0.0)


def sum_kernel(*refs):
    total = refs[0][...].astype(F32)
    for r in refs[1:-1]:
        total += r[...].astype(F32)
    refs[-1][...] = total.astype(BF)


def sum_call(line, parts, firsts, count):
    n = count // 2
    shape = (n,) + parts[0].shape[1:]
    return run_kernel(
        sum_kernel, shaped((count,) + shape[1:]),
        [pl.BlockSpec(shape, functools.partial(lambda f, k: (k + f, 0, 0), f // n)) for f in firsts],
        pl.BlockSpec(shape, lambda k: (k, 0, 0)), parts, "sum", grid=(2,), line=line,
    )


def core_kernel(kt, kx, kb, ot, ox, ob, x1, t1):
    half = kb.shape[1] // 2
    add = lambda a, b: (a.astype(F32) + b.astype(F32)).astype(BF)
    x1[:, :half] = add(kb[:, :half], ob[:, :half])
    x1[:, half:] = add(kx[...], ox[...])
    t1[:, :half] = add(kb[:, half:], ob[:, half:])
    t1[:, half:] = add(kt[...], ot[...])


def cross_kernel(kt, kx, ot, ox, x1, t1, t2, x2):
    add = lambda a, b, c: (a[...].astype(F32) + b[...].astype(F32) + c[...].astype(F32)).astype(BF)
    t2[...] = add(kt, ot, x1)
    x2[...] = add(kx, ox, t1)


def face_sum(place, kept, other, x1, t1, t2, x2, natural):
    half = kept.shape[1] // 2
    left, right = slice(0, half), slice(half, 2 * half)
    natural[:, left] = kept[:, left].astype(F32) + other[:, left].astype(F32) + x1[...].astype(F32) + t2[...].astype(F32)
    natural[:, right] = kept[:, right].astype(F32) + other[:, right].astype(F32) + t1[...].astype(F32) + x2[...].astype(F32)
    return jnp.concatenate([natural[:, spot(place, b, half // 2)] for b in range(4)], axis=1)


def output_kernel(place, x_ref, bias_ref, kept, other, x1, t1, t2, x2, out_ref, natural):
    total = face_sum(place, kept, other, x1, t1, t2, x2, natural) + bias_ref[...] + x_ref[...].astype(F32)
    out_ref[...] = total.astype(BF)


def input_grad_kernel(place, x_ref, cot_ref, kept, other, x1, t1, t2, x2, out_ref, natural):
    pulled = face_sum(place, kept, other, x1, t1, t2, x2, natural)
    x = x_ref[...].astype(F32)
    centred = x - jnp.mean(x, axis=1, keepdims=True)
    rstd = lax.rsqrt(jnp.mean(centred * centred, axis=1, keepdims=True) + EPSILON)
    unit = centred * rstd
    along = jnp.mean(pulled * unit, axis=1, keepdims=True)
    level = jnp.mean(pulled, axis=1, keepdims=True)
    out_ref[...] = (cot_ref[...].astype(F32) + rstd * (pulled - level - unit * along)).astype(BF)


def own_rows_call(line, kernel, place, rows_in, row_in, sums, name):
    rows, width = rows_in[0].shape
    block = rows // STEPS
    spec = pl.BlockSpec((block, width), lambda r: (r, 0))
    half = pl.BlockSpec((block, width // 2), lambda r: (r, 0))
    second = pl.BlockSpec((block, width // 2), lambda r: (r, 1))
    vector = pl.BlockSpec((1, width), lambda r: (0, 0))
    return run_kernel(
        kernel, shaped((rows, width)),
        [SCALARS] + [spec] * len(rows_in) + [vector] * len(row_in) + [spec] * 2 + [second] * 2 + [half] * 2,
        spec, (place, *rows_in, *row_in, *sums), name, grid=(STEPS,), scratch=[pltpu.VMEM((block, width), F32)],
        line=line,
    )


def tail_kernel(piece, nq, nf, share, tensor, place, n_attn, n0, n1, n2, sum_q, f0, f1, f2, cot_sum, tail):
    total = tail.shape[0]
    per = total // 4
    width = per * piece
    tail[...] = jnp.zeros_like(tail)

    def lay(k, b, row):
        rows = jnp.concatenate([row[:, r * piece : (r + 1) * piece] for r in range(per)], axis=0)
        tail[b * per : (b + 1) * per, k * piece : (k + 1) * piece] = rows

    for b in range(4):
        at = spot(place, b, width)
        attn = n_attn[:, at]
        feeds = n0[:, at] + n1[:, at] + n2[:, at]
        for k, row in enumerate((attn[0:1], attn[1:2], feeds[0:1], feeds[1:2])):
            lay(k, b, row)
        lay(4, b, cot_sum[:, b * width : (b + 1) * width])
    hidden = jnp.concatenate([f0[...], f1[...], f2[...]], axis=1)
    query = sum_q[...]
    at = full_lanes(5 * piece)
    rest = jnp.zeros((1, full_lanes(nq + nf) - nq - nf), F32)
    line = lax.broadcasted_iota(jnp.int32, (total, 1), 0)
    below = jnp.zeros((total, full_lanes(nq + nf)), F32)
    for k in range(share):
        row = (place[INSIDE] * share + k) * tensor + place[SIDE]
        both = [query[:, k * nq : (k + 1) * nq], hidden[:, k * nf : (k + 1) * nf]]
        both = jnp.concatenate(both + [rest] if rest.shape[1] else both, axis=1)
        below = jnp.where(line == row, both, below)
    tail[:, at:] = below


def make(dp, tensor):
    outer = dp // INNER
    face = INNER * tensor
    total = dp * tensor
    short = outer == 4

    def permute(v, pairs):
        return lax.ppermute(v.reshape(-1, v.shape[-1]), AXES, pairs).reshape(v.shape)

    def flip(v, k):
        return permute(v, [(l, l ^ k) for l in range(total)])

    def hop(v, moves):
        return permute(v, [(a * face + f, b * face + f) for a, b in moves for f in range(face)])

    column_groups = [[o * face + f for o in range(outer)] for f in range(face)]
    ring_groups = [[o * face + i * tensor + t for i in range(INNER)] for o in range(outer) for t in range(tensor)]
    towards_middle = [(0, 1), (3, 2)]
    across_middle = [(1, 2), (2, 1)]
    towards_ends = [(1, 0), (2, 3)]

    back_table = [[0, 1, 2, 3], [1, 0, 2, 3], [3, 2, 0, 1], [3, 2, 1, 0]]

    def swap_ring(v):
        return lax.all_to_all(v, AXES, split_axis=0, concat_axis=0, tiled=True, axis_index_groups=ring_groups)

    def swap_all(v):
        return lax.all_to_all(v, AXES, split_axis=0, concat_axis=0, tiled=True)

    class Near:
        def __init__(self, v):
            self.own = v
            self.near = flip(v, face) if short else None

    class Gather:
        def __init__(self, line, v, cols, at):
            if not short:
                own = v.own[:, at * cols : (at + 1) * cols]
                every = lax.all_gather(own, AXES, axis=0, tiled=True, axis_index_groups=column_groups)
                every = every.transpose(1, 0, 2).reshape(cols, 16, LANES).transpose(1, 0, 2)
                self.parts = [every[:8], every[8:], jnp.zeros_like(every[8:])]
                return
            self.both = cat_call(line, v.own, v.near, cols, at)
            self.far = hop(self.both, across_middle)

        def far_came(self, line):
            if short:
                self.far = line(self.far)
                self.passed = hop(self.far, towards_ends)

        def passed_came(self, line):
            if short:
                self.passed = line(self.passed)
                self.parts = [self.both, self.far, self.passed]

    class Reduce:
        def __init__(self, line, own, rest):
            if not short:
                v = jnp.concatenate([own, rest], axis=0)
                v = v.transpose(1, 0, 2).reshape(v.shape[1], dp, -1).transpose(1, 0, 2)
                self.total = lax.psum_scatter(
                    v, AXES, scatter_dimension=0, tiled=True, axis_index_groups=column_groups
                )
                return
            self.own, self.rest = own, line(rest)
            self.first = hop(self.rest, towards_middle)

        def first_came(self, line):
            if short:
                far = sum_call(line, (self.rest, self.first), (4, 4), 8)
                self.second = hop(far, across_middle)

        def second_came(self, line):
            if short:
                near = sum_call(line, (self.rest, self.second), (0, 4), 4)
                self.third = hop(near, towards_ends)

        def third_came(self, line):
            if short:
                self.total = sum_call(line, (self.own, self.first, self.second, self.third), (0, 0, 0, 0), 4)
            self.final = swap_ring(self.total)

    class FaceReduce:
        def __init__(self, sent):
            self.other = flip(sent, 2)

        def core_came(self, line):
            self.rows, self.width = self.kept.shape[0] // 4, self.kept.shape[1]
            spec = pl.BlockSpec((self.rows // STEPS, self.width), lambda r: (r, 0))
            x1, t1 = run_kernel(
                core_kernel, [shaped((self.rows, self.width))] * 2, self.block_specs((1, 1), (2, 0), (3, None)) * 2, [spec] * 2,
                (self.kept,) * 3 + (self.other,) * 3, "core", grid=(STEPS,), line=line,
            )
            self.x1, self.t1 = flip(x1, 4), flip(t1, 1)

        def block_specs(self, *blocks):
            block = self.rows // STEPS
            return [
                pl.BlockSpec(
                    (block, self.width if half is None else self.width // 2),
                    functools.partial(lambda k, h, r: (k * STEPS + r, h), k, half or 0),
                )
                for k, half in blocks
            ]

        def first_came(self, line):
            rows, width = self.rows, self.width
            half = pl.BlockSpec((rows // STEPS, width // 2), lambda r: (r, 0))
            t2, x2 = run_kernel(
                cross_kernel, [shaped((rows, width // 2))] * 2, self.block_specs((1, 0), (2, 1)) * 2 + [half] * 2, [half] * 2,
                (self.kept, self.kept, self.other, self.other, self.x1, self.t1), "cross", grid=(STEPS,), line=line,
            )
            self.t2, self.x2 = flip(t2, 1), flip(x2, 4)

        def second_came(self):
            return self.kept, self.other, self.x1, self.t1, self.t2, self.x2

    def per_device(
        layer_input, doc_lengths, ln1_gain, ln1_bias, ln2_gain, ln2_bias, w_qkv, b_qkv, w_dense, b_dense,
        w_fc1, b_fc1, w_fc2, b_fc2, cotangent,
    ):
        d, t = lax.axis_index("dp"), lax.axis_index("tensor")
        o, i = d // INNER, d % INNER
        own_rows, width = layer_input.shape
        rows, group_rows = own_rows * face, own_rows * tensor
        strip = width // dp
        hidden_own = w_fc1.shape[1] // INNER
        qkv_own = w_qkv.shape[1] // INNER
        quarter = hidden_own // 4
        piece, nq, nf = width // total, b_qkv.shape[0], b_fc1.shape[0]
        share = dp // INNER
        line = Line()
        if short:
            spots = jnp.array(back_table, jnp.int32)[o]
        else:
            spots = jnp.arange(4, dtype=jnp.int32)
        doc_rows = (o * INNER + (i ^ jnp.arange(INNER, dtype=jnp.int32))) * tensor
        place = jnp.concatenate([jnp.stack([o, i, t]).astype(jnp.int32), spots, doc_rows.astype(jnp.int32)])

        forms = {
            0: ((w_fc1, w_fc2) * 2, tuple((cross, quarter, k, 4) for k in (0, 1) for cross in (True, False))),
            2: ((w_qkv,) * 3 + (w_dense,), tuple((True, HD, k, 3) for k in (0, 1, 2)) + ((False, HD, 0, 1),)),
            4: ((w_fc1, w_fc2), ((True, 2 * quarter, 1, 2), (False, 2 * quarter, 1, 2))),
        }
        cuts_of = {0: (0, 2 * quarter, 0), 1: (0, 2 * quarter, 1), 2: (2, 2 * HD, 0), 3: (2, 2 * HD, 1), 4: (4, 4 * quarter, 0)}
        s = {}
        steps = {}

        def own():
            s["own"], s["cot_sum"] = own_call(line, place, layer_input, cotangent)
            s["t"], s["x"], s["c"] = flip(s["own"], 1), flip(s["own"], 4), flip(s["own"], 2)

        def own_c():
            s["c"] = line(s["c"])

        def own_xt():
            s["x"], s["t"] = line(s["x"], s["t"])
            s["bu"], s["bv"] = flip(s["x"][0], 1), flip(s["t"][1], 4)
            s["tc"], s["xc"] = flip(s["t"], 2), flip(s["x"], 2)

        def own_tc():
            s["tc"], s["xc"] = line(s["tc"], s["xc"])

        def own_b():
            s["bu"], s["bv"] = line(s["bu"], s["bv"])
            s["buc"], s["bvc"] = flip(s["bu"], 2), flip(s["bv"], 2)

        def own_bc():
            s["buc"], s["bvc"] = line(s["buc"], s["bvc"])

        steps.update({"own": own, "c": own_c, "xt": own_xt, "tc": own_tc, "b": own_b, "bc": own_bc})

        def small():
            v = jnp.concatenate(
                [ln1_gain, ln1_bias, ln2_gain, ln2_bias, b_dense + b_fc2, b_qkv.astype(F32), b_fc1.astype(F32),
                 doc_lengths[0].astype(F32), jnp.zeros((LANES - DOCS,), F32)]
            )
            s["small"] = swap_all(line(jnp.broadcast_to(v[None], (total, v.shape[0]))))

        def small_came():
            s["small"] = line(s["small"])

        def vectors():
            v = s["small"].reshape(total, -1)
            row, fine = shaped((1, width), F32), shaped((16, width))
            *s["vec"], s["bias_q"], s["bias_f"], s["lengths"] = run_kernel(
                functools.partial(vectors_kernel, piece, nq, nf, share, tensor),
                [row] * 4 + [fine] * 2 + [row, shaped((1, qkv_own), F32), shaped((1, hidden_own), F32),
                                          shaped((INNER, LANES), jnp.int32)],
                [SCALARS, VECTORS], [VECTORS] * 10, (place, v), "vectors", line=line,
            )
            turn_spec = pl.BlockSpec((group_rows, LANES), lambda g: (g, 0))
            s["turns"] = run_kernel(
                functools.partial(turns_kernel, own_rows), [shaped((rows, LANES), F32)] * 3, [SCALARS] * 2,
                [turn_spec] * 3, (place, s["lengths"]), "turns", grid=(INNER,), line=line,
            )

        steps.update({"sm": small, "sw": small_came, "vec": vectors})
        nears, gathers, done, sums = {}, {}, {}, {}

        def near_steps(k):
            def p():
                arrays, parts = forms[k]
                s[f"ring{k}"] = swap_ring(piece_call(line, arrays, parts, strip))

            def g():
                nears[k] = Near(line(s[f"ring{k}"]))

            steps.update({f"p{k}": p, f"g{k}": g})

        def gather_steps(k):
            def h():
                of, cols, at = cuts_of[k]
                gathers[k] = Gather(line, nears[of], cols, at)

            steps.update({
                f"h{k}": h, f"i{k}": lambda: gathers[k].far_came(line), f"j{k}": lambda: gathers[k].passed_came(line),
            })

        for k in forms:
            near_steps(k)
        for k in cuts_of:
            gather_steps(k)

        def pieces():
            return [s[n] for n in ("own", "t", "c", "tc", "x", "xc", "bu", "bv", "buc", "bvc")]

        def feed(k, first, split, sets):
            def run():
                gain, shift, ratio = s["vec"][2], s["vec"][3], s["vec"][5]
                cols = split * quarter
                bias = s["bias_f"][:, first * quarter : first * quarter + cols]
                done[k] = chunk_call(
                    line, functools.partial(feed_kernel, cols, split, len(sets)), "feed", pieces(), (), [],
                    [gathers[j].parts for j in sets], (gain, shift, ratio, bias), cols, cols, split,
                )

            return run

        def attention():
            gain, shift, ratio = s["vec"][0], s["vec"][1], s["vec"][4]
            one, two = gathers[2].parts, gathers[3].parts
            turn_spec = pl.BlockSpec((group_rows, LANES), lambda r: (r, 0))
            done[2] = chunk_call(
                line, functools.partial(attention_kernel, qkv_own), "attention", pieces(),
                (s["lengths"], place, *s["turns"]), [SCALARS, SCALARS] + [turn_spec] * 3, [one, two],
                (gain, shift, ratio, s["bias_q"]), qkv_own, HD, 1,
            )

        steps.update({"K0": feed(0, 0, 1, (0,)), "K1": feed(1, 1, 1, (1,)), "KA": attention, "K4": feed(4, 2, 2, (4,))})

        def reduce_steps(k, chunk, at):
            def r():
                sums[k] = Reduce(line, *done[chunk][at : at + 2])

            def z():
                final = sums[k].final
                if k == 2:
                    s["qkv"], s["dense"] = unpiece_call(
                        line, final, (w_qkv.shape, w_dense.shape), ((True, qkv_own, 0, 1), (False, HD, 0, 1)), ()
                    )
                elif k < 2:
                    s["fc1"], s["fc2"] = unpiece_call(
                        line, final, (w_fc1.shape, w_fc2.shape), forms[0][1][2 * k : 2 * k + 2], (s.get("fc1"), s.get("fc2"))
                    )
                else:
                    name, w, form = (("fc1", w_fc1, 0), ("fc2", w_fc2, 1))[k - 3]
                    s[name], = unpiece_call(line, final, (w.shape,), forms[4][1][form : form + 1], (s[name],))

            steps.update({
                f"r{k}": r, f"u{k}": lambda: sums[k].first_came(line), f"v{k}": lambda: sums[k].second_came(line),
                f"w{k}": lambda: sums[k].third_came(line), f"z{k}": z,
            })

        for k, chunk, at in ((0, 0, 6), (1, 1, 6), (2, 2, 6), (3, 4, 6), (4, 4, 8)):
            reduce_steps(k, chunk, at)

        def face_steps(name, act, weight, finish):
            def parts():
                chunks = [done[k] for k in (0, 1, 2, 4)]
                return [c[act] for c in chunks], [c[weight] for c in chunks]

            def sent():
                s["face" + name] = FaceReduce(join_call(line, *parts(), True))

            def kept():
                s["face" + name].kept = join_call(line, *parts(), False)

            steps.update({
                "J" + name: sent, "k" + name: kept, "C" + name: lambda: s["face" + name].core_came(line),
                "D" + name: lambda: s["face" + name].first_came(line),
                "E" + name: lambda: finish(s["face" + name].second_came()),
            })

        def finish_back(sums_in):
            s["input_grad"] = own_rows_call(
                line, input_grad_kernel, place, (layer_input, cotangent), (), sums_in, "input_grad"
            )

        def finish_out(sums_in):
            s["output"] = own_rows_call(line, output_kernel, place, (layer_input,), (s["vec"][6],), sums_in, "output")

        face_steps("B", 1, 2, finish_back)
        face_steps("O", 0, 3, finish_out)

        def tail():
            feeds = [done[k] for k in (0, 1, 4)]
            v = run_kernel(
                functools.partial(tail_kernel, piece, nq, nf, share, tensor),
                shaped((total, full_lanes(5 * piece) + full_lanes(nq + nf)), F32), [SCALARS] + [VECTORS] * 9, VECTORS,
                (place, done[2][4], *[p[4] for p in feeds], done[2][5], *[p[5] for p in feeds], s["cot_sum"]), "tail", line=line,
            )
            s["tail"] = swap_all(v)

        def tail_came():
            s["tail"] = jnp.sum(line(s["tail"]), axis=0)

        steps.update({"tail": tail, "tz": tail_came})
        for name in ORDER:
            steps[name]()

        tail_row = s["tail"]
        cuts = [tail_row[j * piece : (j + 1) * piece] for j in range(5)]
        at = full_lanes(5 * piece)
        return (
            s["output"], s["input_grad"], cuts[0], cuts[1], cuts[2], cuts[3], s["qkv"], tail_row[at : at + nq],
            s["dense"], cuts[4], s["fc1"], tail_row[at + nq : at + nq + nf], s["fc2"], cuts[4],
        )

    return per_device


def solution(mesh):
    rows = P(("dp", "tensor"), None)
    vector = P(("dp", "tensor"))
    crossed = P(("tensor", "dp"))
    wide = P("dp", "tensor")
    tall = P("tensor", "dp")
    return jax.shard_map(
        make(mesh.shape["dp"], mesh.shape["tensor"]),
        mesh=mesh,
        in_specs=(rows, P("dp", None), vector, vector, vector, vector, wide, crossed, tall, vector, wide, crossed,
                  tall, vector, rows),
        out_specs=(rows, rows, vector, vector, vector, vector, wide, crossed, tall, vector, wide, crossed, tall,
                   vector),
        check_vma=False,
    )
```
